512 devices in a mesh: branch: 128 (over y, z, core), level: 4 (over x).
Axes of the slice: x: 4, y: 8, z: 8, core: 2. Of those that a mesh axis runs over, the one named last changes fastest.
Arguments:
- basis: bfloat16 [512, 64, 4096], P('branch', None, 'level'), may hold values from -0.09375 to 0.09375
- bottom_transfer: bfloat16 [512, 4096], P('branch'), may hold values from -0.75 to 0.75
- bottom_rank: int32 [512], P('branch'), may hold values from 16 to 64
- upper_transfer: bfloat16 [254, 4096], replicated, may hold values from -0.75 to 0.75
- upper_rank: int32 [254], replicated, may hold values from 16 to 64
- couplings: bfloat16 [49152, 4096], P(('branch', 'level')), may hold values from -6 to 6
- row_cluster: int32 [49152], P(('branch', 'level')), may hold values from 0 to 3
- column_owner: int32 [49152, 1], P(('branch', 'level')), may hold values from 0 to 127; in each aligned block of 96 rows (0 to 95, 96 to 191, ...) at most 2 rows name the same one
- column_cluster: int32 [49152], P(('branch', 'level')), may hold values from 0 to 3
Outputs:
- upper_grams: float32 [128, 4096], P('branch')
- projected: float32 [49152, 4096], P(('branch', 'level'))
The draws below stay inside these ranges and needn't reach their ends.
Inputs may be any that keep to these rules, and one draw needn't show every extreme that they name: Among the 96 blocks of one device at most 2 have the same column_owner, and in every draw some owner is named by exactly 2 of them.
All inputs are finite; a program needn't handle non-finite values.
Results may differ from the reference program's by a relative error of at most 0.0052.
Values may be sent and summed in bfloat16 or wider, within the bound.
No kernel may reach another device: no remote copies, remote signals or barrier semaphores. Data moves between devices by JAX's collectives and lax.ppermute only.
A program may use at most 64 MiB of HBM per device.

```python
import math
import jax
import jax.numpy as jnp
import numpy as np
from jax import lax

K = 64
NODE_DEV = 4
BLK_DEV = 96
NB = 512
PTS = 4096
CAP = 2
BLOCKS = 49152
UPPER = 254
N_BRANCH = 128
N_LEVEL = 4


def with_ends(drawn, own_key, smallest, top_value):
    index_at = [jax.random.randint(jax.random.fold_in(own_key, axis), (), 0, length) for axis, length in enumerate(drawn.shape)]
    main_axis = drawn.shape.index(max(drawn.shape))
    beside = index_at[:main_axis] + [(index_at[main_axis] + 1) % drawn.shape[main_axis]] + index_at[main_axis + 1:]
    return drawn.at[tuple(index_at)].set(smallest).at[tuple(beside)].set(top_value)


def levels(rng, dims, shards, low, largest):
    def one(position, shards_of):
        draws = jax.random.uniform(jax.random.fold_in(jax.random.fold_in(rng, 6), position), (shards_of,), jnp.float32, low / len(shards), largest / len(shards))
        return jnp.repeat(jnp.exp(draws), dims[position] // shards_of).reshape((-1,) + (1,) * (len(dims) - position - 1))

    gain = one(*shards[0])
    for cut in shards[1:]:
        gain = gain * one(*cut)
    return gain


def assign_block(rng, own, number, rows, count, top, reach, lean):
    order = jax.random.permutation(rng, count)
    heavy_load, common = portions_of(count, rows * top, reach, lean, True), portions_of(count, rows * top, reach, lean, False)
    places = jnp.arange(count)

    def named(sizes, rotation):
        used = int((sizes > 0).sum())
        fixed = max(1, used // 4)
        shifted = fixed + (places - fixed + rotation * (used - fixed)) % max(1, count - fixed)
        return jnp.zeros((count,), jnp.int32).at[order[jnp.where(places < fixed, places, shifted)]].set(jnp.asarray(sizes, jnp.int32))

    sizes = jnp.where(number % 4 == 0, named(heavy_load, number // 4), named(common, number - number // 4 - 1))
    mixed = jax.random.permutation(jax.random.fold_in(own, 3), count)
    source_of, receiver = mixed[0:count // 2 * 2:2], mixed[1:count // 2 * 2:2]
    margin = jnp.minimum(sizes[source_of] - 1, reach - sizes[receiver]) // 2
    margin = jnp.where((source_of == order[0]) | (receiver == order[0]) | (sizes[receiver] == 0), 0, jnp.maximum(margin, 0))
    shifted = jax.random.randint(jax.random.fold_in(own, 4), (count // 2,), 0, 1 << 20) % (margin + 1)
    sizes = sizes.at[source_of].add(-shifted).at[receiver].add(shifted)
    items = jnp.searchsorted(jnp.cumsum(sizes), jnp.arange(rows * top), side="right").astype(jnp.int32)
    grid = items.reshape(top, rows).T
    grid = grid[jax.random.permutation(jax.random.fold_in(own, 1), rows)]
    rotation = jax.random.randint(jax.random.fold_in(own, 2), (rows, 1), 0, top)
    return jnp.take_along_axis(grid, (jnp.arange(top)[None, :] + rotation) % top, axis=1)


def portions_of(number_of, total, limit, skew, full):
    weights = [(1 << 20) // math.isqrt(grade ** skew) + 1 for grade in range(1, number_of + 1)]
    largest = limit if full else min(limit, max(-(-total // number_of), total * weights[0] // sum(weights)))
    least = 1 if total - largest >= number_of - 1 else 0
    given, rest = [largest] + [least] * (number_of - 1), total - largest - least * (number_of - 1)
    while rest > 0:
        free = [i for i in range(1, number_of) if given[i] < largest] or [i for i in range(1, number_of) if given[i] < limit]
        whole, remaining = sum([weights[i] for i in free]), rest
        for i in free:
            addition = min(limit - given[i], max(1, remaining * weights[i] // whole), rest)
            given[i] = given[i] + addition
            rest = rest - addition
    return np.array(given)


def normal_values(own_key, shape, deviation, limit, cuts=(), kind=jnp.bfloat16):
    values = jax.random.normal(own_key, shape, jnp.float32) * deviation
    if len(cuts) > 0:
        values = levels(own_key, shape, cuts, -0.22, 0.18) * values
    return jnp.clip(values, min=-limit, max=limit).astype(kind)


def setup_inputs(seed: int = 0) -> dict:
    key_of = jax.random.split(jax.random.key(seed), 10)
    basis = normal_values(key_of[0], (NB, K, PTS), PTS ** -0.5, 0.09375, ((0, 128), (2, 4)))
    bottom_transfer = normal_values(key_of[1], (NB, K * K), K ** -0.5, 0.75, ((0, 128),))
    bottom_rank = with_ends(jax.random.randint(key_of[2], (NB,), K // 4, K + 1), jax.random.fold_in(key_of[2], 1), K // 4, K).astype(jnp.int32)
    upper_transfer = normal_values(key_of[3], (UPPER, K * K), K ** -0.5, 0.75)
    upper_rank = with_ends(jax.random.randint(key_of[4], (UPPER,), K // 4, K + 1), jax.random.fold_in(key_of[4], 1), K // 4, K).astype(jnp.int32)
    couplings = normal_values(key_of[5], (BLOCKS, K * K), 1.0, 6.0, ((0, 512),))
    row_cluster = with_ends(jax.random.randint(key_of[6], (BLOCKS,), 0, NODE_DEV), jax.random.fold_in(key_of[6], 1), 0, NODE_DEV - 1).astype(jnp.int32)
    column_owner_keys = jax.random.split(jax.random.fold_in(key_of[7], 1), BLOCKS // BLK_DEV)
    column_owner_turns = jax.random.permutation(jax.random.fold_in(key_of[7], 3), BLOCKS // BLK_DEV)
    column_owner = jax.vmap(lambda own, number: assign_block(jax.random.fold_in(key_of[7], 2), own, number, BLK_DEV, N_BRANCH, 1, CAP, 2))(column_owner_keys, column_owner_turns).reshape((BLOCKS, 1))
    column_cluster = with_ends(jax.random.randint(key_of[8], (BLOCKS,), 0, NODE_DEV), jax.random.fold_in(key_of[8], 1), 0, NODE_DEV - 1).astype(jnp.int32)
    return {"basis": basis, "bottom_transfer": bottom_transfer, "bottom_rank": bottom_rank, "upper_transfer": upper_transfer, "upper_rank": upper_rank, "couplings": couplings, "row_cluster": row_cluster, "column_owner": column_owner, "column_cluster": column_cluster}


HIGH = lax.Precision.HIGHEST


def rank_mask(ranks, width):
    index = jnp.arange(width, dtype=jnp.int32)
    keep = (index[None, :] < ranks[:, None]).astype(jnp.float32)
    return keep[:, :, None] * keep[:, None, :]


def lift(grams, transfer, ranks):
    width = grams.shape[1]
    masked = grams * rank_mask(ranks, width)
    mats = transfer.astype(jnp.float32).reshape(-1, width, width)
    inner = jnp.einsum('nij,njk->nik', masked, mats, precision=HIGH)
    return jnp.einsum('nji,njk->nik', mats, inner, precision=HIGH)


def reference(basis, bottom_transfer, bottom_rank, upper_transfer, upper_rank, couplings, row_cluster, column_owner, column_cluster):
    width = basis.shape[1]
    grams = lax.map(lambda v: jnp.dot(v, v.T, preferred_element_type=jnp.float32), basis)
    terms = lift(grams, bottom_transfer, bottom_rank)
    current = jnp.sum(terms.reshape(-1, NODE_DEV, width, width), axis=1)
    stored = [current]
    branches = current.shape[0]
    height = 0
    while branches >> height >= 2:
        count = branches >> height
        start = 2 * branches - 2 * count
        lifted = lift(current, upper_transfer[start:start + count], upper_rank[start:start + count])
        current = lifted[0::2] + lifted[1::2]
        stored.append(current)
        height = height + 1
    rows = []
    for index in range(branches):
        top = (index ^ ((index + 1) % branches)).bit_length()
        rows.append(stored[top][index >> top])
    upper_grams = jnp.stack(rows).reshape(branches, width * width)

    masked = (grams * rank_mask(bottom_rank, width)).astype(jnp.bfloat16)
    groups = BLOCKS // BLK_DEV
    device_of = (jnp.arange(groups, dtype=jnp.int32) // N_LEVEL).astype(jnp.int32)

    def project(items):
        blocks, rows_local, owners, columns, device = items
        row_index = (device * NODE_DEV + rows_local).astype(jnp.int32)
        col_index = (owners * NODE_DEV + columns).astype(jnp.int32)
        left = jnp.take(masked, row_index, axis=0).astype(jnp.float32)
        right = jnp.take(masked, col_index, axis=0).astype(jnp.float32)
        mats = blocks.reshape(-1, width, width).astype(jnp.float32)
        carried = jnp.einsum('bij,bjk->bik', mats, right).astype(jnp.bfloat16)
        out = jnp.einsum('bij,bjk->bik', left, carried.astype(jnp.float32))
        return out.reshape(-1, width * width)

    projected = lax.map(project, (couplings.reshape(groups, BLK_DEV, width * width),
                                  row_cluster.reshape(groups, BLK_DEV),
                                  column_owner.reshape(groups, BLK_DEV),
                                  column_cluster.reshape(groups, BLK_DEV),
                                  device_of))
    return upper_grams, projected.reshape(BLOCKS, width * width)
```

```python
import functools

import jax
import jax.numpy as jnp
from jax import lax
from jax.experimental import pallas as pl
from jax.experimental.pallas import tpu as pltpu
from jax.sharding import PartitionSpec as P

VMEM = pl.BlockSpec(memory_space=pltpu.VMEM)
SMEM = pl.BlockSpec(memory_space=pltpu.SMEM)
ROWS = 16
TOGETHER = 4
F32 = jnp.float32
BF16 = jnp.bfloat16


def iota(shape, axis):
    return lax.broadcasted_iota(jnp.int32, shape, axis)


def nn(a, b):
    return jnp.dot(a, b, preferred_element_type=F32)


def nt(a, b):
    return lax.dot_general(a, b, (((1,), (1,)), ((), ())), preferred_element_type=F32)


def tn(a, b):
    return lax.dot_general(a, b, (((0,), (0,)), ((), ())), preferred_element_type=F32)


def halves(x):
    high = x.astype(BF16)
    return high, (x - high.astype(F32)).astype(BF16)


def keep_rank(gram, rank):
    return jnp.where((iota(gram.shape, 0) < rank) & (iota(gram.shape, 1) < rank), gram, 0.0)


def lift(masked, transfer):
    inner = []
    for gram, mat in zip(masked, transfer):
        high, low = halves(gram)
        inner.append(nn(high, mat) + nn(low, mat))
    high, low = halves(jnp.concatenate(inner, axis=0))
    mats = jnp.concatenate(transfer, axis=0)
    return tn(mats, high) + tn(mats, low)


def pack(square):
    half = square.shape[0] // 2
    return jnp.concatenate([square[:half], square[half:]], axis=1)


def unpack(packed):
    half = packed.shape[1] // 2
    return jnp.concatenate([packed[:, :half], packed[:, half:]], axis=0)


def reach(index, count):
    return (index ^ ((index + 1) % count)).bit_length()


def gram_kernel(basis_ref, out_ref):
    copies = out_ref.shape[0]
    width = basis_ref.shape[1]
    wide = 2 * width
    row = iota((width, wide), 0)
    lane = iota((width, wide), 1)
    column = lane & (width - 1)
    sides = []
    for side in range(2):
        both = jnp.concatenate([basis_ref[side], basis_ref[side + 2]], axis=0)
        crossed = nt(both, both)
        sides.append(jnp.where(lane < width, crossed[:width], crossed[width:]))
    folded = jnp.where(row <= column, sides[0], sides[1])
    diagonal = jnp.sum(jnp.where(row == column, sides[1], 0.0), axis=0, keepdims=True)
    for copy in range(copies):
        out_ref[copy, :width] = folded
        out_ref[copy, width:] = jnp.broadcast_to(diagonal, (8, wide))


def share_kernel(rank_ref, level_ref, parts_ref, share_ref, total_ref, scratch):
    copies, share, wide = share_ref.shape
    width = wide // 2
    total = parts_ref[0]
    for part in range(1, parts_ref.shape[0]):
        total = total + parts_ref[part]
    total_ref[...] = total
    row = iota((width, wide), 0)
    lane = iota((width, wide), 1)
    column = lane & (width - 1)
    low = lane < width
    upper = jnp.where(low, rank_ref[0], rank_ref[2])
    lower = jnp.where(low, rank_ref[1], rank_ref[3])
    kept = jnp.maximum(row, column) < jnp.where(row <= column, upper, lower)
    scratch[...] = jnp.where(kept, total[:width], 0.0)
    mine = scratch[pl.ds(pl.multiple_of(level_ref[0] * share, share), share), :].astype(BF16)
    for copy in range(copies):
        share_ref[copy] = mine


def near_kernel(rank_ref, path_rank_ref, place_ref, total_ref, bottom_ref, path_ref, left_ref, sent_ref):
    nodes, width, _ = bottom_ref.shape
    wide = 2 * width
    group, rows, _ = sent_ref.shape
    heights = path_ref.shape[0]
    half = width // 2
    folded = total_ref[:width]
    diagonal = total_ref[width : width + 1]
    turned = folded.T
    row = iota((width, width), 0)
    column = iota((width, width), 1)
    even_first = jnp.where(row < half, 2 * row, 2 * row - width + 1)
    order = (column == even_first).astype(F32).astype(BF16)
    masked = []
    for node in range(nodes):
        pair, side = node // 2, node % 2
        here = folded[:, pair * width : (pair + 1) * width]
        there = turned[pair * width : (pair + 1) * width]
        if side == 0:
            gram = jnp.where(row <= column, here, there)
        else:
            centre = jnp.broadcast_to(diagonal[:, pair * width : (pair + 1) * width], (width, width))
            gram = jnp.where(row > column, here, jnp.where(row < column, there, centre))
        gram = keep_rank(gram, rank_ref[node])
        masked.append(gram)
        left_ref[node] = nt(nn(order, gram.astype(BF16)).astype(BF16), order).astype(BF16)
    current = lift(masked, [bottom_ref[node] for node in range(nodes)])
    terms = []
    for height in range(heights):
        current = lift([keep_rank(current, path_rank_ref[height])], [path_ref[height]])
        terms.append(pack(current).astype(BF16))
    place = place_ref[0]
    lane = iota((1, wide), 1)
    lower = jnp.where(lane < width, rank_ref[1], rank_ref[3])
    diagonal = jnp.where((lane & (width - 1)) < lower, diagonal, 0.0)
    diagonal = jnp.broadcast_to(diagonal, (rows - half, wide)).astype(BF16)
    none = jnp.zeros((half, wide), BF16)
    for target in range(group):
        height = min(reach(target, 2 * group), heights)
        inside = jnp.right_shift(place, height) == target >> height

        @pl.when(inside)
        def _():
            sent_ref[target, :half] = terms[height - 1]

        @pl.when(jnp.logical_not(inside))
        def _():
            sent_ref[target, :half] = none

        sent_ref[target, half:] = diagonal


def far_kernel(path_rank_ref, place_ref, received_ref, path_ref, near_ref, sent_ref):
    group, rows, wide = received_ref.shape
    targets = sent_ref.shape[0]
    width = wide // 2
    half = width // 2
    heights = path_ref.shape[0]
    total = received_ref[0, :half].astype(F32)
    for member in range(1, group):
        total = total + received_ref[member, :half].astype(F32)
    near_ref[...] = total
    diagonals = [received_ref[member, half:].astype(F32)[:1] for member in range(group)]
    diagonals += [jnp.zeros((rows - half - group, wide), F32)] if group < rows - half else []
    diagonals = jnp.concatenate(diagonals, axis=0).astype(BF16)
    current = unpack(total)
    terms = []
    for height in range(heights):
        current = lift([keep_rank(current, path_rank_ref[height])], [path_ref[height]])
        terms.append(pack(current).astype(BF16))
    place = place_ref[0]
    none = jnp.zeros((half, wide), BF16)
    for target in range(targets):
        height = reach(target, targets)
        inside = jnp.right_shift(place, height) == target >> height

        @pl.when(inside)
        def _():
            sent_ref[target, :half] = terms[height - 1]

        @pl.when(jnp.logical_not(inside))
        def _():
            sent_ref[target, :half] = none

        sent_ref[target, half:] = diagonals


def top_kernel(last_ref, near_ref, received_ref, out_ref, diagonal_ref, scratch):
    targets, rows, wide = received_ref.shape
    half = wide // 4
    total = received_ref[0, :half].astype(F32)
    for member in range(1, targets):
        total = total + received_ref[member, :half].astype(F32)
    total = jnp.where(last_ref[0] == 1, total, near_ref[...])
    scratch[...] = unpack(total)
    natural = jnp.concatenate([scratch[pl.ds(side, half, stride=2), :] for side in range(2)], axis=1)
    for tile in range(half):
        out_ref[:, tile * wide : (tile + 1) * wide] = natural[tile : tile + 1]
    group = diagonal_ref.shape[0] // targets
    for member in range(targets):
        diagonal_ref[member * group : (member + 1) * group] = received_ref[member, half:].astype(F32)[:group]


def project_kernel(
    owner_ref,
    column_ref,
    row_ref,
    core_ref,
    blocks_ref,
    own_ref,
    other_ref,
    diagonal_ref,
    left_ref,
    out_ref,
    spread,
    result,
    triangles,
):
    step = pl.program_id(0)
    count, flat = blocks_ref.shape
    depth = own_ref.shape[2]
    width = left_ref.shape[1]
    wide = 2 * width
    tiles = flat // wide
    row = iota((width, wide), 0)
    lane = iota((width, wide), 1)
    column = lane & (width - 1)
    low = lane < width

    @pl.when(step == 0)
    def _():
        triangles[0, 0] = (row <= column).astype(F32)
        triangles[0, 1] = (row < column).astype(F32)
        triangles[0, 2] = jnp.zeros((width, wide), F32)
        triangles[1, 0] = (row > column).astype(F32)
        triangles[1, 1] = (row > column).astype(F32)
        triangles[1, 2] = (row == column).astype(F32)

    for tile in range(tiles):
        spread[tile * count : (tile + 1) * count, :] = blocks_ref[:, tile * wide : (tile + 1) * wide].astype(F32)

    def right_product(index):
        block = step * count + index
        owner = owner_ref[block]
        cluster = column_ref[block]
        pair = jnp.right_shift(cluster, 1)
        side = cluster & 1
        across = jnp.right_shift(owner, 1) & (depth - 1)
        along = owner // (2 * depth)
        near = own_ref[along, :, across].reshape(width, wide)
        far = other_ref[along, :, across].reshape(width, wide)
        folded = jnp.where((owner & 1) == core_ref[0], near, far).astype(F32)
        centre = jnp.broadcast_to(diagonal_ref[pl.ds(owner, 1), :], (width, wide))
        direct = folded * triangles[side, 0] + centre * triangles[side, 2]
        mirrored = folded * triangles[side, 1]
        wanted = low == (pair == 0)
        direct = jnp.where(wanted, direct, pltpu.roll(direct, width, 1)).astype(BF16)
        mirrored = jnp.where(wanted, mirrored, pltpu.roll(mirrored, width, 1)).astype(BF16)[:, :width]
        here = spread[pl.ds(index, tiles, stride=count), :]
        rows = jnp.concatenate([here, pltpu.roll(here, width, 1)], axis=0).astype(BF16)[:, :width]
        return nn(rows, direct) + nt(rows, jnp.concatenate([mirrored, mirrored], axis=0))

    for first in range(0, count, TOGETHER):
        group = range(first, first + TOGETHER)
        carried = [right_product(index).astype(BF16) for index in group]
        for index, value in zip(group, carried):
            full = nn(left_ref[row_ref[step * count + index]], value)
            result[pl.ds(index, tiles, stride=count), :] = jnp.where(low[:tiles], full[:tiles], full[tiles:])
    for tile in range(tiles):
        out_ref[:, tile * wide : (tile + 1) * wide] = result[tile * count : (tile + 1) * count, :]


def copies_of(block, count):
    return jnp.broadcast_to(block[None], (count,) + block.shape)


def shape(dims, dtype):
    return jax.ShapeDtypeStruct(dims, dtype)


def on_device(
    depth,
    basis,
    bottom_transfer,
    bottom_rank,
    upper_transfer,
    upper_rank,
    couplings,
    row_cluster,
    column_owner,
    column_cluster,
):
    nodes, width, _ = basis.shape
    wide = 2 * width
    half = width // 2
    branches = lax.axis_size("branch")
    parts = lax.axis_size("level")
    levels = branches.bit_length() - 1
    group = 2 * depth
    spans = branches // group
    near_levels = group.bit_length() - 1
    share = width // parts
    me_branch = lax.axis_index("branch")
    me_level = lax.axis_index("level")
    core = me_branch & 1
    me_near = me_branch & (group - 1)
    me_far = me_branch // group
    blk = couplings.shape[0]

    along_z = [[y * group + z * 2 + c for z in range(depth)] for y in range(spans) for c in range(2)]
    along_y = [[y * group + near for y in range(spans)] for near in range(group)]
    same_y = [[y * group + near for near in range(group)] for y in range(spans)]
    along_yx = [[(y * group + near) * parts + x for y in range(spans) for x in range(parts)] for near in range(group)]

    partial_sums = pl.pallas_call(
        gram_kernel,
        out_shape=shape((parts, width + 8, wide), F32),
        in_specs=[VMEM],
        out_specs=VMEM,
        name="gram",
    )(basis)
    gathered = lax.all_to_all(partial_sums, "level", 0, 0)
    shares, total = pl.pallas_call(
        share_kernel,
        out_shape=[shape((depth, share, wide), BF16), shape((width + 8, wide), F32)],
        in_specs=[SMEM, SMEM, VMEM],
        out_specs=[VMEM, VMEM],
        scratch_shapes=[pltpu.VMEM((width, wide), F32)],
        name="share",
    )(bottom_rank, me_level[None], gathered)

    column = lax.all_to_all(shares, "branch", 0, 0, axis_index_groups=along_z)
    own = lax.all_to_all(
        copies_of(column, spans * parts), ("branch", "level"), 0, 0, axis_index_groups=along_yx
    ).reshape(spans, parts, depth, share, wide)
    other = lax.ppermute(own, "branch", [(i, i ^ 1) for i in range(branches)])

    heights = jnp.arange(levels, dtype=jnp.int32)
    slots = 2 * branches - jnp.right_shift(2 * branches, heights) + jnp.right_shift(me_branch, heights)
    path = jnp.take(upper_transfer, slots, axis=0).reshape(levels, width, width)
    path_rank = jnp.take(upper_rank, slots, axis=0)
    left, near_sent = pl.pallas_call(
        near_kernel,
        out_shape=[shape((nodes, width, width), BF16), shape((group, half + 16, wide), BF16)],
        in_specs=[SMEM, SMEM, SMEM, VMEM, VMEM, VMEM],
        out_specs=[VMEM, VMEM],
        name="near",
    )(
        bottom_rank,
        path_rank[:near_levels],
        me_near[None],
        total,
        bottom_transfer.reshape(nodes, width, width),
        path[:near_levels],
    )
    near_received = lax.all_to_all(near_sent, "branch", 0, 0, axis_index_groups=same_y)
    near_gram, far_sent = pl.pallas_call(
        far_kernel,
        out_shape=[shape((half, wide), F32), shape((spans, half + 16, wide), BF16)],
        in_specs=[SMEM, SMEM, VMEM, VMEM],
        out_specs=[VMEM, VMEM],
        name="far",
    )(path_rank[near_levels:], me_far[None], near_received, path[near_levels:])
    far_received = lax.all_to_all(far_sent, "branch", 0, 0, axis_index_groups=along_y)
    upper_grams, diagonals = pl.pallas_call(
        top_kernel,
        out_shape=[shape((1, width * width), F32), shape((branches, wide), F32)],
        in_specs=[SMEM, VMEM, VMEM],
        out_specs=[VMEM, VMEM],
        scratch_shapes=[pltpu.VMEM((width, width), F32)],
        name="top",
    )((me_near == group - 1).astype(jnp.int32)[None], near_gram, far_received)

    whole = pl.BlockSpec(own.shape, lambda i, *_: (0, 0, 0, 0, 0))
    projected = pl.pallas_call(
        project_kernel,
        out_shape=shape((blk, width * width), F32),
        grid_spec=pltpu.PrefetchScalarGridSpec(
            num_scalar_prefetch=4,
            grid=(blk // ROWS,),
            in_specs=[
                pl.BlockSpec((ROWS, width * width), lambda i, *_: (i, 0)),
                whole,
                whole,
                pl.BlockSpec((branches, wide), lambda i, *_: (0, 0)),
                pl.BlockSpec((nodes, width, width), lambda i, *_: (0, 0, 0)),
            ],
            out_specs=pl.BlockSpec((ROWS, width * width), lambda i, *_: (i, 0)),
            scratch_shapes=[
                pltpu.VMEM((ROWS * half, wide), F32),
                pltpu.VMEM((ROWS * half, wide), F32),
                pltpu.VMEM((2, 3, width, wide), F32),
            ],
        ),
        compiler_params=pltpu.CompilerParams(vmem_limit_bytes=24 * 1024 * 1024),
        name="project",
    )(column_owner[:, 0], column_cluster, row_cluster, core[None], couplings, own, other, diagonals, left)
    return (upper_grams, projected)


def solution(mesh):
    placed = (
        P("branch", None, "level"),
        P("branch", None),
        P("branch"),
        P(),
        P(),
        P(("branch", "level"), None),
        P(("branch", "level")),
        P(("branch", "level"), None),
        P(("branch", "level")),
    )
    depth = min(8, mesh.shape["branch"] // 4)
    return jax.shard_map(
        functools.partial(on_device, depth),
        mesh=mesh,
        in_specs=placed,
        out_specs=(P("branch", None), P(("branch", "level"), None)),
        check_vma=False,
    )
```

```python
import jax
import jax.numpy as jnp
from jax import lax
from jax.experimental import pallas as pl
from jax.experimental.pallas import tpu as pltpu
from jax.sharding import PartitionSpec as P

VMEM = pl.BlockSpec(memory_space=pltpu.VMEM)
SMEM = pl.BlockSpec(memory_space=pltpu.SMEM)
SMALL = pltpu.CompilerParams(vmem_limit_bytes=8 * 1024 * 1024)
ROWS = 16
TOGETHER = 4
F32 = jnp.float32
BF16 = jnp.bfloat16


def iota(shape, axis):
    return lax.broadcasted_iota(jnp.int32, shape, axis)


def nn(a, b):
    return jnp.dot(a, b, preferred_element_type=F32)


def nt(a, b):
    return lax.dot_general(a, b, (((1,), (1,)), ((), ())), preferred_element_type=F32)


def tn(a, b):
    return lax.dot_general(a, b, (((0,), (0,)), ((), ())), preferred_element_type=F32)


def halves(x):
    high = x.astype(BF16)
    return high, (x - high.astype(F32)).astype(BF16)


def keep_rank(gram, rank):
    return jnp.where((iota(gram.shape, 0) < rank) & (iota(gram.shape, 1) < rank), gram, 0.0)


def lift(masked, transfer):
    inner = []
    for gram, mat in zip(masked, transfer):
        high, low = halves(gram)
        inner.append(nn(high, mat) + nn(low, mat))
    high, low = halves(jnp.concatenate(inner, axis=0))
    mats = jnp.concatenate(transfer, axis=0)
    return tn(mats, high) + tn(mats, low)


def product(multiply, a, b):
    return multiply(a[0], b[0]) + (multiply(a[0], b[1]) + multiply(a[1], b[0]))


def fold(square):
    half = square.shape[0] // 2
    row, column = iota((half, half), 0), iota((half, half), 1)
    first = square[:half, :half]
    mixed = jnp.where(row < column, first, square[half:, half:])
    centre = jnp.sum(jnp.where(row == column, first, 0.0), axis=0, keepdims=True)
    return jnp.concatenate([mixed, square[:half, half:]], axis=1), centre


def unfold(folded, centre):
    half = folded.shape[0]
    row, column = iota((half, half), 0), iota((half, half), 1)
    turned = folded.T
    mixed, mixed_turned = folded[:, :half], turned[:half]
    first = jnp.where(row < column, mixed, jnp.where(row > column, mixed_turned, centre))
    last = jnp.where(row >= column, mixed, mixed_turned)
    top = jnp.concatenate([first, folded[:, half:]], axis=1)
    return jnp.concatenate([top, jnp.concatenate([turned[half:], last], axis=1)], axis=0)


def pack(square):
    half = square.shape[0] // 2
    return jnp.concatenate([square[:half], square[half:]], axis=1)


def unpack(packed):
    half = packed.shape[1] // 2
    return jnp.concatenate([packed[:, :half], packed[:, half:]], axis=0)


def reach(index, count):
    return (index ^ ((index + 1) % count)).bit_length()


def gram_kernel(basis_ref, out_ref):
    copies = out_ref.shape[0]
    width = basis_ref.shape[1]
    wide = 2 * width
    row = iota((width, wide), 0)
    lane = iota((width, wide), 1)
    column = lane & (width - 1)
    sides = []
    for side in range(2):
        both = jnp.concatenate([basis_ref[side], basis_ref[side + 2]], axis=0)
        crossed = nt(both, both)
        sides.append(jnp.where(lane < width, crossed[:width], crossed[width:]))
    folded = jnp.where(row <= column, sides[0], sides[1])
    diagonal = jnp.sum(jnp.where(row == column, sides[1], 0.0), axis=0, keepdims=True)
    for copy in range(copies):
        out_ref[copy, :width] = folded
        out_ref[copy, width:] = jnp.broadcast_to(diagonal, (8, wide))


def path_kernel(rank_ref, path_ref, high_ref, low_ref):
    heights = path_ref.shape[0]
    row = iota(path_ref.shape[1:], 0)
    for height in range(heights):
        step = jnp.where(row < rank_ref[height], path_ref[height].astype(F32), 0.0)
        if height == 0:
            whole = step
        else:
            step = step.astype(BF16)
            whole = nn(high, step) + nn(low, step)
        high, low = halves(whole)
        high_ref[height] = high
        low_ref[height] = low


def near_kernel(
    rank_ref, place_ref, level_ref, parts_ref, bottom_ref, high_ref, low_ref, left_ref, sent_ref, first_ref, tiles
):
    nodes, width, _ = bottom_ref.shape
    wide = 2 * width
    half = width // 2
    targets = sent_ref.shape[0]
    heights = high_ref.shape[0]
    total = parts_ref[0]
    for part in range(1, parts_ref.shape[0]):
        total = total + parts_ref[part]
    folded = total[:width]
    diagonal = total[width : width + 1]
    turned = folded.T
    row = iota((width, width), 0)
    column = iota((width, width), 1)
    masked = []
    for node in range(nodes):
        pair, side = node // 2, node % 2
        here = folded[:, pair * width : (pair + 1) * width]
        there = turned[pair * width : (pair + 1) * width]
        if side == 0:
            gram = jnp.where(row <= column, here, there)
        else:
            centre = jnp.broadcast_to(diagonal[:, pair * width : (pair + 1) * width], (width, width))
            gram = jnp.where(row > column, here, jnp.where(row < column, there, centre))
        masked.append(keep_rank(gram, rank_ref[node]))
    bottom = halves(lift(masked, [bottom_ref[node] for node in range(nodes)]))
    lane = iota((1, wide), 1)
    lower = jnp.where(lane < width, rank_ref[1], rank_ref[3])
    diagonal = jnp.where((lane & (width - 1)) < lower, diagonal, 0.0)
    tiles[0] = jnp.concatenate([diagonal, jnp.zeros((7, wide), F32)], axis=0)
    parts = parts_ref.shape[0]
    share = half // (2 * parts)
    for height in range(heights):
        path = (high_ref[height], low_ref[height])
        term = product(tn, path, halves(product(nn, bottom, path)))
        if height == 0:
            first_ref[...] = pack(term)
            continue
        square, centre = fold(term)
        packed = pack(square)
        mine = packed[:share]
        for part in range(1, parts):
            mine = jnp.where(level_ref[0] == part, packed[part * share : (part + 1) * share], mine)
        centre = jnp.concatenate([centre, jnp.zeros((1, wide - half), F32)], axis=1)
        tiles[height] = jnp.concatenate([diagonal, mine, centre, jnp.zeros((6 - share, wide), F32)], axis=0)

    row = iota((width, wide), 0)
    lane = iota((width, wide), 1)
    column = lane & (width - 1)
    low = lane < width
    upper = jnp.where(low, rank_ref[0], rank_ref[2])
    lower = jnp.where(low, rank_ref[1], rank_ref[3])
    kept = jnp.maximum(row, column) < jnp.where(row <= column, upper, lower)
    share_rows = jnp.where(kept, folded, 0.0).astype(BF16)
    place = place_ref[0]
    for target in range(targets):
        device = 2 * target + 1
        height = reach(device, 2 * targets)
        inside = jnp.right_shift(place, height) == device >> height
        sent_ref[target, :width] = share_rows
        sent_ref[target, width:] = tiles[jnp.where(inside, height - 1, 0)].astype(BF16)

    row = iota((width, width), 0)
    even_first = jnp.where(row < half, 2 * row, 2 * row - width + 1)
    order = (iota((width, width), 1) == even_first).astype(F32).astype(BF16)
    for node in range(nodes):
        left_ref[node] = nt(nn(order, masked[node].astype(BF16)).astype(BF16), order).astype(BF16)


def sum_kernel(received_ref, out_ref):
    sources, rows, _ = received_ref.shape
    total = received_ref[0, rows - 8 :].astype(F32)
    for source in range(1, sources):
        total = total + received_ref[source, rows - 8 :].astype(F32)
    out_ref[...] = total


def top_kernel(core_ref, received_ref, first_ref, other_ref, out_ref, scratch):
    parts, _, wide = received_ref.shape
    width = wide // 2
    half = width // 2
    share = half // (2 * parts)
    packed = jnp.concatenate([received_ref[part, 1 : 1 + share] for part in range(parts)], axis=0)
    high = unfold(unpack(packed), received_ref[0, 1 + share : 2 + share, :half])
    scratch[...] = jnp.where(core_ref[0] == 1, high, unpack(first_ref[...] + other_ref[...]))
    natural = jnp.concatenate([scratch[pl.ds(side, half, stride=2), :] for side in range(2)], axis=1)
    for tile in range(half):
        out_ref[:, tile * wide : (tile + 1) * wide] = natural[tile : tile + 1]


def project_kernel(
    owner_ref,
    column_ref,
    row_ref,
    core_ref,
    blocks_ref,
    own_ref,
    other_ref,
    left_ref,
    out_ref,
    spread,
    result,
    triangles,
):
    step = pl.program_id(0)
    count, flat = blocks_ref.shape
    width = left_ref.shape[1]
    wide = 2 * width
    tiles = flat // wide
    row = iota((width, wide), 0)
    lane = iota((width, wide), 1)
    column = lane & (width - 1)
    low = lane < width

    @pl.when(step == 0)
    def _():
        triangles[0, 0] = (row <= column).astype(F32)
        triangles[0, 1] = (row < column).astype(F32)
        triangles[0, 2] = jnp.zeros((width, wide), F32)
        triangles[1, 0] = (row > column).astype(F32)
        triangles[1, 1] = (row > column).astype(F32)
        triangles[1, 2] = (row == column).astype(F32)

    for tile in range(tiles):
        spread[tile * count : (tile + 1) * count, :] = blocks_ref[:, tile * wide : (tile + 1) * wide].astype(F32)

    def right_product(index):
        block = step * count + index
        owner = owner_ref[block]
        cluster = column_ref[block]
        pair = jnp.right_shift(cluster, 1)
        side = cluster & 1
        source = jnp.right_shift(owner, 1)
        at_home = (owner & 1) == core_ref[0]
        folded = jnp.where(at_home, own_ref[source, :width], other_ref[source, :width]).astype(F32)
        centre = jnp.where(at_home, own_ref[source, width:], other_ref[source, width:]).astype(F32)[:1]
        wanted = low == (pair == 0)
        folded = jnp.where(wanted, folded, pltpu.roll(folded, width, 1))
        centre = jnp.where(wanted[:1], centre, pltpu.roll(centre, width, 1))
        direct = (folded * triangles[side, 0] + centre * triangles[side, 2]).astype(BF16)
        mirrored = (folded * triangles[side, 1]).astype(BF16)[:, :width]
        here = spread[pl.ds(index, tiles, stride=count), :]
        rows = jnp.concatenate([here, pltpu.roll(here, width, 1)], axis=0).astype(BF16)[:, :width]
        return nn(rows, direct) + nt(rows, jnp.concatenate([mirrored, mirrored], axis=0))

    for first in range(0, count, TOGETHER):
        group = range(first, first + TOGETHER)
        carried = [right_product(index).astype(BF16) for index in group]
        for index, value in zip(group, carried):
            full = nn(left_ref[row_ref[step * count + index]], value)
            result[pl.ds(index, tiles, stride=count), :] = jnp.where(low[:tiles], full[:tiles], full[tiles:])
    for tile in range(tiles):
        out_ref[:, tile * wide : (tile + 1) * wide] = result[tile * count : (tile + 1) * count, :]


def shape(dims, dtype):
    return jax.ShapeDtypeStruct(dims, dtype)


def on_device(
    basis,
    bottom_transfer,
    bottom_rank,
    upper_transfer,
    upper_rank,
    couplings,
    row_cluster,
    column_owner,
    column_cluster,
):
    nodes, width, _ = basis.shape
    wide = 2 * width
    half = width // 2
    branches = lax.axis_size("branch")
    parts = lax.axis_size("level")
    levels = branches.bit_length() - 1
    me_branch = lax.axis_index("branch")
    me_level = lax.axis_index("level")
    core = me_branch & 1
    blk = couplings.shape[0]
    same_core = [list(range(c, branches, 2)) for c in range(2)]
    partners = [(i, i ^ 1) for i in range(branches)]

    partial_sums = pl.pallas_call(
        gram_kernel,
        out_shape=shape((parts, width + 8, wide), F32),
        in_specs=[VMEM],
        out_specs=VMEM,
        compiler_params=SMALL,
        name="gram",
    )(basis)
    partial_sums, upper_transfer, upper_rank, bottom_transfer = lax.optimization_barrier(
        (partial_sums, upper_transfer, upper_rank, bottom_transfer)
    )
    gathered = lax.all_to_all(partial_sums, "level", 0, 0)
    heights = jnp.arange(levels, dtype=jnp.int32)
    slots = 2 * branches - jnp.right_shift(2 * branches, heights) + jnp.right_shift(me_branch, heights)
    path = jnp.take(upper_transfer, slots, axis=0).reshape(levels, width, width)
    path_high, path_low = pl.pallas_call(
        path_kernel,
        out_shape=[shape((levels, width, width), BF16)] * 2,
        in_specs=[SMEM, VMEM],
        out_specs=[VMEM, VMEM],
        compiler_params=SMALL,
        name="path",
    )(jnp.take(upper_rank, slots, axis=0), path)
    left, sent, first = pl.pallas_call(
        near_kernel,
        out_shape=[
            shape((nodes, width, width), BF16),
            shape((branches // 2, width + 8, wide), BF16),
            shape((half, wide), F32),
        ],
        in_specs=[SMEM, SMEM, SMEM, VMEM, VMEM, VMEM, VMEM],
        out_specs=[VMEM, VMEM, VMEM],
        scratch_shapes=[pltpu.VMEM((levels, 8, wide), F32)],
        compiler_params=SMALL,
        name="near",
    )(
        bottom_rank,
        me_branch[None],
        me_level[None],
        gathered,
        bottom_transfer.reshape(nodes, width, width),
        path_high,
        path_low,
    )
    own = lax.all_to_all(sent, "branch", 0, 0, axis_index_groups=same_core)
    first_other = lax.ppermute(first, "branch", partners)
    own, first_other = lax.optimization_barrier((own, first_other))
    summed = pl.pallas_call(
        sum_kernel,
        out_shape=shape((8, wide), F32),
        in_specs=[VMEM],
        out_specs=VMEM,
        compiler_params=SMALL,
        name="sum",
    )(own)
    summed_other = lax.ppermute(summed, "branch", partners)
    other = lax.ppermute(own, "branch", partners)
    quarters = lax.all_to_all(
        jnp.broadcast_to((summed + summed_other)[None], (parts, 8, wide)), "level", 0, 0
    )
    upper_grams = pl.pallas_call(
        top_kernel,
        out_shape=shape((1, width * width), F32),
        in_specs=[SMEM, VMEM, VMEM, VMEM],
        out_specs=VMEM,
        scratch_shapes=[pltpu.VMEM((width, width), F32)],
        compiler_params=SMALL,
        name="top",
    )(core[None], quarters, first, first_other)

    whole = pl.BlockSpec(own.shape, lambda i, *_: (0, 0, 0))
    projected = pl.pallas_call(
        project_kernel,
        out_shape=shape((blk, width * width), F32),
        grid_spec=pltpu.PrefetchScalarGridSpec(
            num_scalar_prefetch=4,
            grid=(blk // ROWS,),
            in_specs=[
                pl.BlockSpec((ROWS, width * width), lambda i, *_: (i, 0)),
                whole,
                whole,
                pl.BlockSpec((nodes, width, width), lambda i, *_: (0, 0, 0)),
            ],
            out_specs=pl.BlockSpec((ROWS, width * width), lambda i, *_: (i, 0)),
            scratch_shapes=[
                pltpu.VMEM((ROWS * half, wide), F32),
                pltpu.VMEM((ROWS * half, wide), F32),
                pltpu.VMEM((2, 3, width, wide), F32),
            ],
        ),
        compiler_params=pltpu.CompilerParams(vmem_limit_bytes=12 * 1024 * 1024),
        name="project",
    )(column_owner[:, 0], column_cluster, row_cluster, core[None], couplings, own, other, left)
    return (upper_grams, projected)


def solution(mesh):
    placed = (
        P("branch", None, "level"),
        P("branch", None),
        P("branch"),
        P(),
        P(),
        P(("branch", "level"), None),
        P(("branch", "level")),
        P(("branch", "level"), None),
        P(("branch", "level")),
    )
    return jax.shard_map(
        on_device,
        mesh=mesh,
        in_specs=placed,
        out_specs=(P("branch", None), P(("branch", "level"), None)),
        check_vma=False,
    )
```

```python
import jax
import jax.numpy as jnp
from jax import lax
from jax.experimental import pallas as pl
from jax.experimental.pallas import tpu as pltpu
from jax.sharding import PartitionSpec as P

VMEM = pl.BlockSpec(memory_space=pltpu.VMEM)
SMEM = pl.BlockSpec(memory_space=pltpu.SMEM)
SMALL = pltpu.CompilerParams(vmem_limit_bytes=8 * 1024 * 1024)
ROWS = 16
F32 = jnp.float32
BF16 = jnp.bfloat16


def iota(shape, axis):
    return lax.broadcasted_iota(jnp.int32, shape, axis)


def nn(a, b):
    return jnp.dot(a, b, preferred_element_type=F32)


def nt(a, b):
    return lax.dot_general(a, b, (((1,), (1,)), ((), ())), preferred_element_type=F32)


def tn(a, b):
    return lax.dot_general(a, b, (((0,), (0,)), ((), ())), preferred_element_type=F32)


def halves(x):
    high = x.astype(BF16)
    return high, (x - high.astype(F32)).astype(BF16)


def keep_rank(gram, rank):
    return jnp.where((iota(gram.shape, 0) < rank) & (iota(gram.shape, 1) < rank), gram, 0.0)


def lift(masked, transfer):
    inner = []
    for gram, mat in zip(masked, transfer):
        high, low = halves(gram)
        inner.append(nn(high, mat) + nn(low, mat))
    high, low = halves(jnp.concatenate(inner, axis=0))
    mats = jnp.concatenate(transfer, axis=0)
    return tn(mats, high) + tn(mats, low)


def product(multiply, a, b):
    return multiply(a[0], b[0]) + (multiply(a[0], b[1]) + multiply(a[1], b[0]))


def fold(square):
    half = square.shape[0] // 2
    row, column = iota((half, half), 0), iota((half, half), 1)
    first = square[:half, :half]
    mixed = jnp.where(row < column, first, square[half:, half:])
    centre = jnp.sum(jnp.where(row == column, first, 0.0), axis=0, keepdims=True)
    return jnp.concatenate([mixed, square[:half, half:]], axis=1), centre


def unfold(folded, centre):
    half = folded.shape[0]
    row, column = iota((half, half), 0), iota((half, half), 1)
    turned = folded.T
    mixed, mixed_turned = folded[:, :half], turned[:half]
    first = jnp.where(row < column, mixed, jnp.where(row > column, mixed_turned, centre))
    last = jnp.where(row >= column, mixed, mixed_turned)
    top = jnp.concatenate([first, folded[:, half:]], axis=1)
    return jnp.concatenate([top, jnp.concatenate([turned[half:], last], axis=1)], axis=0)


def pack(square):
    half = square.shape[0] // 2
    return jnp.concatenate([square[:half], square[half:]], axis=1)


def unpack(packed):
    half = packed.shape[1] // 2
    return jnp.concatenate([packed[:, :half], packed[:, half:]], axis=0)


def reach(index, count):
    return (index ^ ((index + 1) % count)).bit_length()


def gram_kernel(basis_ref, out_ref):
    copies = out_ref.shape[0]
    width = basis_ref.shape[1]
    wide = 2 * width
    row = iota((width, wide), 0)
    lane = iota((width, wide), 1)
    column = lane & (width - 1)
    sides = []
    for side in range(2):
        both = jnp.concatenate([basis_ref[side], basis_ref[side + 2]], axis=0)
        crossed = nt(both, both)
        sides.append(jnp.where(lane < width, crossed[:width], crossed[width:]))
    folded = jnp.where(row <= column, sides[0], sides[1])
    diagonal = jnp.sum(jnp.where(row == column, sides[1], 0.0), axis=0, keepdims=True)
    for copy in range(copies):
        out_ref[copy, :width] = folded
        out_ref[copy, width:] = jnp.broadcast_to(diagonal, (8, wide))


def path_kernel(rank_ref, path_ref, high_ref, low_ref):
    heights = path_ref.shape[0]
    row = iota(path_ref.shape[1:], 0)
    for height in range(heights):
        step = jnp.where(row < rank_ref[height], path_ref[height].astype(F32), 0.0)
        if height == 0:
            whole = step
        else:
            step = step.astype(BF16)
            whole = nn(high, step) + nn(low, step)
        high, low = halves(whole)
        high_ref[height] = high
        low_ref[height] = low


def near_kernel(
    rank_ref, place_ref, level_ref, parts_ref, bottom_ref, high_ref, low_ref, left_ref, sent_ref, first_ref, tiles
):
    nodes, width, _ = bottom_ref.shape
    wide = 2 * width
    half = width // 2
    targets = sent_ref.shape[0]
    heights = high_ref.shape[0]
    total = parts_ref[0]
    for part in range(1, parts_ref.shape[0]):
        total = total + parts_ref[part]
    folded = total[:width]
    diagonal = total[width : width + 1]
    turned = folded.T
    row = iota((width, width), 0)
    column = iota((width, width), 1)
    masked = []
    for node in range(nodes):
        pair, side = node // 2, node % 2
        here = folded[:, pair * width : (pair + 1) * width]
        there = turned[pair * width : (pair + 1) * width]
        if side == 0:
            gram = jnp.where(row <= column, here, there)
        else:
            centre = jnp.broadcast_to(diagonal[:, pair * width : (pair + 1) * width], (width, width))
            gram = jnp.where(row > column, here, jnp.where(row < column, there, centre))
        masked.append(keep_rank(gram, rank_ref[node]))
    bottom = halves(lift(masked, [bottom_ref[node] for node in range(nodes)]))
    lane = iota((1, wide), 1)
    lower = jnp.where(lane < width, rank_ref[1], rank_ref[3])
    diagonal = jnp.where((lane & (width - 1)) < lower, diagonal, 0.0)
    tiles[0] = jnp.concatenate([diagonal, jnp.zeros((7, wide), F32)], axis=0)
    parts = parts_ref.shape[0]
    share = half // (2 * parts)
    for height in range(heights):
        path = (high_ref[height], low_ref[height])
        term = product(tn, path, halves(product(nn, bottom, path)))
        if height == 0:
            first_ref[...] = pack(term)
            continue
        square, centre = fold(term)
        packed = pack(square)
        mine = packed[:share]
        for part in range(1, parts):
            mine = jnp.where(level_ref[0] == part, packed[part * share : (part + 1) * share], mine)
        centre = jnp.concatenate([centre, jnp.zeros((1, wide - half), F32)], axis=1)
        tiles[height] = jnp.concatenate([diagonal, mine, centre, jnp.zeros((6 - share, wide), F32)], axis=0)

    row = iota((width, wide), 0)
    lane = iota((width, wide), 1)
    column = lane & (width - 1)
    low = lane < width
    upper = jnp.where(low, rank_ref[0], rank_ref[2])
    lower = jnp.where(low, rank_ref[1], rank_ref[3])
    kept = jnp.maximum(row, column) < jnp.where(row <= column, upper, lower)
    share_rows = jnp.where(kept, folded, 0.0).astype(BF16)
    place = place_ref[0]
    for target in range(targets):
        device = 2 * target + 1
        height = reach(device, 2 * targets)
        inside = jnp.right_shift(place, height) == device >> height
        sent_ref[target, :width] = share_rows
        sent_ref[target, width:] = tiles[jnp.where(inside, height - 1, 0)].astype(BF16)

    row = iota((width, width), 0)
    even_first = jnp.where(row < half, 2 * row, 2 * row - width + 1)
    order = (iota((width, width), 1) == even_first).astype(F32).astype(BF16)
    for node in range(nodes):
        left_ref[node] = nt(nn(order, masked[node].astype(BF16)).astype(BF16), order).astype(BF16)


def sum_kernel(received_ref, out_ref):
    sources, rows, _ = received_ref.shape
    total = received_ref[0, rows - 8 :].astype(F32)
    for source in range(1, sources):
        total = total + received_ref[source, rows - 8 :].astype(F32)
    for copy in range(out_ref.shape[0]):
        out_ref[copy] = total


def top_kernel(core_ref, received_ref, first_ref, other_ref, out_ref, scratch):
    parts = received_ref.shape[0] // 2
    wide = received_ref.shape[2]
    width = wide // 2
    half = width // 2
    share = half // (2 * parts)
    sums = [received_ref[part] + received_ref[parts + part] for part in range(parts)]
    packed = jnp.concatenate([value[1 : 1 + share] for value in sums], axis=0)
    high = unfold(unpack(packed), sums[0][1 + share : 2 + share, :half])
    scratch[...] = jnp.where(core_ref[0] == 1, high, unpack(first_ref[...] + other_ref[...]))
    natural = jnp.concatenate([scratch[pl.ds(side, half, stride=2), :] for side in range(2)], axis=1)
    for tile in range(half):
        out_ref[:, tile * wide : (tile + 1) * wide] = natural[tile : tile + 1]


def left_kernel(row_ref, column_ref, blocks_ref, left_ref, out_ref, spread):
    step = pl.program_id(0)
    count, flat = blocks_ref.shape
    width = left_ref.shape[1]
    wide = 2 * width
    tiles = flat // wide
    low = iota((width, wide), 1) < width
    for tile in range(tiles):
        spread[tile * count : (tile + 1) * count, :] = blocks_ref[:, tile * wide : (tile + 1) * wide].astype(F32)
    for index in range(count):
        block = step * count + index
        here = spread[pl.ds(index, tiles, stride=count), :]
        turned = pltpu.roll(here, width, 1)
        rows = jnp.where(
            low, jnp.concatenate([here, turned], axis=0), jnp.concatenate([turned, here], axis=0)
        ).astype(BF16)
        product = nn(left_ref[row_ref[block]], rows)
        out_ref[index] = jnp.where(low == (column_ref[block] < 2), product, 0.0).astype(BF16)


def project_kernel(
    owner_ref, column_ref, core_ref, rows_ref, own_ref, other_ref, out_ref, result, triangles
):
    step = pl.program_id(0)
    count, width, wide = rows_ref.shape
    tiles = width // 2
    low = iota((tiles, wide), 1) < width

    @pl.when(step == 0)
    def _():
        row = iota((width, wide), 0)
        column = iota((width, wide), 1) & (width - 1)
        triangles[0, 0] = (row <= column).astype(F32).astype(BF16)
        triangles[0, 1] = (row < column).astype(F32).astype(BF16)
        triangles[0, 2] = jnp.zeros((width, wide), BF16)
        triangles[1, 0] = (row > column).astype(F32).astype(BF16)
        triangles[1, 1] = (row > column).astype(F32).astype(BF16)
        triangles[1, 2] = (row == column).astype(F32).astype(BF16)

    for index in range(count):
        block = step * count + index
        owner = owner_ref[block]
        cluster = column_ref[block]
        first = cluster < 2
        side = cluster & 1
        source = jnp.right_shift(owner, 1)
        at_home = (owner & 1) == core_ref[0]
        folded = jnp.where(at_home, own_ref[source, :width], other_ref[source, :width])
        centre = jnp.where(at_home, own_ref[source, width:], other_ref[source, width:])[:1]
        direct = folded * triangles[side, 0] + centre * triangles[side, 2]
        mirrored = folded * triangles[side, 1]
        rows = rows_ref[index]
        full = nn(rows, jnp.concatenate([direct, direct], axis=0))
        full = full + nt(rows, jnp.concatenate([mirrored, mirrored], axis=0))
        top, bottom = full[:tiles], full[tiles:]
        stay = jnp.where(first, top, bottom)
        move = pltpu.roll(jnp.where(first, bottom, top), width, 1)
        result[pl.ds(index, tiles, stride=count), :] = jnp.where(low == first, stay, move)
    for tile in range(tiles):
        out_ref[:, tile * wide : (tile + 1) * wide] = result[tile * count : (tile + 1) * count, :]


def shape(dims, dtype):
    return jax.ShapeDtypeStruct(dims, dtype)


def on_device(
    basis,
    bottom_transfer,
    bottom_rank,
    upper_transfer,
    upper_rank,
    couplings,
    row_cluster,
    column_owner,
    column_cluster,
):
    nodes, width, _ = basis.shape
    wide = 2 * width
    half = width // 2
    branches = lax.axis_size("branch")
    parts = lax.axis_size("level")
    levels = branches.bit_length() - 1
    me_branch = lax.axis_index("branch")
    me_level = lax.axis_index("level")
    core = me_branch & 1
    blk = couplings.shape[0]
    same_core = [list(range(c, branches, 2)) for c in range(2)]
    same_chip = [list(range(2 * parts * chip, 2 * parts * (chip + 1))) for chip in range(branches // 2)]
    partners = [(i, i ^ 1) for i in range(branches)]

    partial_sums = pl.pallas_call(
        gram_kernel,
        out_shape=shape((parts, width + 8, wide), F32),
        in_specs=[VMEM],
        out_specs=VMEM,
        compiler_params=SMALL,
        name="gram",
    )(basis)
    partial_sums, upper_transfer, upper_rank, bottom_transfer = lax.optimization_barrier(
        (partial_sums, upper_transfer, upper_rank, bottom_transfer)
    )
    gathered = lax.all_to_all(partial_sums, "level", 0, 0)
    heights = jnp.arange(levels, dtype=jnp.int32)
    slots = 2 * branches - jnp.right_shift(2 * branches, heights) + jnp.right_shift(me_branch, heights)
    path = jnp.take(upper_transfer, slots, axis=0).reshape(levels, width, width)
    path_high, path_low = pl.pallas_call(
        path_kernel,
        out_shape=[shape((levels, width, width), BF16)] * 2,
        in_specs=[SMEM, VMEM],
        out_specs=[VMEM, VMEM],
        compiler_params=SMALL,
        name="path",
    )(jnp.take(upper_rank, slots, axis=0), path)
    left, sent, first = pl.pallas_call(
        near_kernel,
        out_shape=[
            shape((nodes, width, width), BF16),
            shape((branches // 2, width + 8, wide), BF16),
            shape((half, wide), F32),
        ],
        in_specs=[SMEM, SMEM, SMEM, VMEM, VMEM, VMEM, VMEM],
        out_specs=[VMEM, VMEM, VMEM],
        scratch_shapes=[pltpu.VMEM((levels, 8, wide), F32)],
        compiler_params=SMALL,
        name="near",
    )(
        bottom_rank,
        me_branch[None],
        me_level[None],
        gathered,
        bottom_transfer.reshape(nodes, width, width),
        path_high,
        path_low,
    )
    own = lax.all_to_all(sent, "branch", 0, 0, axis_index_groups=same_core)
    first_other = lax.ppermute(first, "branch", partners)
    square = pl.BlockSpec((ROWS, width, wide), lambda i, *_: (i, 0, 0))
    rows = pl.pallas_call(
        left_kernel,
        out_shape=shape((blk, width, wide), BF16),
        grid_spec=pltpu.PrefetchScalarGridSpec(
            num_scalar_prefetch=2,
            grid=(blk // ROWS,),
            in_specs=[
                pl.BlockSpec((ROWS, width * width), lambda i, *_: (i, 0)),
                pl.BlockSpec((nodes, width, width), lambda i, *_: (0, 0, 0)),
            ],
            out_specs=square,
            scratch_shapes=[pltpu.VMEM((ROWS * half, wide), F32)],
        ),
        compiler_params=SMALL,
        cost_estimate=pl.CostEstimate(
            flops=4 * blk * width**3, bytes_accessed=4 * blk * width * width, transcendentals=0
        ),
        name="left",
    )(row_cluster, column_cluster, couplings, left)
    own, first_other, rows = lax.optimization_barrier((own, first_other, rows))
    summed = pl.pallas_call(
        sum_kernel,
        out_shape=shape((2 * parts, 8, wide), F32),
        in_specs=[VMEM],
        out_specs=VMEM,
        compiler_params=SMALL,
        name="sum",
    )(own)
    other = lax.ppermute(own, "branch", partners)
    quarters = lax.all_to_all(summed, ("branch", "level"), 0, 0, axis_index_groups=same_chip)

    whole = pl.BlockSpec(own.shape, lambda i, *_: (0, 0, 0))
    projected = pl.pallas_call(
        project_kernel,
        out_shape=shape((blk, width * width), F32),
        grid_spec=pltpu.PrefetchScalarGridSpec(
            num_scalar_prefetch=3,
            grid=(blk // ROWS,),
            in_specs=[square, whole, whole],
            out_specs=pl.BlockSpec((ROWS, width * width), lambda i, *_: (i, 0)),
            scratch_shapes=[
                pltpu.VMEM((ROWS * half, wide), F32),
                pltpu.VMEM((2, 3, width, wide), BF16),
            ],
        ),
        compiler_params=pltpu.CompilerParams(vmem_limit_bytes=56 * 1024 * 1024),
        cost_estimate=pl.CostEstimate(
            flops=8 * blk * width**3, bytes_accessed=6 * blk * width * width, transcendentals=0
        ),
        name="project",
    )(column_owner[:, 0], column_cluster, core[None], rows, own, other)
    projected, quarters = lax.optimization_barrier((projected, quarters))
    upper_grams = pl.pallas_call(
        top_kernel,
        out_shape=shape((1, width * width), F32),
        in_specs=[SMEM, VMEM, VMEM, VMEM],
        out_specs=VMEM,
        scratch_shapes=[pltpu.VMEM((width, width), F32)],
        compiler_params=SMALL,
        name="top",
    )(core[None], quarters, first, first_other)
    return (upper_grams, projected)


def solution(mesh):
    placed = (
        P("branch", None, "level"),
        P("branch", None),
        P("branch"),
        P(),
        P(),
        P(("branch", "level"), None),
        P(("branch", "level")),
        P(("branch", "level"), None),
        P(("branch", "level")),
    )
    return jax.shard_map(
        on_device,
        mesh=mesh,
        in_specs=placed,
        out_specs=(P("branch", None), P(("branch", "level"), None)),
        check_vma=False,
    )
```

```python
import jax
import jax.numpy as jnp
from jax import lax
from jax.experimental import pallas as pl
from jax.experimental.pallas import tpu as pltpu
from jax.sharding import PartitionSpec as P

VMEM = pl.BlockSpec(memory_space=pltpu.VMEM)
SMEM = pl.BlockSpec(memory_space=pltpu.SMEM)
SMALL = pltpu.CompilerParams(vmem_limit_bytes=8 * 1024 * 1024)
ROWS = 16
F32 = jnp.float32
BF16 = jnp.bfloat16


def iota(shape, axis):
    return lax.broadcasted_iota(jnp.int32, shape, axis)


def nn(a, b):
    return jnp.dot(a, b, preferred_element_type=F32)


def nt(a, b):
    return lax.dot_general(a, b, (((1,), (1,)), ((), ())), preferred_element_type=F32)


def tn(a, b):
    return lax.dot_general(a, b, (((0,), (0,)), ((), ())), preferred_element_type=F32)


def halves(x):
    high = x.astype(BF16)
    return high, (x - high.astype(F32)).astype(BF16)


def keep_rank(gram, rank):
    return jnp.where((iota(gram.shape, 0) < rank) & (iota(gram.shape, 1) < rank), gram, 0.0)


def lift(masked, transfer):
    inner = []
    for gram, mat in zip(masked, transfer):
        high, low = halves(gram)
        inner.append(nn(high, mat) + nn(low, mat))
    high, low = halves(jnp.concatenate(inner, axis=0))
    mats = jnp.concatenate(transfer, axis=0)
    return tn(mats, high) + tn(mats, low)


def product(multiply, a, b):
    return multiply(a[0], b[0]) + (multiply(a[0], b[1]) + multiply(a[1], b[0]))


def fold(square):
    half = square.shape[0] // 2
    row, column = iota((half, half), 0), iota((half, half), 1)
    first = square[:half, :half]
    mixed = jnp.where(row < column, first, square[half:, half:])
    centre = jnp.sum(jnp.where(row == column, first, 0.0), axis=0, keepdims=True)
    return jnp.concatenate([mixed, square[:half, half:]], axis=1), centre


def unfold(folded, centre):
    half = folded.shape[0]
    row, column = iota((half, half), 0), iota((half, half), 1)
    turned = folded.T
    mixed, mixed_turned = folded[:, :half], turned[:half]
    first = jnp.where(row < column, mixed, jnp.where(row > column, mixed_turned, centre))
    last = jnp.where(row >= column, mixed, mixed_turned)
    top = jnp.concatenate([first, folded[:, half:]], axis=1)
    return jnp.concatenate([top, jnp.concatenate([turned[half:], last], axis=1)], axis=0)


def pack(square):
    half = square.shape[0] // 2
    return jnp.concatenate([square[:half], square[half:]], axis=1)


def unpack(packed):
    half = packed.shape[1] // 2
    return jnp.concatenate([packed[:, :half], packed[:, half:]], axis=0)


def reach(index, count):
    return (index ^ ((index + 1) % count)).bit_length()


def gram_kernel(basis_ref, out_ref):
    copies = out_ref.shape[0]
    width = basis_ref.shape[1]
    wide = 2 * width
    row = iota((width, wide), 0)
    lane = iota((width, wide), 1)
    column = lane & (width - 1)
    sides = []
    for side in range(2):
        both = jnp.concatenate([basis_ref[side], basis_ref[side + 2]], axis=0)
        crossed = nt(both, both)
        sides.append(jnp.where(lane < width, crossed[:width], crossed[width:]))
    folded = jnp.where(row <= column, sides[0], sides[1])
    diagonal = jnp.sum(jnp.where(row == column, sides[1], 0.0), axis=0, keepdims=True)
    for copy in range(copies):
        out_ref[copy, :width] = folded
        out_ref[copy, width:] = jnp.broadcast_to(diagonal, (8, wide))


def path_kernel(rank_ref, path_ref, high_ref, low_ref):
    heights = path_ref.shape[0]
    row = iota(path_ref.shape[1:], 0)
    for height in range(heights):
        step = jnp.where(row < rank_ref[height], path_ref[height].astype(F32), 0.0)
        if height == 0:
            whole = step
        else:
            step = step.astype(BF16)
            whole = nn(high, step) + nn(low, step)
        high, low = halves(whole)
        high_ref[height] = high
        low_ref[height] = low


def near_kernel(
    rank_ref, place_ref, level_ref, parts_ref, bottom_ref, high_ref, low_ref, left_ref, sent_ref, first_ref, tiles
):
    nodes, width, _ = bottom_ref.shape
    wide = 2 * width
    half = width // 2
    targets = sent_ref.shape[0]
    heights = high_ref.shape[0]
    total = parts_ref[0]
    for part in range(1, parts_ref.shape[0]):
        total = total + parts_ref[part]
    folded = total[:width]
    diagonal = total[width : width + 1]
    turned = folded.T
    row = iota((width, width), 0)
    column = iota((width, width), 1)
    masked = []
    for node in range(nodes):
        pair, side = node // 2, node % 2
        here = folded[:, pair * width : (pair + 1) * width]
        there = turned[pair * width : (pair + 1) * width]
        if side == 0:
            gram = jnp.where(row <= column, here, there)
        else:
            centre = jnp.broadcast_to(diagonal[:, pair * width : (pair + 1) * width], (width, width))
            gram = jnp.where(row > column, here, jnp.where(row < column, there, centre))
        masked.append(keep_rank(gram, rank_ref[node]))
    bottom = halves(lift(masked, [bottom_ref[node] for node in range(nodes)]))
    lane = iota((1, wide), 1)
    lower = jnp.where(lane < width, rank_ref[1], rank_ref[3])
    diagonal = jnp.where((lane & (width - 1)) < lower, diagonal, 0.0)
    tiles[0] = jnp.concatenate([diagonal, jnp.zeros((7, wide), F32)], axis=0)
    parts = parts_ref.shape[0]
    share = half // (2 * parts)
    for height in range(heights):
        path = (high_ref[height], low_ref[height])
        term = product(tn, path, halves(product(nn, bottom, path)))
        if height == 0:
            first_ref[...] = pack(term)
            continue
        square, centre = fold(term)
        packed = pack(square)
        mine = packed[:share]
        for part in range(1, parts):
            mine = jnp.where(level_ref[0] == part, packed[part * share : (part + 1) * share], mine)
        centre = jnp.concatenate([centre, jnp.zeros((1, wide - half), F32)], axis=1)
        tiles[height] = jnp.concatenate([diagonal, mine, centre, jnp.zeros((6 - share, wide), F32)], axis=0)

    row = iota((width, wide), 0)
    lane = iota((width, wide), 1)
    column = lane & (width - 1)
    low = lane < width
    upper = jnp.where(low, rank_ref[0], rank_ref[2])
    lower = jnp.where(low, rank_ref[1], rank_ref[3])
    kept = jnp.maximum(row, column) < jnp.where(row <= column, upper, lower)
    share_rows = jnp.where(kept, folded, 0.0).astype(BF16)
    place = place_ref[0]
    for target in range(targets):
        device = 2 * target + 1
        height = reach(device, 2 * targets)
        inside = jnp.right_shift(place, height) == device >> height
        sent_ref[target, :width] = share_rows
        sent_ref[target, width:] = tiles[jnp.where(inside, height - 1, 0)].astype(BF16)

    row = iota((width, width), 0)
    even_first = jnp.where(row < half, 2 * row, 2 * row - width + 1)
    order = (iota((width, width), 1) == even_first).astype(F32).astype(BF16)
    for node in range(nodes):
        left_ref[node] = nt(nn(order, masked[node].astype(BF16)).astype(BF16), order).astype(BF16)


def sum_kernel(received_ref, out_ref):
    sources, rows, _ = received_ref.shape
    total = received_ref[0, rows - 8 :].astype(F32)
    for source in range(1, sources):
        total = total + received_ref[source, rows - 8 :].astype(F32)
    for copy in range(out_ref.shape[0]):
        out_ref[copy] = total


def top_kernel(core_ref, received_ref, first_ref, other_ref, out_ref, scratch):
    parts = received_ref.shape[0] // 2
    wide = received_ref.shape[2]
    width = wide // 2
    half = width // 2
    share = half // (2 * parts)
    sums = [received_ref[part] + received_ref[parts + part] for part in range(parts)]
    packed = jnp.concatenate([value[1 : 1 + share] for value in sums], axis=0)
    high = unfold(unpack(packed), sums[0][1 + share : 2 + share, :half])
    scratch[...] = jnp.where(core_ref[0] == 1, high, unpack(first_ref[...] + other_ref[...]))
    natural = jnp.concatenate([scratch[pl.ds(side, half, stride=2), :] for side in range(2)], axis=1)
    for tile in range(half):
        out_ref[:, tile * wide : (tile + 1) * wide] = natural[tile : tile + 1]


def left_kernel(row_ref, blocks_ref, left_ref, out_ref, spread):
    step = pl.program_id(0)
    count, flat = blocks_ref.shape
    width = left_ref.shape[1]
    wide = 2 * width
    tiles = flat // wide
    low = iota((width, wide), 1) < width
    for tile in range(tiles):
        spread[tile * count : (tile + 1) * count, :] = blocks_ref[:, tile * wide : (tile + 1) * wide].astype(F32)
    for index in range(count):
        block = step * count + index
        here = spread[pl.ds(index, tiles, stride=count), :]
        turned = pltpu.roll(here, width, 1)
        rows = jnp.where(
            low, jnp.concatenate([here, turned], axis=0), jnp.concatenate([turned, here], axis=0)
        ).astype(BF16)
        out_ref[index] = nn(left_ref[row_ref[block]], rows).astype(BF16)


def project_kernel(
    owner_ref, column_ref, core_ref, rows_ref, own_ref, other_ref, out_ref, result, triangles
):
    step = pl.program_id(0)
    count, width, wide = rows_ref.shape
    tiles = width // 2

    @pl.when(step == 0)
    def _():
        row = iota((width, wide), 0)
        lane = iota((width, wide), 1)
        column = lane & (width - 1)
        for cluster in range(triangles.shape[0]):
            mine = (lane < width) == (cluster < 2)
            if cluster % 2 == 0:
                parts = (row <= column, row < column, row < 0)
            else:
                parts = (row > column, row > column, row == column)
            for index, part in enumerate(parts):
                triangles[cluster, index] = (mine & part).astype(F32).astype(BF16)

    for index in range(count):
        block = step * count + index
        owner = owner_ref[block]
        cluster = column_ref[block]
        first = cluster < 2
        source = jnp.right_shift(owner, 1)
        at_home = (owner & 1) == core_ref[0]
        folded = jnp.where(at_home, own_ref[source, :width], other_ref[source, :width])
        centre = jnp.where(at_home, own_ref[source, width:], other_ref[source, width:])[:1]
        direct = folded * triangles[cluster, 0] + centre * triangles[cluster, 2]
        mirrored = folded * triangles[cluster, 1]
        rows = rows_ref[index]
        one = nn(rows[:, :width], direct)
        two = jnp.concatenate([nt(rows, mirrored), jnp.zeros((width, width), F32)], axis=1)
        stay = jnp.where(first, one[:tiles], one[tiles:]) + two[:tiles]
        move = jnp.where(first, one[tiles:], one[:tiles]) + two[tiles:]
        result[pl.ds(index, tiles, stride=count), :] = stay + pltpu.roll(move, width, 1)
    for tile in range(tiles):
        out_ref[:, tile * wide : (tile + 1) * wide] = result[tile * count : (tile + 1) * count, :]


def shape(dims, dtype):
    return jax.ShapeDtypeStruct(dims, dtype)


def on_device(
    basis,
    bottom_transfer,
    bottom_rank,
    upper_transfer,
    upper_rank,
    couplings,
    row_cluster,
    column_owner,
    column_cluster,
):
    nodes, width, _ = basis.shape
    wide = 2 * width
    half = width // 2
    branches = lax.axis_size("branch")
    parts = lax.axis_size("level")
    levels = branches.bit_length() - 1
    me_branch = lax.axis_index("branch")
    me_level = lax.axis_index("level")
    core = me_branch & 1
    blk = couplings.shape[0]
    same_core = [list(range(c, branches, 2)) for c in range(2)]
    same_chip = [list(range(2 * parts * chip, 2 * parts * (chip + 1))) for chip in range(branches // 2)]
    partners = [(i, i ^ 1) for i in range(branches)]

    partial_sums = pl.pallas_call(
        gram_kernel,
        out_shape=shape((parts, width + 8, wide), F32),
        in_specs=[VMEM],
        out_specs=VMEM,
        compiler_params=SMALL,
        name="gram",
    )(basis)
    partial_sums, upper_transfer, upper_rank, bottom_transfer = lax.optimization_barrier(
        (partial_sums, upper_transfer, upper_rank, bottom_transfer)
    )
    gathered = lax.all_to_all(partial_sums, "level", 0, 0)
    heights = jnp.arange(levels, dtype=jnp.int32)
    slots = 2 * branches - jnp.right_shift(2 * branches, heights) + jnp.right_shift(me_branch, heights)
    path = jnp.take(upper_transfer, slots, axis=0).reshape(levels, width, width)
    path_high, path_low = pl.pallas_call(
        path_kernel,
        out_shape=[shape((levels, width, width), BF16)] * 2,
        in_specs=[SMEM, VMEM],
        out_specs=[VMEM, VMEM],
        compiler_params=SMALL,
        name="path",
    )(jnp.take(upper_rank, slots, axis=0), path)
    left, sent, first = pl.pallas_call(
        near_kernel,
        out_shape=[
            shape((nodes, width, width), BF16),
            shape((branches // 2, width + 8, wide), BF16),
            shape((half, wide), F32),
        ],
        in_specs=[SMEM, SMEM, SMEM, VMEM, VMEM, VMEM, VMEM],
        out_specs=[VMEM, VMEM, VMEM],
        scratch_shapes=[pltpu.VMEM((levels, 8, wide), F32)],
        compiler_params=SMALL,
        name="near",
    )(
        bottom_rank,
        me_branch[None],
        me_level[None],
        gathered,
        bottom_transfer.reshape(nodes, width, width),
        path_high,
        path_low,
    )
    own = lax.all_to_all(sent, "branch", 0, 0, axis_index_groups=same_core)
    first_other = lax.ppermute(first, "branch", partners)
    square = pl.BlockSpec((ROWS, width, wide), lambda i, *_: (i, 0, 0))
    rows = pl.pallas_call(
        left_kernel,
        out_shape=shape((blk, width, wide), BF16),
        grid_spec=pltpu.PrefetchScalarGridSpec(
            num_scalar_prefetch=1,
            grid=(blk // ROWS,),
            in_specs=[
                pl.BlockSpec((ROWS, width * width), lambda i, *_: (i, 0)),
                pl.BlockSpec((nodes, width, width), lambda i, *_: (0, 0, 0)),
            ],
            out_specs=square,
            scratch_shapes=[pltpu.VMEM((ROWS * half, wide), F32)],
        ),
        compiler_params=SMALL,
        cost_estimate=pl.CostEstimate(
            flops=4 * blk * width**3, bytes_accessed=4 * blk * width * width, transcendentals=0
        ),
        name="left",
    )(row_cluster, couplings, left)
    own, first_other, rows = lax.optimization_barrier((own, first_other, rows))
    summed = pl.pallas_call(
        sum_kernel,
        out_shape=shape((2 * parts, 8, wide), F32),
        in_specs=[VMEM],
        out_specs=VMEM,
        compiler_params=SMALL,
        name="sum",
    )(own)
    other = lax.ppermute(own, "branch", partners)
    quarters = lax.all_to_all(summed, ("branch", "level"), 0, 0, axis_index_groups=same_chip)

    whole = pl.BlockSpec(own.shape, lambda i, *_: (0, 0, 0))
    projected = pl.pallas_call(
        project_kernel,
        out_shape=shape((blk, width * width), F32),
        grid_spec=pltpu.PrefetchScalarGridSpec(
            num_scalar_prefetch=3,
            grid=(blk // ROWS,),
            in_specs=[square, whole, whole],
            out_specs=pl.BlockSpec((ROWS, width * width), lambda i, *_: (i, 0)),
            scratch_shapes=[
                pltpu.VMEM((ROWS * half, wide), F32),
                pltpu.VMEM((nodes, 3, width, wide), BF16),
            ],
        ),
        compiler_params=pltpu.CompilerParams(vmem_limit_bytes=56 * 1024 * 1024),
        cost_estimate=pl.CostEstimate(
            flops=8 * blk * width**3, bytes_accessed=6 * blk * width * width, transcendentals=0
        ),
        name="project",
    )(column_owner[:, 0], column_cluster, core[None], rows, own, other)
    projected, quarters = lax.optimization_barrier((projected, quarters))
    upper_grams = pl.pallas_call(
        top_kernel,
        out_shape=shape((1, width * width), F32),
        in_specs=[SMEM, VMEM, VMEM, VMEM],
        out_specs=VMEM,
        scratch_shapes=[pltpu.VMEM((width, width), F32)],
        compiler_params=SMALL,
        name="top",
    )(core[None], quarters, first, first_other)
    return (upper_grams, projected)


def solution(mesh):
    placed = (
        P("branch", None, "level"),
        P("branch", None),
        P("branch"),
        P(),
        P(),
        P(("branch", "level"), None),
        P(("branch", "level")),
        P(("branch", "level"), None),
        P(("branch", "level")),
    )
    return jax.shard_map(
        on_device,
        mesh=mesh,
        in_specs=placed,
        out_specs=(P("branch", None), P(("branch", "level"), None)),
        check_vma=False,
    )
```

```python
import jax
import jax.numpy as jnp
from jax import lax
from jax.experimental import pallas as pl
from jax.experimental.pallas import tpu as pltpu
from jax.sharding import PartitionSpec as P

VMEM = pl.BlockSpec(memory_space=pltpu.VMEM)
SMEM = pl.BlockSpec(memory_space=pltpu.SMEM)
SMALL = pltpu.CompilerParams(vmem_limit_bytes=8 * 1024 * 1024)
ROWS = 16
F32 = jnp.float32
BF16 = jnp.bfloat16


def iota(shape, axis):
    return lax.broadcasted_iota(jnp.int32, shape, axis)


def nn(a, b):
    return jnp.dot(a, b, preferred_element_type=F32)


def nt(a, b):
    return lax.dot_general(a, b, (((1,), (1,)), ((), ())), preferred_element_type=F32)


def tn(a, b):
    return lax.dot_general(a, b, (((0,), (0,)), ((), ())), preferred_element_type=F32)


def halves(x):
    high = x.astype(BF16)
    return high, (x - high.astype(F32)).astype(BF16)


def keep_rank(gram, rank):
    return jnp.where((iota(gram.shape, 0) < rank) & (iota(gram.shape, 1) < rank), gram, 0.0)


def lift(masked, transfer):
    inner = []
    for gram, mat in zip(masked, transfer):
        high, low = halves(gram)
        inner.append(nn(high, mat) + nn(low, mat))
    high, low = halves(jnp.concatenate(inner, axis=0))
    mats = jnp.concatenate(transfer, axis=0)
    return tn(mats, high) + tn(mats, low)


def product(multiply, a, b):
    return multiply(a[0], b[0]) + (multiply(a[0], b[1]) + multiply(a[1], b[0]))


def fold(square):
    half = square.shape[0] // 2
    row, column = iota((half, half), 0), iota((half, half), 1)
    first = square[:half, :half]
    mixed = jnp.where(row < column, first, square[half:, half:])
    centre = jnp.sum(jnp.where(row == column, first, 0.0), axis=0, keepdims=True)
    return jnp.concatenate([mixed, square[:half, half:]], axis=1), centre


def unfold(folded, centre):
    half = folded.shape[0]
    row, column = iota((half, half), 0), iota((half, half), 1)
    turned = folded.T
    mixed, mixed_turned = folded[:, :half], turned[:half]
    first = jnp.where(row < column, mixed, jnp.where(row > column, mixed_turned, centre))
    last = jnp.where(row >= column, mixed, mixed_turned)
    top = jnp.concatenate([first, folded[:, half:]], axis=1)
    return jnp.concatenate([top, jnp.concatenate([turned[half:], last], axis=1)], axis=0)


def pack(square):
    half = square.shape[0] // 2
    return jnp.concatenate([square[:half], square[half:]], axis=1)


def unpack(packed):
    half = packed.shape[1] // 2
    return jnp.concatenate([packed[:, :half], packed[:, half:]], axis=0)


def reach(index, count):
    return (index ^ ((index + 1) % count)).bit_length()


def gram_kernel(basis_ref, out_ref):
    copies = out_ref.shape[0]
    width = basis_ref.shape[1]
    wide = 2 * width
    row = iota((width, wide), 0)
    lane = iota((width, wide), 1)
    column = lane & (width - 1)
    sides = []
    for side in range(2):
        both = jnp.concatenate([basis_ref[side], basis_ref[side + 2]], axis=0)
        crossed = nt(both, both)
        sides.append(jnp.where(lane < width, crossed[:width], crossed[width:]))
    folded = jnp.where(row <= column, sides[0], sides[1])
    diagonal = jnp.sum(jnp.where(row == column, sides[1], 0.0), axis=0, keepdims=True)
    for copy in range(copies):
        out_ref[copy, :width] = folded
        out_ref[copy, width:] = jnp.broadcast_to(diagonal, (8, wide))


def path_kernel(rank_ref, path_ref, high_ref, low_ref):
    heights = path_ref.shape[0]
    row = iota(path_ref.shape[1:], 0)
    for height in range(heights):
        step = jnp.where(row < rank_ref[height], path_ref[height].astype(F32), 0.0)
        if height == 0:
            whole = step
        else:
            step = step.astype(BF16)
            whole = nn(high, step) + nn(low, step)
        high, low = halves(whole)
        high_ref[height] = high
        low_ref[height] = low


def near_kernel(
    rank_ref, place_ref, level_ref, parts_ref, bottom_ref, high_ref, low_ref, left_ref, sent_ref, first_ref, tiles
):
    nodes, width, _ = bottom_ref.shape
    wide = 2 * width
    half = width // 2
    targets = sent_ref.shape[0]
    heights = high_ref.shape[0]
    total = parts_ref[0]
    for part in range(1, parts_ref.shape[0]):
        total = total + parts_ref[part]
    folded = total[:width]
    diagonal = total[width : width + 1]
    turned = folded.T
    row = iota((width, width), 0)
    column = iota((width, width), 1)
    masked = []
    for node in range(nodes):
        pair, side = node // 2, node % 2
        here = folded[:, pair * width : (pair + 1) * width]
        there = turned[pair * width : (pair + 1) * width]
        if side == 0:
            gram = jnp.where(row <= column, here, there)
        else:
            centre = jnp.broadcast_to(diagonal[:, pair * width : (pair + 1) * width], (width, width))
            gram = jnp.where(row > column, here, jnp.where(row < column, there, centre))
        masked.append(keep_rank(gram, rank_ref[node]))
    bottom = halves(lift(masked, [bottom_ref[node] for node in range(nodes)]))
    lane = iota((1, wide), 1)
    lower = jnp.where(lane < width, rank_ref[1], rank_ref[3])
    diagonal = jnp.where((lane & (width - 1)) < lower, diagonal, 0.0)
    tiles[0] = jnp.concatenate([diagonal, jnp.zeros((7, wide), F32)], axis=0)
    parts = parts_ref.shape[0]
    share = half // (2 * parts)
    for height in range(heights):
        path = (high_ref[height], low_ref[height])
        term = product(tn, path, halves(product(nn, bottom, path)))
        if height == 0:
            first_ref[...] = pack(term)
            continue
        square, centre = fold(term)
        packed = pack(square)
        mine = packed[:share]
        for part in range(1, parts):
            mine = jnp.where(level_ref[0] == part, packed[part * share : (part + 1) * share], mine)
        centre = jnp.concatenate([centre, jnp.zeros((1, wide - half), F32)], axis=1)
        tiles[height] = jnp.concatenate([diagonal, mine, centre, jnp.zeros((6 - share, wide), F32)], axis=0)

    row = iota((width, wide), 0)
    lane = iota((width, wide), 1)
    column = lane & (width - 1)
    low = lane < width
    upper = jnp.where(low, rank_ref[0], rank_ref[2])
    lower = jnp.where(low, rank_ref[1], rank_ref[3])
    kept = jnp.maximum(row, column) < jnp.where(row <= column, upper, lower)
    share_rows = jnp.where(kept, folded, 0.0).astype(BF16)
    place = place_ref[0]
    for target in range(targets):
        device = 2 * target + 1
        height = reach(device, 2 * targets)
        inside = jnp.right_shift(place, height) == device >> height
        sent_ref[target, :width] = share_rows
        sent_ref[target, width:] = tiles[jnp.where(inside, height - 1, 0)].astype(BF16)

    row = iota((width, width), 0)
    even_first = jnp.where(row < half, 2 * row, 2 * row - width + 1)
    order = (iota((width, width), 1) == even_first).astype(F32).astype(BF16)
    for node in range(nodes):
        left_ref[node] = nt(nn(order, masked[node].astype(BF16)).astype(BF16), order).astype(BF16)


def sum_kernel(received_ref, out_ref):
    sources, rows, _ = received_ref.shape
    total = received_ref[0, rows - 8 :].astype(F32)
    for source in range(1, sources):
        total = total + received_ref[source, rows - 8 :].astype(F32)
    for copy in range(out_ref.shape[0]):
        out_ref[copy] = total


def top_kernel(core_ref, received_ref, first_ref, other_ref, out_ref, scratch):
    parts = received_ref.shape[0] // 2
    wide = received_ref.shape[2]
    width = wide // 2
    half = width // 2
    share = half // (2 * parts)
    sums = [received_ref[part] + received_ref[parts + part] for part in range(parts)]
    packed = jnp.concatenate([value[1 : 1 + share] for value in sums], axis=0)
    high = unfold(unpack(packed), sums[0][1 + share : 2 + share, :half])
    scratch[...] = jnp.where(core_ref[0] == 1, high, unpack(first_ref[...] + other_ref[...]))
    natural = jnp.concatenate([scratch[pl.ds(side, half, stride=2), :] for side in range(2)], axis=1)
    for tile in range(half):
        out_ref[:, tile * wide : (tile + 1) * wide] = natural[tile : tile + 1]


def left_kernel(row_ref, blocks_ref, left_ref, out_ref, spread):
    step = pl.program_id(0)
    count, flat = blocks_ref.shape
    width = left_ref.shape[1]
    wide = 2 * width
    tiles = flat // wide
    low = iota((width, wide), 1) < width
    for tile in range(tiles):
        spread[tile * count : (tile + 1) * count, :] = blocks_ref[:, tile * wide : (tile + 1) * wide].astype(F32)
    for index in range(count):
        block = step * count + index
        here = spread[pl.ds(index, tiles, stride=count), :]
        turned = pltpu.roll(here, width, 1)
        rows = jnp.where(
            low, jnp.concatenate([here, turned], axis=0), jnp.concatenate([turned, here], axis=0)
        ).astype(BF16)
        out_ref[index] = nn(left_ref[row_ref[block]], rows).astype(BF16)


def project_kernel(
    owner_ref, column_ref, core_ref, rows_ref, own_ref, other_ref, out_ref, result, triangles
):
    step = pl.program_id(0)
    count, width, wide = rows_ref.shape
    tiles = width // 2

    low = iota((tiles, wide), 1) < width

    @pl.when(step == 0)
    def _():
        row = iota((width, wide), 0)
        lane = iota((width, wide), 1)
        column = lane & (width - 1)
        for cluster in range(4):
            mine = (lane < width) == (cluster < 2)
            parts = (row <= column, row < 0) if cluster % 2 == 0 else (row > column, row == column)
            for index, part in enumerate(parts):
                triangles[cluster, index] = (mine & part).astype(F32).astype(BF16)
        for place in range(2):
            mine = (lane < width) == (place == 0)
            triangles[4 + place, 0] = (mine & (row > column)).astype(F32).astype(BF16)
            triangles[4 + place, 1] = (mine & (row < column)).astype(F32).astype(BF16)

    for index in range(0, count, 2):
        folded = []
        for place in range(2):
            owner = owner_ref[step * count + index + place]
            source = jnp.right_shift(owner, 1)
            at_home = (owner & 1) == core_ref[0]
            folded.append(
                (
                    jnp.where(at_home, own_ref[source, :width], other_ref[source, :width]),
                    jnp.where(at_home, own_ref[source, width:], other_ref[source, width:])[:1],
                )
            )
        turned = jnp.concatenate([folded[0][0], folded[1][0]], axis=0).T
        for place in range(2):
            cluster = column_ref[step * count + index + place]
            here, centre = folded[place]
            mirrored = jnp.where(cluster < 2, turned[:width], turned[width:])
            right = (
                here * triangles[cluster, 0]
                + centre * triangles[cluster, 1]
                + mirrored * triangles[4 + place, cluster & 1]
            )
            full = nn(rows_ref[index + place][:, :width], right)
            top, bottom = full[:tiles], full[tiles:]
            out = jnp.where(low, top, bottom) + pltpu.roll(jnp.where(low, bottom, top), width, 1)
            result[pl.ds(index + place, tiles, stride=count), :] = out
    for tile in range(tiles):
        out_ref[:, tile * wide : (tile + 1) * wide] = result[tile * count : (tile + 1) * count, :]


def shape(dims, dtype):
    return jax.ShapeDtypeStruct(dims, dtype)


def on_device(
    basis,
    bottom_transfer,
    bottom_rank,
    upper_transfer,
    upper_rank,
    couplings,
    row_cluster,
    column_owner,
    column_cluster,
):
    nodes, width, _ = basis.shape
    wide = 2 * width
    half = width // 2
    branches = lax.axis_size("branch")
    parts = lax.axis_size("level")
    levels = branches.bit_length() - 1
    me_branch = lax.axis_index("branch")
    me_level = lax.axis_index("level")
    core = me_branch & 1
    blk = couplings.shape[0]
    same_core = [list(range(c, branches, 2)) for c in range(2)]
    same_chip = [list(range(2 * parts * chip, 2 * parts * (chip + 1))) for chip in range(branches // 2)]
    partners = [(i, i ^ 1) for i in range(branches)]

    partial_sums = pl.pallas_call(
        gram_kernel,
        out_shape=shape((parts, width + 8, wide), F32),
        in_specs=[VMEM],
        out_specs=VMEM,
        compiler_params=SMALL,
        name="gram",
    )(basis)
    partial_sums, upper_transfer, upper_rank, bottom_transfer = lax.optimization_barrier(
        (partial_sums, upper_transfer, upper_rank, bottom_transfer)
    )
    gathered = lax.all_to_all(partial_sums, "level", 0, 0)
    heights = jnp.arange(levels, dtype=jnp.int32)
    slots = 2 * branches - jnp.right_shift(2 * branches, heights) + jnp.right_shift(me_branch, heights)
    path = jnp.take(upper_transfer, slots, axis=0).reshape(levels, width, width)
    path_high, path_low = pl.pallas_call(
        path_kernel,
        out_shape=[shape((levels, width, width), BF16)] * 2,
        in_specs=[SMEM, VMEM],
        out_specs=[VMEM, VMEM],
        compiler_params=SMALL,
        name="path",
    )(jnp.take(upper_rank, slots, axis=0), path)
    left, sent, first = pl.pallas_call(
        near_kernel,
        out_shape=[
            shape((nodes, width, width), BF16),
            shape((branches // 2, width + 8, wide), BF16),
            shape((half, wide), F32),
        ],
        in_specs=[SMEM, SMEM, SMEM, VMEM, VMEM, VMEM, VMEM],
        out_specs=[VMEM, VMEM, VMEM],
        scratch_shapes=[pltpu.VMEM((levels, 8, wide), F32)],
        compiler_params=SMALL,
        name="near",
    )(
        bottom_rank,
        me_branch[None],
        me_level[None],
        gathered,
        bottom_transfer.reshape(nodes, width, width),
        path_high,
        path_low,
    )
    sent, first = lax.optimization_barrier((sent, first))
    own = lax.all_to_all(sent, "branch", 0, 0, axis_index_groups=same_core)
    first_other = lax.ppermute(first, "branch", partners)
    square = pl.BlockSpec((ROWS, width, wide), lambda i, *_: (i, 0, 0))
    rows = pl.pallas_call(
        left_kernel,
        out_shape=shape((blk, width, wide), BF16),
        grid_spec=pltpu.PrefetchScalarGridSpec(
            num_scalar_prefetch=1,
            grid=(blk // ROWS,),
            in_specs=[
                pl.BlockSpec((ROWS, width * width), lambda i, *_: (i, 0)),
                pl.BlockSpec((nodes, width, width), lambda i, *_: (0, 0, 0)),
            ],
            out_specs=square,
            scratch_shapes=[pltpu.VMEM((ROWS * half, wide), F32)],
        ),
        compiler_params=SMALL,
        cost_estimate=pl.CostEstimate(
            flops=4 * blk * width**3, bytes_accessed=4 * blk * width * width, transcendentals=0
        ),
        name="left",
    )(row_cluster, couplings, left)
    own, first_other, rows = lax.optimization_barrier((own, first_other, rows))
    summed = pl.pallas_call(
        sum_kernel,
        out_shape=shape((2 * parts, 8, wide), F32),
        in_specs=[VMEM],
        out_specs=VMEM,
        compiler_params=SMALL,
        name="sum",
    )(own)
    other = lax.ppermute(own, "branch", partners)
    quarters = lax.all_to_all(summed, ("branch", "level"), 0, 0, axis_index_groups=same_chip)

    whole = pl.BlockSpec(own.shape, lambda i, *_: (0, 0, 0))
    projected = pl.pallas_call(
        project_kernel,
        out_shape=shape((blk, width * width), F32),
        grid_spec=pltpu.PrefetchScalarGridSpec(
            num_scalar_prefetch=3,
            grid=(blk // ROWS,),
            in_specs=[square, whole, whole],
            out_specs=pl.BlockSpec((ROWS, width * width), lambda i, *_: (i, 0)),
            scratch_shapes=[
                pltpu.VMEM((ROWS * half, wide), F32),
                pltpu.VMEM((6, 2, width, wide), BF16),
            ],
        ),
        compiler_params=pltpu.CompilerParams(vmem_limit_bytes=56 * 1024 * 1024),
        cost_estimate=pl.CostEstimate(
            flops=8 * blk * width**3, bytes_accessed=6 * blk * width * width, transcendentals=0
        ),
        name="project",
    )(column_owner[:, 0], column_cluster, core[None], rows, own, other)
    projected, quarters = lax.optimization_barrier((projected, quarters))
    upper_grams = pl.pallas_call(
        top_kernel,
        out_shape=shape((1, width * width), F32),
        in_specs=[SMEM, VMEM, VMEM, VMEM],
        out_specs=VMEM,
        scratch_shapes=[pltpu.VMEM((width, width), F32)],
        compiler_params=SMALL,
        name="top",
    )(core[None], quarters, first, first_other)
    return (upper_grams, projected)


def solution(mesh):
    placed = (
        P("branch", None, "level"),
        P("branch", None),
        P("branch"),
        P(),
        P(),
        P(("branch", "level"), None),
        P(("branch", "level")),
        P(("branch", "level"), None),
        P(("branch", "level")),
    )
    return jax.shard_map(
        on_device,
        mesh=mesh,
        in_specs=placed,
        out_specs=(P("branch", None), P(("branch", "level"), None)),
        check_vma=False,
    )
```

```python
import jax
import jax.numpy as jnp
from jax import lax
from jax.experimental import pallas as pl
from jax.experimental.pallas import tpu as pltpu
from jax.sharding import PartitionSpec as P

VMEM = pl.BlockSpec(memory_space=pltpu.VMEM)
SMEM = pl.BlockSpec(memory_space=pltpu.SMEM)
SMALL = pltpu.CompilerParams(vmem_limit_bytes=8 * 1024 * 1024)
ROWS = 16
F32 = jnp.float32
BF16 = jnp.bfloat16


def iota(shape, axis):
    return lax.broadcasted_iota(jnp.int32, shape, axis)


def nn(a, b):
    return jnp.dot(a, b, preferred_element_type=F32)


def nt(a, b):
    return lax.dot_general(a, b, (((1,), (1,)), ((), ())), preferred_element_type=F32)


def tn(a, b):
    return lax.dot_general(a, b, (((0,), (0,)), ((), ())), preferred_element_type=F32)


def halves(x):
    high = x.astype(BF16)
    return high, (x - high.astype(F32)).astype(BF16)


def keep_rank(gram, rank):
    return jnp.where((iota(gram.shape, 0) < rank) & (iota(gram.shape, 1) < rank), gram, 0.0)


def lift(masked, transfer):
    inner = []
    for gram, mat in zip(masked, transfer):
        high, low = halves(gram)
        inner.append(nn(high, mat) + nn(low, mat))
    high, low = halves(jnp.concatenate(inner, axis=0))
    mats = jnp.concatenate(transfer, axis=0)
    return tn(mats, high) + tn(mats, low)


def product(multiply, a, b):
    return multiply(a[0], b[0]) + (multiply(a[0], b[1]) + multiply(a[1], b[0]))


def fold(square):
    half = square.shape[0] // 2
    row, column = iota((half, half), 0), iota((half, half), 1)
    first = square[:half, :half]
    mixed = jnp.where(row < column, first, square[half:, half:])
    centre = jnp.sum(jnp.where(row == column, first, 0.0), axis=0, keepdims=True)
    return jnp.concatenate([mixed, square[:half, half:]], axis=1), centre


def unfold(folded, centre):
    half = folded.shape[0]
    row, column = iota((half, half), 0), iota((half, half), 1)
    turned = folded.T
    mixed, mixed_turned = folded[:, :half], turned[:half]
    first = jnp.where(row < column, mixed, jnp.where(row > column, mixed_turned, centre))
    last = jnp.where(row >= column, mixed, mixed_turned)
    top = jnp.concatenate([first, folded[:, half:]], axis=1)
    return jnp.concatenate([top, jnp.concatenate([turned[half:], last], axis=1)], axis=0)


def pack(square):
    half = square.shape[0] // 2
    return jnp.concatenate([square[:half], square[half:]], axis=1)


def unpack(packed):
    half = packed.shape[1] // 2
    return jnp.concatenate([packed[:, :half], packed[:, half:]], axis=0)


def reach(index, count):
    return (index ^ ((index + 1) % count)).bit_length()


def gram_kernel(basis_ref, out_ref):
    copies = out_ref.shape[0]
    width = basis_ref.shape[1]
    wide = 2 * width
    row = iota((width, wide), 0)
    lane = iota((width, wide), 1)
    column = lane & (width - 1)
    sides = []
    for side in range(2):
        both = jnp.concatenate([basis_ref[side], basis_ref[side + 2]], axis=0)
        crossed = nt(both, both)
        sides.append(jnp.where(lane < width, crossed[:width], crossed[width:]))
    folded = jnp.where(row <= column, sides[0], sides[1])
    diagonal = jnp.sum(jnp.where(row == column, sides[1], 0.0), axis=0, keepdims=True)
    for copy in range(copies):
        out_ref[copy, :width] = folded
        out_ref[copy, width:] = jnp.broadcast_to(diagonal, (8, wide))


def path_kernel(rank_ref, path_ref, high_ref, low_ref):
    heights = path_ref.shape[0]
    row = iota(path_ref.shape[1:], 0)
    for height in range(heights):
        step = jnp.where(row < rank_ref[height], path_ref[height].astype(F32), 0.0)
        if height == 0:
            whole = step
        else:
            step = step.astype(BF16)
            whole = nn(high, step) + nn(low, step)
        high, low = halves(whole)
        high_ref[height] = high
        low_ref[height] = low


def near_kernel(
    rank_ref, place_ref, level_ref, parts_ref, bottom_ref, high_ref, low_ref, left_ref, sent_ref, first_ref, tiles
):
    nodes, width, _ = bottom_ref.shape
    wide = 2 * width
    half = width // 2
    targets = sent_ref.shape[0]
    heights = high_ref.shape[0]
    total = parts_ref[0]
    for part in range(1, parts_ref.shape[0]):
        total = total + parts_ref[part]
    folded = total[:width]
    diagonal = total[width : width + 1]
    turned = folded.T
    row = iota((width, width), 0)
    column = iota((width, width), 1)
    masked = []
    for node in range(nodes):
        pair, side = node // 2, node % 2
        here = folded[:, pair * width : (pair + 1) * width]
        there = turned[pair * width : (pair + 1) * width]
        if side == 0:
            gram = jnp.where(row <= column, here, there)
        else:
            centre = jnp.broadcast_to(diagonal[:, pair * width : (pair + 1) * width], (width, width))
            gram = jnp.where(row > column, here, jnp.where(row < column, there, centre))
        masked.append(keep_rank(gram, rank_ref[node]))
    bottom = halves(lift(masked, [bottom_ref[node] for node in range(nodes)]))
    lane = iota((1, wide), 1)
    lower = jnp.where(lane < width, rank_ref[1], rank_ref[3])
    diagonal = jnp.where((lane & (width - 1)) < lower, diagonal, 0.0)
    tiles[0] = jnp.concatenate([diagonal, jnp.zeros((7, wide), F32)], axis=0)
    parts = parts_ref.shape[0]
    share = half // (2 * parts)
    for height in range(heights):
        path = (high_ref[height], low_ref[height])
        term = product(tn, path, halves(product(nn, bottom, path)))
        if height == 0:
            first_ref[...] = pack(term)
            continue
        square, centre = fold(term)
        packed = pack(square)
        mine = packed[:share]
        for part in range(1, parts):
            mine = jnp.where(level_ref[0] == part, packed[part * share : (part + 1) * share], mine)
        centre = jnp.concatenate([centre, jnp.zeros((1, wide - half), F32)], axis=1)
        tiles[height] = jnp.concatenate([diagonal, mine, centre, jnp.zeros((6 - share, wide), F32)], axis=0)

    row = iota((width, wide), 0)
    lane = iota((width, wide), 1)
    column = lane & (width - 1)
    low = lane < width
    upper = jnp.where(low, rank_ref[0], rank_ref[2])
    lower = jnp.where(low, rank_ref[1], rank_ref[3])
    kept = jnp.maximum(row, column) < jnp.where(row <= column, upper, lower)
    share_rows = jnp.where(kept, folded, 0.0).astype(BF16)
    place = place_ref[0]
    for target in range(targets):
        device = 2 * target + 1
        height = reach(device, 2 * targets)
        inside = jnp.right_shift(place, height) == device >> height
        sent_ref[target, :width] = share_rows
        sent_ref[target, width:] = tiles[jnp.where(inside, height - 1, 0)].astype(BF16)

    row = iota((width, width), 0)
    even_first = jnp.where(row < half, 2 * row, 2 * row - width + 1)
    order = (iota((width, width), 1) == even_first).astype(F32).astype(BF16)
    for node in range(nodes):
        left_ref[node] = nt(nn(order, masked[node].astype(BF16)).astype(BF16), order).astype(BF16)


def sum_kernel(received_ref, out_ref):
    sources, rows, _ = received_ref.shape
    total = received_ref[0, rows - 8 :].astype(F32)
    for source in range(1, sources):
        total = total + received_ref[source, rows - 8 :].astype(F32)
    for copy in range(out_ref.shape[0]):
        out_ref[copy] = total


def top_kernel(core_ref, received_ref, first_ref, other_ref, done_ref, out_ref, scratch):
    parts = received_ref.shape[0] // 2
    wide = received_ref.shape[2]
    width = wide // 2
    half = width // 2
    share = half // (2 * parts)
    sums = [received_ref[part] + received_ref[parts + part] for part in range(parts)]
    packed = jnp.concatenate([value[1 : 1 + share] for value in sums], axis=0)
    high = unfold(unpack(packed), sums[0][1 + share : 2 + share, :half])
    scratch[...] = jnp.where(core_ref[0] == 1, high, unpack(first_ref[...] + other_ref[...]))
    natural = jnp.concatenate([scratch[pl.ds(side, half, stride=2), :] for side in range(2)], axis=1)
    for tile in range(half):
        out_ref[:, tile * wide : (tile + 1) * wide] = natural[tile : tile + 1]


def left_kernel(row_ref, blocks_ref, left_ref, out_ref, done_ref, spread):
    step = pl.program_id(0)
    count, flat = blocks_ref.shape
    width = left_ref.shape[1]
    wide = 2 * width
    tiles = flat // wide
    low = iota((width, wide), 1) < width
    for tile in range(tiles):
        spread[tile * count : (tile + 1) * count, :] = blocks_ref[:, tile * wide : (tile + 1) * wide].astype(F32)
    for index in range(0, count, 2):
        products = []
        for place in range(2):
            here = spread[pl.ds(index + place, tiles, stride=count), :]
            turned = pltpu.roll(here, width, 1)
            rows = jnp.where(
                low, jnp.concatenate([here, turned], axis=0), jnp.concatenate([turned, here], axis=0)
            ).astype(BF16)
            products.append(nn(left_ref[row_ref[step * count + index + place]], rows))
        out_ref[index // 2] = jnp.where(low, products[0], products[1]).astype(BF16)
    done_ref[...] = jnp.zeros_like(done_ref)


def project_kernel(
    owner_ref, column_ref, core_ref, rows_ref, own_ref, other_ref, out_ref, result, triangles
):
    step = pl.program_id(0)
    pairs, width, wide = rows_ref.shape
    count = 2 * pairs
    tiles = width // 2
    low = iota((tiles, wide), 1) < width
    none = jnp.zeros((width, wide), BF16)

    @pl.when(step == 0)
    def _():
        row = iota((width, wide), 0)
        lane = iota((width, wide), 1)
        column = lane & (width - 1)
        for cluster in range(4):
            mine = (lane < width) == (cluster < 2)
            parts = (row <= column, row < 0) if cluster % 2 == 0 else (row > column, row == column)
            for index, part in enumerate(parts):
                triangles[cluster, index] = (mine & part).astype(F32).astype(BF16)
        for place in range(2):
            mine = (lane < width) == (place == 0)
            triangles[4 + place, 0] = (mine & (row > column)).astype(F32).astype(BF16)
            triangles[4 + place, 1] = (mine & (row < column)).astype(F32).astype(BF16)

    for index in range(0, count, 2):
        folded = []
        for place in range(2):
            owner = owner_ref[step * count + index + place]
            source = jnp.right_shift(owner, 1)
            at_home = (owner & 1) == core_ref[0]
            folded.append(
                (
                    jnp.where(at_home, own_ref[source, :width], other_ref[source, :width]),
                    jnp.where(at_home, own_ref[source, width:], other_ref[source, width:])[:1],
                )
            )
        turned = jnp.concatenate([folded[0][0], folded[1][0]], axis=0).T
        for place in range(2):
            cluster = column_ref[step * count + index + place]
            here, centre = folded[place]
            mirrored = jnp.where(cluster < 2, turned[:width], turned[width:])
            right = (
                here * triangles[cluster, 0]
                + centre * triangles[cluster, 1]
                + mirrored * triangles[4 + place, cluster & 1]
            )
            weights = [right, none] if place == 0 else [none, right]
            full = nn(rows_ref[index // 2], jnp.concatenate(weights, axis=0))
            top, bottom = full[:tiles], full[tiles:]
            out = jnp.where(low, top, bottom) + pltpu.roll(jnp.where(low, bottom, top), width, 1)
            result[pl.ds(index + place, tiles, stride=count), :] = out
    for tile in range(tiles):
        out_ref[:, tile * wide : (tile + 1) * wide] = result[tile * count : (tile + 1) * count, :]


def shape(dims, dtype):
    return jax.ShapeDtypeStruct(dims, dtype)


def on_device(
    basis,
    bottom_transfer,
    bottom_rank,
    upper_transfer,
    upper_rank,
    couplings,
    row_cluster,
    column_owner,
    column_cluster,
):
    nodes, width, _ = basis.shape
    wide = 2 * width
    half = width // 2
    branches = lax.axis_size("branch")
    parts = lax.axis_size("level")
    levels = branches.bit_length() - 1
    me_branch = lax.axis_index("branch")
    me_level = lax.axis_index("level")
    core = me_branch & 1
    blk = couplings.shape[0]
    same_core = [list(range(c, branches, 2)) for c in range(2)]
    same_chip = [list(range(2 * parts * chip, 2 * parts * (chip + 1))) for chip in range(branches // 2)]
    partners = [(i, i ^ 1) for i in range(branches)]

    partial_sums = pl.pallas_call(
        gram_kernel,
        out_shape=shape((parts, width + 8, wide), F32),
        in_specs=[VMEM],
        out_specs=VMEM,
        compiler_params=SMALL,
        name="gram",
    )(basis)
    partial_sums, upper_transfer, upper_rank, bottom_transfer = lax.optimization_barrier(
        (partial_sums, upper_transfer, upper_rank, bottom_transfer)
    )
    gathered = lax.all_to_all(partial_sums, "level", 0, 0)
    heights = jnp.arange(levels, dtype=jnp.int32)
    slots = 2 * branches - jnp.right_shift(2 * branches, heights) + jnp.right_shift(me_branch, heights)
    path = jnp.take(upper_transfer, slots, axis=0).reshape(levels, width, width)
    path_high, path_low = pl.pallas_call(
        path_kernel,
        out_shape=[shape((levels, width, width), BF16)] * 2,
        in_specs=[SMEM, VMEM],
        out_specs=[VMEM, VMEM],
        compiler_params=SMALL,
        name="path",
    )(jnp.take(upper_rank, slots, axis=0), path)
    left, sent, first = pl.pallas_call(
        near_kernel,
        out_shape=[
            shape((nodes, width, width), BF16),
            shape((branches // 2, width + 8, wide), BF16),
            shape((half, wide), F32),
        ],
        in_specs=[SMEM, SMEM, SMEM, VMEM, VMEM, VMEM, VMEM],
        out_specs=[VMEM, VMEM, VMEM],
        scratch_shapes=[pltpu.VMEM((levels, 8, wide), F32)],
        compiler_params=SMALL,
        name="near",
    )(
        bottom_rank,
        me_branch[None],
        me_level[None],
        gathered,
        bottom_transfer.reshape(nodes, width, width),
        path_high,
        path_low,
    )
    own = lax.all_to_all(sent, "branch", 0, 0, axis_index_groups=same_core)
    first_other = lax.ppermute(first, "branch", partners)
    square = pl.BlockSpec((ROWS // 2, width, wide), lambda i, *_: (i, 0, 0))
    rows, done = pl.pallas_call(
        left_kernel,
        out_shape=[shape((blk // 2, width, wide), BF16), shape((8, wide), F32)],
        grid_spec=pltpu.PrefetchScalarGridSpec(
            num_scalar_prefetch=1,
            grid=(blk // ROWS,),
            in_specs=[
                pl.BlockSpec((ROWS, width * width), lambda i, *_: (i, 0)),
                pl.BlockSpec((nodes, width, width), lambda i, *_: (0, 0, 0)),
            ],
            out_specs=[square, pl.BlockSpec((8, wide), lambda i, *_: (0, 0))],
            scratch_shapes=[pltpu.VMEM((ROWS * half, wide), F32)],
        ),
        compiler_params=SMALL,
        cost_estimate=pl.CostEstimate(
            flops=4 * blk * width**3, bytes_accessed=4 * blk * width * width, transcendentals=0
        ),
        name="left",
    )(row_cluster, couplings, left)
    own, first_other, done = lax.optimization_barrier((own, first_other, done))
    summed = pl.pallas_call(
        sum_kernel,
        out_shape=shape((2 * parts, 8, wide), F32),
        in_specs=[VMEM],
        out_specs=VMEM,
        compiler_params=SMALL,
        name="sum",
    )(own)
    other = lax.ppermute(own, "branch", partners)
    quarters = lax.all_to_all(summed, ("branch", "level"), 0, 0, axis_index_groups=same_chip)

    whole = pl.BlockSpec(own.shape, lambda i, *_: (0, 0, 0))
    projected = pl.pallas_call(
        project_kernel,
        out_shape=shape((blk, width * width), F32),
        grid_spec=pltpu.PrefetchScalarGridSpec(
            num_scalar_prefetch=3,
            grid=(blk // ROWS,),
            in_specs=[square, whole, whole],
            out_specs=pl.BlockSpec((ROWS, width * width), lambda i, *_: (i, 0)),
            scratch_shapes=[
                pltpu.VMEM((ROWS * half, wide), F32),
                pltpu.VMEM((6, 2, width, wide), BF16),
            ],
        ),
        compiler_params=pltpu.CompilerParams(vmem_limit_bytes=12 * 1024 * 1024),
        cost_estimate=pl.CostEstimate(
            flops=8 * blk * width**3, bytes_accessed=6 * blk * width * width, transcendentals=0
        ),
        name="project",
    )(column_owner[:, 0], column_cluster, core[None], rows, own, other)
    projected, quarters = lax.optimization_barrier((projected, quarters))
    upper_grams = pl.pallas_call(
        top_kernel,
        out_shape=shape((1, width * width), F32),
        in_specs=[SMEM, VMEM, VMEM, VMEM, VMEM],
        out_specs=VMEM,
        scratch_shapes=[pltpu.VMEM((width, width), F32)],
        compiler_params=SMALL,
        name="top",
    )(core[None], quarters, first, first_other, done)
    return (upper_grams, projected)


def solution(mesh):
    placed = (
        P("branch", None, "level"),
        P("branch", None),
        P("branch"),
        P(),
        P(),
        P(("branch", "level"), None),
        P(("branch", "level")),
        P(("branch", "level"), None),
        P(("branch", "level")),
    )
    return jax.shard_map(
        on_device,
        mesh=mesh,
        in_specs=placed,
        out_specs=(P("branch", None), P(("branch", "level"), None)),
        check_vma=False,
    )
```

```python
import functools

import jax
import jax.numpy as jnp
from jax import lax
from jax.experimental import pallas as pl
from jax.experimental.pallas import tpu as pltpu
from jax.sharding import PartitionSpec as P

VMEM = pl.BlockSpec(memory_space=pltpu.VMEM)
SMEM = pl.BlockSpec(memory_space=pltpu.SMEM)
SMALL = pltpu.CompilerParams(vmem_limit_bytes=8 * 1024 * 1024)
ROWS = 16
F32 = jnp.float32
BF16 = jnp.bfloat16


def iota(shape, axis):
    return lax.broadcasted_iota(jnp.int32, shape, axis)


def nn(a, b):
    return jnp.dot(a, b, preferred_element_type=F32)


def nt(a, b):
    return lax.dot_general(a, b, (((1,), (1,)), ((), ())), preferred_element_type=F32)


def tn(a, b):
    return lax.dot_general(a, b, (((0,), (0,)), ((), ())), preferred_element_type=F32)


def halves(x):
    high = x.astype(BF16)
    return high, (x - high.astype(F32)).astype(BF16)


def keep_rank(gram, rank):
    return jnp.where((iota(gram.shape, 0) < rank) & (iota(gram.shape, 1) < rank), gram, 0.0)


def lift(masked, transfer):
    inner = []
    for gram, mat in zip(masked, transfer):
        high, low = halves(gram)
        inner.append(nn(high, mat) + nn(low, mat))
    high, low = halves(jnp.concatenate(inner, axis=0))
    mats = jnp.concatenate(transfer, axis=0)
    return tn(mats, high) + tn(mats, low)


def product(multiply, a, b):
    return multiply(a[0], b[0]) + (multiply(a[0], b[1]) + multiply(a[1], b[0]))


def fold(square):
    half = square.shape[0] // 2
    row, column = iota((half, half), 0), iota((half, half), 1)
    first = square[:half, :half]
    mixed = jnp.where(row < column, first, square[half:, half:])
    centre = jnp.sum(jnp.where(row == column, first, 0.0), axis=0, keepdims=True)
    return jnp.concatenate([mixed, square[:half, half:]], axis=1), centre


def unfold(folded, centre):
    half = folded.shape[0]
    row, column = iota((half, half), 0), iota((half, half), 1)
    turned = folded.T
    mixed, mixed_turned = folded[:, :half], turned[:half]
    first = jnp.where(row < column, mixed, jnp.where(row > column, mixed_turned, centre))
    last = jnp.where(row >= column, mixed, mixed_turned)
    top = jnp.concatenate([first, folded[:, half:]], axis=1)
    return jnp.concatenate([top, jnp.concatenate([turned[half:], last], axis=1)], axis=0)


def pack(square):
    half = square.shape[0] // 2
    return jnp.concatenate([square[:half], square[half:]], axis=1)


def unpack(packed):
    half = packed.shape[1] // 2
    return jnp.concatenate([packed[:, :half], packed[:, half:]], axis=0)


def reach(index, count):
    return (index ^ ((index + 1) % count)).bit_length()


def gram_kernel(basis_ref, out_ref):
    copies = out_ref.shape[0]
    width = basis_ref.shape[1]
    wide = 2 * width
    row = iota((width, wide), 0)
    lane = iota((width, wide), 1)
    column = lane & (width - 1)
    sides = []
    for side in range(2):
        both = jnp.concatenate([basis_ref[side], basis_ref[side + 2]], axis=0)
        crossed = nt(both, both)
        sides.append(jnp.where(lane < width, crossed[:width], crossed[width:]))
    folded = jnp.where(row <= column, sides[0], sides[1])
    diagonal = jnp.sum(jnp.where(row == column, sides[1], 0.0), axis=0, keepdims=True)
    for copy in range(copies):
        out_ref[copy, :width] = folded
        out_ref[copy, width:] = jnp.broadcast_to(diagonal, (8, wide))


def path_kernel(rank_ref, path_ref, high_ref, low_ref):
    heights = path_ref.shape[0]
    row = iota(path_ref.shape[1:], 0)
    for height in range(heights):
        step = jnp.where(row < rank_ref[height], path_ref[height].astype(F32), 0.0)
        if height == 0:
            whole = step
        else:
            step = step.astype(BF16)
            whole = nn(high, step) + nn(low, step)
        high, low = halves(whole)
        high_ref[height] = high
        low_ref[height] = low


def near_kernel(
    parts, rank_ref, place_ref, level_ref, parts_ref, bottom_ref, high_ref, low_ref, left_ref, sent_ref, first_ref, tiles
):
    nodes, width, _ = bottom_ref.shape
    wide = 2 * width
    half = width // 2
    targets = sent_ref.shape[0]
    heights = high_ref.shape[0]
    total = parts_ref[0]
    for part in range(1, parts_ref.shape[0]):
        total = total + parts_ref[part]
    folded = total[:width]
    diagonal = total[width : width + 1]
    turned = folded.T
    row = iota((width, width), 0)
    column = iota((width, width), 1)
    masked = []
    for node in range(nodes):
        pair, side = node // 2, node % 2
        here = folded[:, pair * width : (pair + 1) * width]
        there = turned[pair * width : (pair + 1) * width]
        if side == 0:
            gram = jnp.where(row <= column, here, there)
        else:
            centre = jnp.broadcast_to(diagonal[:, pair * width : (pair + 1) * width], (width, width))
            gram = jnp.where(row > column, here, jnp.where(row < column, there, centre))
        masked.append(keep_rank(gram, rank_ref[node]))
    bottom = halves(lift(masked, [bottom_ref[node] for node in range(nodes)]))
    lane = iota((1, wide), 1)
    lower = jnp.where(lane < width, rank_ref[1], rank_ref[3])
    diagonal = jnp.where((lane & (width - 1)) < lower, diagonal, 0.0)
    tiles[0] = jnp.concatenate([diagonal, jnp.zeros((7, wide), F32)], axis=0)
    share = half // (2 * parts)
    for height in range(heights):
        path = (high_ref[height], low_ref[height])
        term = product(tn, path, halves(product(nn, bottom, path)))
        if height == 0:
            first_ref[...] = pack(term)
            continue
        square, centre = fold(term)
        packed = pack(square)
        mine = packed[:share]
        for part in range(1, parts):
            mine = jnp.where(level_ref[0] == part, packed[part * share : (part + 1) * share], mine)
        centre = jnp.concatenate([centre, jnp.zeros((1, wide - half), F32)], axis=1)
        tiles[height] = jnp.concatenate([diagonal, mine, centre, jnp.zeros((6 - share, wide), F32)], axis=0)

    row = iota((width, wide), 0)
    lane = iota((width, wide), 1)
    column = lane & (width - 1)
    low = lane < width
    upper = jnp.where(low, rank_ref[0], rank_ref[2])
    lower = jnp.where(low, rank_ref[1], rank_ref[3])
    kept = jnp.maximum(row, column) < jnp.where(row <= column, upper, lower)
    share_rows = jnp.where(kept, folded, 0.0).astype(BF16)
    place = place_ref[0]
    for target in range(targets):
        device = 2 * target + 1
        height = reach(device, 2 * targets)
        inside = jnp.right_shift(place, height) == device >> height
        sent_ref[target, :width] = share_rows
        sent_ref[target, width:] = tiles[jnp.where(inside, height - 1, 0)].astype(BF16)

    row = iota((width, width), 0)
    even_first = jnp.where(row < half, 2 * row, 2 * row - width + 1)
    order = (iota((width, width), 1) == even_first).astype(F32).astype(BF16)
    for node in range(nodes):
        left_ref[node] = nt(nn(order, masked[node].astype(BF16)).astype(BF16), order).astype(BF16)


def sum_kernel(received_ref, out_ref):
    sources, rows, _ = received_ref.shape
    total = received_ref[0, rows - 8 :].astype(F32)
    for source in range(1, sources):
        total = total + received_ref[source, rows - 8 :].astype(F32)
    for copy in range(out_ref.shape[0]):
        out_ref[copy] = total


def top_kernel(core_ref, received_ref, first_ref, other_ref, done_ref, out_ref, scratch):
    parts = received_ref.shape[0] // 2
    wide = received_ref.shape[2]
    width = wide // 2
    half = width // 2
    share = half // (2 * parts)
    sums = [received_ref[part] + received_ref[parts + part] for part in range(parts)]
    packed = jnp.concatenate([value[1 : 1 + share] for value in sums], axis=0)
    high = unfold(unpack(packed), sums[0][1 + share : 2 + share, :half])
    scratch[...] = jnp.where(core_ref[0] == 1, high, unpack(first_ref[...] + other_ref[...]))
    natural = jnp.concatenate([scratch[pl.ds(side, half, stride=2), :] for side in range(2)], axis=1)
    for tile in range(half):
        out_ref[:, tile * wide : (tile + 1) * wide] = natural[tile : tile + 1]


def left_kernel(row_ref, blocks_ref, left_ref, out_ref, done_ref, spread):
    step = pl.program_id(0)
    count, flat = blocks_ref.shape
    width = left_ref.shape[1]
    wide = 2 * width
    tiles = flat // wide
    low = iota((width, wide), 1) < width
    for tile in range(tiles):
        spread[tile * count : (tile + 1) * count, :] = blocks_ref[:, tile * wide : (tile + 1) * wide].astype(F32)
    for index in range(0, count, 2):
        products = []
        for place in range(2):
            here = spread[pl.ds(index + place, tiles, stride=count), :]
            turned = pltpu.roll(here, width, 1)
            rows = jnp.where(
                low, jnp.concatenate([here, turned], axis=0), jnp.concatenate([turned, here], axis=0)
            ).astype(BF16)
            products.append(nn(left_ref[row_ref[step * count + index + place]], rows))
        out_ref[index // 2] = jnp.where(low, products[0], products[1]).astype(BF16)
    done_ref[...] = jnp.zeros_like(done_ref)


def project_kernel(
    owner_ref, column_ref, core_ref, rows_ref, own_ref, other_ref, out_ref, result, triangles
):
    step = pl.program_id(0)
    pairs, width, wide = rows_ref.shape
    count = 2 * pairs
    tiles = width // 2
    low = iota((tiles, wide), 1) < width
    none = jnp.zeros((width, wide), BF16)

    @pl.when(step == 0)
    def _():
        row = iota((width, wide), 0)
        lane = iota((width, wide), 1)
        column = lane & (width - 1)
        for cluster in range(4):
            mine = (lane < width) == (cluster < 2)
            parts = (row <= column, row < 0) if cluster % 2 == 0 else (row > column, row == column)
            for index, part in enumerate(parts):
                triangles[cluster, index] = (mine & part).astype(F32).astype(BF16)
        for place in range(2):
            mine = (lane < width) == (place == 0)
            triangles[4 + place, 0] = (mine & (row > column)).astype(F32).astype(BF16)
            triangles[4 + place, 1] = (mine & (row < column)).astype(F32).astype(BF16)

    for index in range(0, count, 2):
        folded = []
        for place in range(2):
            owner = owner_ref[step * count + index + place]
            source = jnp.right_shift(owner, 1)
            at_home = (owner & 1) == core_ref[0]
            folded.append(
                (
                    jnp.where(at_home, own_ref[source, :width], other_ref[source, :width]),
                    jnp.where(at_home, own_ref[source, width:], other_ref[source, width:])[:1],
                )
            )
        turned = jnp.concatenate([folded[0][0], folded[1][0]], axis=0).T
        for place in range(2):
            cluster = column_ref[step * count + index + place]
            here, centre = folded[place]
            mirrored = jnp.where(cluster < 2, turned[:width], turned[width:])
            right = (
                here * triangles[cluster, 0]
                + centre * triangles[cluster, 1]
                + mirrored * triangles[4 + place, cluster & 1]
            )
            weights = [right, none] if place == 0 else [none, right]
            full = nn(rows_ref[index // 2], jnp.concatenate(weights, axis=0))
            top, bottom = full[:tiles], full[tiles:]
            out = jnp.where(low, top, bottom) + pltpu.roll(jnp.where(low, bottom, top), width, 1)
            result[pl.ds(index + place, tiles, stride=count), :] = out
    for tile in range(tiles):
        out_ref[:, tile * wide : (tile + 1) * wide] = result[tile * count : (tile + 1) * count, :]


def shape(dims, dtype):
    return jax.ShapeDtypeStruct(dims, dtype)


def on_device(
    basis,
    bottom_transfer,
    bottom_rank,
    upper_transfer,
    upper_rank,
    couplings,
    row_cluster,
    column_owner,
    column_cluster,
):
    nodes, width, _ = basis.shape
    wide = 2 * width
    half = width // 2
    branches = lax.axis_size("branch")
    parts = lax.axis_size("level")
    levels = branches.bit_length() - 1
    me_branch = lax.axis_index("branch")
    me_level = lax.axis_index("level")
    core = me_branch & 1
    blk = couplings.shape[0]
    same_core = [list(range(c, branches, 2)) for c in range(2)]
    same_chip = [list(range(2 * parts * chip, 2 * parts * (chip + 1))) for chip in range(branches // 2)]
    partners = [(i, i ^ 1) for i in range(branches)]

    partial_sums = pl.pallas_call(
        gram_kernel,
        out_shape=shape((1, width + 8, wide), F32),
        in_specs=[VMEM],
        out_specs=VMEM,
        compiler_params=SMALL,
        name="gram",
    )(basis)
    partial_sums, upper_transfer, upper_rank, bottom_transfer = lax.optimization_barrier(
        (partial_sums, upper_transfer, upper_rank, bottom_transfer)
    )
    same_branch = [list(range(parts * branch, parts * (branch + 1))) for branch in range(branches)]
    gathered = lax.psum(partial_sums, ("branch", "level"), axis_index_groups=same_branch)
    heights = jnp.arange(levels, dtype=jnp.int32)
    slots = 2 * branches - jnp.right_shift(2 * branches, heights) + jnp.right_shift(me_branch, heights)
    path = jnp.take(upper_transfer, slots, axis=0).reshape(levels, width, width)
    path_high, path_low = pl.pallas_call(
        path_kernel,
        out_shape=[shape((levels, width, width), BF16)] * 2,
        in_specs=[SMEM, VMEM],
        out_specs=[VMEM, VMEM],
        compiler_params=SMALL,
        name="path",
    )(jnp.take(upper_rank, slots, axis=0), path)
    left, sent, first = pl.pallas_call(
        functools.partial(near_kernel, parts),
        out_shape=[
            shape((nodes, width, width), BF16),
            shape((branches // 2, width + 8, wide), BF16),
            shape((half, wide), F32),
        ],
        in_specs=[SMEM, SMEM, SMEM, VMEM, VMEM, VMEM, VMEM],
        out_specs=[VMEM, VMEM, VMEM],
        scratch_shapes=[pltpu.VMEM((levels, 8, wide), F32)],
        compiler_params=SMALL,
        name="near",
    )(
        bottom_rank,
        me_branch[None],
        me_level[None],
        gathered,
        bottom_transfer.reshape(nodes, width, width),
        path_high,
        path_low,
    )
    own = lax.all_to_all(sent, "branch", 0, 0, axis_index_groups=same_core)
    first_other = lax.ppermute(first, "branch", partners)
    square = pl.BlockSpec((ROWS // 2, width, wide), lambda i, *_: (i, 0, 0))
    rows, done = pl.pallas_call(
        left_kernel,
        out_shape=[shape((blk // 2, width, wide), BF16), shape((8, wide), F32)],
        grid_spec=pltpu.PrefetchScalarGridSpec(
            num_scalar_prefetch=1,
            grid=(blk // ROWS,),
            in_specs=[
                pl.BlockSpec((ROWS, width * width), lambda i, *_: (i, 0)),
                pl.BlockSpec((nodes, width, width), lambda i, *_: (0, 0, 0)),
            ],
            out_specs=[square, pl.BlockSpec((8, wide), lambda i, *_: (0, 0))],
            scratch_shapes=[pltpu.VMEM((ROWS * half, wide), F32)],
        ),
        compiler_params=SMALL,
        cost_estimate=pl.CostEstimate(
            flops=4 * blk * width**3, bytes_accessed=4 * blk * width * width, transcendentals=0
        ),
        name="left",
    )(row_cluster, couplings, left)
    own, first_other, done = lax.optimization_barrier((own, first_other, done))
    summed = pl.pallas_call(
        sum_kernel,
        out_shape=shape((2 * parts, 8, wide), F32),
        in_specs=[VMEM],
        out_specs=VMEM,
        compiler_params=SMALL,
        name="sum",
    )(own)
    other = lax.ppermute(own, "branch", partners)
    quarters = lax.all_to_all(summed, ("branch", "level"), 0, 0, axis_index_groups=same_chip)

    whole = pl.BlockSpec(own.shape, lambda i, *_: (0, 0, 0))
    projected = pl.pallas_call(
        project_kernel,
        out_shape=shape((blk, width * width), F32),
        grid_spec=pltpu.PrefetchScalarGridSpec(
            num_scalar_prefetch=3,
            grid=(blk // ROWS,),
            in_specs=[square, whole, whole],
            out_specs=pl.BlockSpec((ROWS, width * width), lambda i, *_: (i, 0)),
            scratch_shapes=[
                pltpu.VMEM((ROWS * half, wide), F32),
                pltpu.VMEM((6, 2, width, wide), BF16),
            ],
        ),
        compiler_params=pltpu.CompilerParams(vmem_limit_bytes=12 * 1024 * 1024),
        cost_estimate=pl.CostEstimate(
            flops=800 * blk * width**3, bytes_accessed=6 * blk * width * width, transcendentals=0
        ),
        name="project",
    )(column_owner[:, 0], column_cluster, core[None], rows, own, other)
    projected, quarters = lax.optimization_barrier((projected, quarters))
    upper_grams = pl.pallas_call(
        top_kernel,
        out_shape=shape((1, width * width), F32),
        in_specs=[SMEM, VMEM, VMEM, VMEM, VMEM],
        out_specs=VMEM,
        scratch_shapes=[pltpu.VMEM((width, width), F32)],
        compiler_params=SMALL,
        name="top",
    )(core[None], quarters, first, first_other, done)
    return (upper_grams, projected)


def solution(mesh):
    placed = (
        P("branch", None, "level"),
        P("branch", None),
        P("branch"),
        P(),
        P(),
        P(("branch", "level"), None),
        P(("branch", "level")),
        P(("branch", "level"), None),
        P(("branch", "level")),
    )
    return jax.shard_map(
        on_device,
        mesh=mesh,
        in_specs=placed,
        out_specs=(P("branch", None), P(("branch", "level"), None)),
        check_vma=False,
    )
```

```python
import jax
import jax.numpy as jnp
from jax import lax
from jax.experimental import pallas as pl
from jax.experimental.pallas import tpu as pltpu
from jax.sharding import PartitionSpec as P

VMEM = pl.BlockSpec(memory_space=pltpu.VMEM)
SMEM = pl.BlockSpec(memory_space=pltpu.SMEM)
SMALL = pltpu.CompilerParams(vmem_limit_bytes=8 * 1024 * 1024)
ROWS = 16
BLOCKS = 32
F32 = jnp.float32
BF16 = jnp.bfloat16


def iota(shape, axis):
    return lax.broadcasted_iota(jnp.int32, shape, axis)


def nn(a, b):
    return jnp.dot(a, b, preferred_element_type=F32)


def nt(a, b):
    return lax.dot_general(a, b, (((1,), (1,)), ((), ())), preferred_element_type=F32)


def tn(a, b):
    return lax.dot_general(a, b, (((0,), (0,)), ((), ())), preferred_element_type=F32)


def halves(x):
    high = x.astype(BF16)
    return high, (x - high.astype(F32)).astype(BF16)


def keep_rank(gram, rank):
    return jnp.where((iota(gram.shape, 0) < rank) & (iota(gram.shape, 1) < rank), gram, 0.0)


def lift(masked, transfer):
    inner = []
    for gram, mat in zip(masked, transfer):
        high, low = halves(gram)
        inner.append(nn(high, mat) + nn(low, mat))
    high, low = halves(jnp.concatenate(inner, axis=0))
    mats = jnp.concatenate(transfer, axis=0)
    return tn(mats, high) + tn(mats, low)


def product(multiply, a, b):
    return multiply(a[0], b[0]) + (multiply(a[0], b[1]) + multiply(a[1], b[0]))


def fold(square):
    half = square.shape[0] // 2
    row, column = iota((half, half), 0), iota((half, half), 1)
    first = square[:half, :half]
    mixed = jnp.where(row < column, first, square[half:, half:])
    centre = jnp.sum(jnp.where(row == column, first, 0.0), axis=0, keepdims=True)
    return jnp.concatenate([mixed, square[:half, half:]], axis=1), centre


def unfold(folded, centre):
    half = folded.shape[0]
    row, column = iota((half, half), 0), iota((half, half), 1)
    turned = folded.T
    mixed, mixed_turned = folded[:, :half], turned[:half]
    first = jnp.where(row < column, mixed, jnp.where(row > column, mixed_turned, centre))
    last = jnp.where(row >= column, mixed, mixed_turned)
    top = jnp.concatenate([first, folded[:, half:]], axis=1)
    return jnp.concatenate([top, jnp.concatenate([turned[half:], last], axis=1)], axis=0)


def pack(square):
    half = square.shape[0] // 2
    return jnp.concatenate([square[:half], square[half:]], axis=1)


def unpack(packed):
    half = packed.shape[1] // 2
    return jnp.concatenate([packed[:, :half], packed[:, half:]], axis=0)


def reach(index, count):
    return (index ^ ((index + 1) % count)).bit_length()


def gram_kernel(basis_ref, out_ref):
    copies = out_ref.shape[0]
    width = basis_ref.shape[1]
    wide = 2 * width
    row = iota((width, wide), 0)
    lane = iota((width, wide), 1)
    column = lane & (width - 1)
    sides = []
    for side in range(2):
        both = jnp.concatenate([basis_ref[side], basis_ref[side + 2]], axis=0)
        crossed = nt(both, both)
        sides.append(jnp.where(lane < width, crossed[:width], crossed[width:]))
    folded = jnp.where(row <= column, sides[0], sides[1])
    diagonal = jnp.sum(jnp.where(row == column, sides[1], 0.0), axis=0, keepdims=True)
    for copy in range(copies):
        out_ref[copy, :width] = folded
        out_ref[copy, width:] = jnp.broadcast_to(diagonal, (8, wide))


def path_kernel(rank_ref, path_ref, high_ref, low_ref):
    heights = path_ref.shape[0]
    row = iota(path_ref.shape[1:], 0)
    for height in range(heights):
        step = jnp.where(row < rank_ref[height], path_ref[height].astype(F32), 0.0)
        if height == 0:
            whole = step
        else:
            step = step.astype(BF16)
            whole = nn(high, step) + nn(low, step)
        high, low = halves(whole)
        high_ref[height] = high
        low_ref[height] = low


def near_kernel(
    rank_ref, place_ref, level_ref, parts_ref, bottom_ref, high_ref, low_ref, left_ref, sent_ref, first_ref, tiles
):
    nodes, width, _ = bottom_ref.shape
    wide = 2 * width
    half = width // 2
    targets = sent_ref.shape[0]
    heights = high_ref.shape[0]
    total = parts_ref[0]
    for part in range(1, parts_ref.shape[0]):
        total = total + parts_ref[part]
    folded = total[:width]
    diagonal = total[width : width + 1]
    turned = folded.T
    row = iota((width, width), 0)
    column = iota((width, width), 1)
    masked = []
    for node in range(nodes):
        pair, side = node // 2, node % 2
        here = folded[:, pair * width : (pair + 1) * width]
        there = turned[pair * width : (pair + 1) * width]
        if side == 0:
            gram = jnp.where(row <= column, here, there)
        else:
            centre = jnp.broadcast_to(diagonal[:, pair * width : (pair + 1) * width], (width, width))
            gram = jnp.where(row > column, here, jnp.where(row < column, there, centre))
        masked.append(keep_rank(gram, rank_ref[node]))
    bottom = halves(lift(masked, [bottom_ref[node] for node in range(nodes)]))
    lane = iota((1, wide), 1)
    lower = jnp.where(lane < width, rank_ref[1], rank_ref[3])
    diagonal = jnp.where((lane & (width - 1)) < lower, diagonal, 0.0)
    tiles[0] = jnp.concatenate([diagonal, jnp.zeros((7, wide), F32)], axis=0)
    parts = parts_ref.shape[0]
    share = half // (2 * parts)
    for height in range(heights):
        path = (high_ref[height], low_ref[height])
        term = product(tn, path, halves(product(nn, bottom, path)))
        if height == 0:
            first_ref[...] = pack(term)
            continue
        square, centre = fold(term)
        packed = pack(square)
        mine = packed[:share]
        for part in range(1, parts):
            mine = jnp.where(level_ref[0] == part, packed[part * share : (part + 1) * share], mine)
        centre = jnp.concatenate([centre, jnp.zeros((1, wide - half), F32)], axis=1)
        tiles[height] = jnp.concatenate([diagonal, mine, centre, jnp.zeros((6 - share, wide), F32)], axis=0)

    row = iota((width, wide), 0)
    lane = iota((width, wide), 1)
    column = lane & (width - 1)
    low = lane < width
    upper = jnp.where(low, rank_ref[0], rank_ref[2])
    lower = jnp.where(low, rank_ref[1], rank_ref[3])
    kept = jnp.maximum(row, column) < jnp.where(row <= column, upper, lower)
    share_rows = jnp.where(kept, folded, 0.0).astype(BF16)
    place = place_ref[0]
    for target in range(targets):
        device = 2 * target + 1
        height = reach(device, 2 * targets)
        inside = jnp.right_shift(place, height) == device >> height
        sent_ref[target, :width] = share_rows
        sent_ref[target, width:] = tiles[jnp.where(inside, height - 1, 0)].astype(BF16)

    row = iota((width, width), 0)
    even_first = jnp.where(row < half, 2 * row, 2 * row - width + 1)
    order = (iota((width, width), 1) == even_first).astype(F32).astype(BF16)
    for node in range(nodes):
        left_ref[node] = nt(nn(order, masked[node].astype(BF16)).astype(BF16), order).astype(BF16)


def sum_kernel(received_ref, out_ref):
    sources, rows, _ = received_ref.shape
    total = received_ref[0, rows - 8 :].astype(F32)
    for source in range(1, sources):
        total = total + received_ref[source, rows - 8 :].astype(F32)
    for copy in range(out_ref.shape[0]):
        out_ref[copy] = total


def top_kernel(core_ref, received_ref, first_ref, other_ref, done_ref, out_ref, scratch):
    parts = received_ref.shape[0] // 2
    wide = received_ref.shape[2]
    width = wide // 2
    half = width // 2
    share = half // (2 * parts)
    sums = [received_ref[part] + received_ref[parts + part] for part in range(parts)]
    packed = jnp.concatenate([value[1 : 1 + share] for value in sums], axis=0)
    high = unfold(unpack(packed), sums[0][1 + share : 2 + share, :half])
    scratch[...] = jnp.where(core_ref[0] == 1, high, unpack(first_ref[...] + other_ref[...]))
    natural = jnp.concatenate([scratch[pl.ds(side, half, stride=2), :] for side in range(2)], axis=1)
    for tile in range(half):
        out_ref[:, tile * wide : (tile + 1) * wide] = natural[tile : tile + 1]


def left_kernel(row_ref, blocks_ref, left_ref, out_ref, done_ref, spread):
    step = pl.program_id(0)
    count, flat = blocks_ref.shape
    width = left_ref.shape[1]
    wide = 2 * width
    tiles = flat // wide
    low = iota((width, wide), 1) < width
    for tile in range(tiles):
        spread[tile * count : (tile + 1) * count, :] = blocks_ref[:, tile * wide : (tile + 1) * wide].astype(F32)
    for index in range(0, count, 2):
        products = []
        for place in range(2):
            here = spread[pl.ds(index + place, tiles, stride=count), :]
            turned = pltpu.roll(here, width, 1)
            rows = jnp.where(
                low, jnp.concatenate([here, turned], axis=0), jnp.concatenate([turned, here], axis=0)
            ).astype(BF16)
            products.append(nn(left_ref[row_ref[step * count + index + place]], rows))
        out_ref[index // 2] = jnp.where(low, products[0], products[1]).astype(BF16)
    done_ref[...] = jnp.zeros_like(done_ref)


def project_kernel(
    owner_ref, column_ref, core_ref, rows_ref, own_ref, other_ref, out_ref, result, triangles
):
    step = pl.program_id(0)
    pairs, width, wide = rows_ref.shape
    count = 2 * pairs
    tiles = width // 2
    low = iota((tiles, wide), 1) < width
    none = jnp.zeros((width, wide), BF16)

    @pl.when(step == 0)
    def _():
        row = iota((width, wide), 0)
        lane = iota((width, wide), 1)
        column = lane & (width - 1)
        for cluster in range(4):
            mine = (lane < width) == (cluster < 2)
            parts = (row <= column, row < 0) if cluster % 2 == 0 else (row > column, row == column)
            for index, part in enumerate(parts):
                triangles[cluster, index] = (mine & part).astype(F32).astype(BF16)
        for place in range(2):
            mine = (lane < width) == (place == 0)
            triangles[4 + place, 0] = (mine & (row > column)).astype(F32).astype(BF16)
            triangles[4 + place, 1] = (mine & (row < column)).astype(F32).astype(BF16)

    for index in range(0, count, 2):
        folded = []
        for place in range(2):
            owner = owner_ref[step * count + index + place]
            source = jnp.right_shift(owner, 1)
            at_home = (owner & 1) == core_ref[0]
            folded.append(
                (
                    jnp.where(at_home, own_ref[source, :width], other_ref[source, :width]),
                    jnp.where(at_home, own_ref[source, width:], other_ref[source, width:])[:1],
                )
            )
        turned = jnp.concatenate([folded[0][0], folded[1][0]], axis=0).T
        for place in range(2):
            cluster = column_ref[step * count + index + place]
            here, centre = folded[place]
            mirrored = jnp.where(cluster < 2, turned[:width], turned[width:])
            right = (
                here * triangles[cluster, 0]
                + centre * triangles[cluster, 1]
                + mirrored * triangles[4 + place, cluster & 1]
            )
            weights = [right, none] if place == 0 else [none, right]
            full = nn(rows_ref[index // 2], jnp.concatenate(weights, axis=0))
            top, bottom = full[:tiles], full[tiles:]
            out = jnp.where(low, top, bottom) + pltpu.roll(jnp.where(low, bottom, top), width, 1)
            result[pl.ds(index + place, tiles, stride=count), :] = out
    for tile in range(tiles):
        out_ref[:, tile * wide : (tile + 1) * wide] = result[tile * count : (tile + 1) * count, :]


def shape(dims, dtype):
    return jax.ShapeDtypeStruct(dims, dtype)


def on_device(
    basis,
    bottom_transfer,
    bottom_rank,
    upper_transfer,
    upper_rank,
    couplings,
    row_cluster,
    column_owner,
    column_cluster,
):
    nodes, width, _ = basis.shape
    wide = 2 * width
    half = width // 2
    branches = lax.axis_size("branch")
    parts = lax.axis_size("level")
    levels = branches.bit_length() - 1
    me_branch = lax.axis_index("branch")
    me_level = lax.axis_index("level")
    core = me_branch & 1
    blk = couplings.shape[0]
    same_core = [list(range(c, branches, 2)) for c in range(2)]
    same_chip = [list(range(2 * parts * chip, 2 * parts * (chip + 1))) for chip in range(branches // 2)]
    partners = [(i, i ^ 1) for i in range(branches)]

    partial_sums = pl.pallas_call(
        gram_kernel,
        out_shape=shape((parts, width + 8, wide), F32),
        in_specs=[VMEM],
        out_specs=VMEM,
        compiler_params=SMALL,
        name="gram",
    )(basis)
    partial_sums, upper_transfer, upper_rank, bottom_transfer = lax.optimization_barrier(
        (partial_sums, upper_transfer, upper_rank, bottom_transfer)
    )
    gathered = lax.all_to_all(partial_sums, "level", 0, 0)
    heights = jnp.arange(levels, dtype=jnp.int32)
    slots = 2 * branches - jnp.right_shift(2 * branches, heights) + jnp.right_shift(me_branch, heights)
    path = jnp.take(upper_transfer, slots, axis=0).reshape(levels, width, width)
    path_high, path_low = pl.pallas_call(
        path_kernel,
        out_shape=[shape((levels, width, width), BF16)] * 2,
        in_specs=[SMEM, VMEM],
        out_specs=[VMEM, VMEM],
        compiler_params=SMALL,
        name="path",
    )(jnp.take(upper_rank, slots, axis=0), path)
    left, sent, first = pl.pallas_call(
        near_kernel,
        out_shape=[
            shape((nodes, width, width), BF16),
            shape((branches // 2, width + 8, wide), BF16),
            shape((half, wide), F32),
        ],
        in_specs=[SMEM, SMEM, SMEM, VMEM, VMEM, VMEM, VMEM],
        out_specs=[VMEM, VMEM, VMEM],
        scratch_shapes=[pltpu.VMEM((levels, 8, wide), F32)],
        compiler_params=SMALL,
        name="near",
    )(
        bottom_rank,
        me_branch[None],
        me_level[None],
        gathered,
        bottom_transfer.reshape(nodes, width, width),
        path_high,
        path_low,
    )
    own = lax.all_to_all(sent, "branch", 0, 0, axis_index_groups=same_core)
    first_other = lax.ppermute(first, "branch", partners)
    square = pl.BlockSpec((ROWS // 2, width, wide), lambda i, *_: (i, 0, 0))
    rows, done = pl.pallas_call(
        left_kernel,
        out_shape=[shape((blk // 2, width, wide), BF16), shape((8, wide), F32)],
        grid_spec=pltpu.PrefetchScalarGridSpec(
            num_scalar_prefetch=1,
            grid=(blk // ROWS,),
            in_specs=[
                pl.BlockSpec((ROWS, width * width), lambda i, *_: (i, 0)),
                pl.BlockSpec((nodes, width, width), lambda i, *_: (0, 0, 0)),
            ],
            out_specs=[square, pl.BlockSpec((8, wide), lambda i, *_: (0, 0))],
            scratch_shapes=[pltpu.VMEM((ROWS * half, wide), F32)],
        ),
        compiler_params=SMALL,
        cost_estimate=pl.CostEstimate(
            flops=4 * blk * width**3, bytes_accessed=4 * blk * width * width, transcendentals=0
        ),
        name="left",
    )(row_cluster, couplings, left)
    own, first_other, done = lax.optimization_barrier((own, first_other, done))
    summed = pl.pallas_call(
        sum_kernel,
        out_shape=shape((2 * parts, 8, wide), F32),
        in_specs=[VMEM],
        out_specs=VMEM,
        compiler_params=SMALL,
        cost_estimate=pl.CostEstimate(flops=10**10, bytes_accessed=own.size, transcendentals=0),
        name="sum",
    )(own)
    other = lax.ppermute(own, "branch", partners)
    quarters = lax.all_to_all(summed, ("branch", "level"), 0, 0, axis_index_groups=same_chip)

    whole = pl.BlockSpec(own.shape, lambda i, *_: (0, 0, 0))
    projected = pl.pallas_call(
        project_kernel,
        out_shape=shape((blk, width * width), F32),
        grid_spec=pltpu.PrefetchScalarGridSpec(
            num_scalar_prefetch=3,
            grid=(blk // BLOCKS,),
            in_specs=[pl.BlockSpec((BLOCKS // 2, width, wide), lambda i, *_: (i, 0, 0)), whole, whole],
            out_specs=pl.BlockSpec((BLOCKS, width * width), lambda i, *_: (i, 0)),
            scratch_shapes=[
                pltpu.VMEM((BLOCKS * half, wide), F32),
                pltpu.VMEM((6, 2, width, wide), BF16),
            ],
        ),
        compiler_params=pltpu.CompilerParams(vmem_limit_bytes=12 * 1024 * 1024),
        cost_estimate=pl.CostEstimate(
            flops=8 * blk * width**3, bytes_accessed=6 * blk * width * width, transcendentals=0
        ),
        name="project",
    )(column_owner[:, 0], column_cluster, core[None], rows, own, other)
    projected, quarters = lax.optimization_barrier((projected, quarters))
    upper_grams = pl.pallas_call(
        top_kernel,
        out_shape=shape((1, width * width), F32),
        in_specs=[SMEM, VMEM, VMEM, VMEM, VMEM],
        out_specs=VMEM,
        scratch_shapes=[pltpu.VMEM((width, width), F32)],
        compiler_params=SMALL,
        name="top",
    )(core[None], quarters, first, first_other, done)
    return (upper_grams, projected)


def solution(mesh):
    placed = (
        P("branch", None, "level"),
        P("branch", None),
        P("branch"),
        P(),
        P(),
        P(("branch", "level"), None),
        P(("branch", "level")),
        P(("branch", "level"), None),
        P(("branch", "level")),
    )
    return jax.shard_map(
        on_device,
        mesh=mesh,
        in_specs=placed,
        out_specs=(P("branch", None), P(("branch", "level"), None)),
        check_vma=False,
    )
```

```python
import jax
import jax.numpy as jnp
from jax import lax
from jax.experimental import pallas as pl
from jax.experimental.pallas import tpu as pltpu
from jax.sharding import PartitionSpec as P

VMEM = pl.BlockSpec(memory_space=pltpu.VMEM)
SMEM = pl.BlockSpec(memory_space=pltpu.SMEM)
SMALL = pltpu.CompilerParams(vmem_limit_bytes=8 * 1024 * 1024)
ROWS = 16
F32 = jnp.float32
BF16 = jnp.bfloat16


def iota(shape, axis):
    return lax.broadcasted_iota(jnp.int32, shape, axis)


def nn(a, b):
    return jnp.dot(a, b, preferred_element_type=F32)


def nt(a, b):
    return lax.dot_general(a, b, (((1,), (1,)), ((), ())), preferred_element_type=F32)


def tn(a, b):
    return lax.dot_general(a, b, (((0,), (0,)), ((), ())), preferred_element_type=F32)


def halves(x):
    high = x.astype(BF16)
    return high, (x - high.astype(F32)).astype(BF16)


def keep_rank(gram, rank):
    return jnp.where((iota(gram.shape, 0) < rank) & (iota(gram.shape, 1) < rank), gram, 0.0)


def lift(masked, transfer):
    inner = []
    for gram, mat in zip(masked, transfer):
        high, low = halves(gram)
        inner.append(nn(high, mat) + nn(low, mat))
    high, low = halves(jnp.concatenate(inner, axis=0))
    mats = jnp.concatenate(transfer, axis=0)
    return tn(mats, high) + tn(mats, low)


def product(multiply, a, b):
    return multiply(a[0], b[0]) + (multiply(a[0], b[1]) + multiply(a[1], b[0]))


def fold(square):
    half = square.shape[0] // 2
    row, column = iota((half, half), 0), iota((half, half), 1)
    first = square[:half, :half]
    mixed = jnp.where(row < column, first, square[half:, half:])
    centre = jnp.sum(jnp.where(row == column, first, 0.0), axis=0, keepdims=True)
    return jnp.concatenate([mixed, square[:half, half:]], axis=1), centre


def unfold(folded, centre):
    half = folded.shape[0]
    row, column = iota((half, half), 0), iota((half, half), 1)
    turned = folded.T
    mixed, mixed_turned = folded[:, :half], turned[:half]
    first = jnp.where(row < column, mixed, jnp.where(row > column, mixed_turned, centre))
    last = jnp.where(row >= column, mixed, mixed_turned)
    top = jnp.concatenate([first, folded[:, half:]], axis=1)
    return jnp.concatenate([top, jnp.concatenate([turned[half:], last], axis=1)], axis=0)


def pack(square):
    half = square.shape[0] // 2
    return jnp.concatenate([square[:half], square[half:]], axis=1)


def unpack(packed):
    half = packed.shape[1] // 2
    return jnp.concatenate([packed[:, :half], packed[:, half:]], axis=0)


def reach(index, count):
    return (index ^ ((index + 1) % count)).bit_length()


def gram_kernel(basis_ref, out_ref):
    copies = out_ref.shape[0]
    width = basis_ref.shape[1]
    wide = 2 * width
    row = iota((width, wide), 0)
    lane = iota((width, wide), 1)
    column = lane & (width - 1)
    sides = []
    for side in range(2):
        both = jnp.concatenate([basis_ref[side], basis_ref[side + 2]], axis=0)
        crossed = nt(both, both)
        sides.append(jnp.where(lane < width, crossed[:width], crossed[width:]))
    folded = jnp.where(row <= column, sides[0], sides[1])
    diagonal = jnp.sum(jnp.where(row == column, sides[1], 0.0), axis=0, keepdims=True)
    for copy in range(copies):
        out_ref[copy, :width] = folded
        out_ref[copy, width:] = jnp.broadcast_to(diagonal, (8, wide))


def path_kernel(rank_ref, path_ref, high_ref, low_ref):
    heights = path_ref.shape[0]
    row = iota(path_ref.shape[1:], 0)
    for height in range(heights):
        step = jnp.where(row < rank_ref[height], path_ref[height].astype(F32), 0.0)
        if height == 0:
            whole = step
        else:
            step = step.astype(BF16)
            whole = nn(high, step) + nn(low, step)
        high, low = halves(whole)
        high_ref[height] = high
        low_ref[height] = low


def near_kernel(
    rank_ref, place_ref, level_ref, parts_ref, bottom_ref, high_ref, low_ref, left_ref, sent_ref, first_ref, tiles
):
    nodes, width, _ = bottom_ref.shape
    wide = 2 * width
    half = width // 2
    targets = sent_ref.shape[0]
    heights = high_ref.shape[0]
    total = parts_ref[0]
    for part in range(1, parts_ref.shape[0]):
        total = total + parts_ref[part]
    folded = total[:width]
    diagonal = total[width : width + 1]
    turned = folded.T
    row = iota((width, width), 0)
    column = iota((width, width), 1)
    masked = []
    for node in range(nodes):
        pair, side = node // 2, node % 2
        here = folded[:, pair * width : (pair + 1) * width]
        there = turned[pair * width : (pair + 1) * width]
        if side == 0:
            gram = jnp.where(row <= column, here, there)
        else:
            centre = jnp.broadcast_to(diagonal[:, pair * width : (pair + 1) * width], (width, width))
            gram = jnp.where(row > column, here, jnp.where(row < column, there, centre))
        masked.append(keep_rank(gram, rank_ref[node]))
    bottom = halves(lift(masked, [bottom_ref[node] for node in range(nodes)]))
    lane = iota((1, wide), 1)
    lower = jnp.where(lane < width, rank_ref[1], rank_ref[3])
    diagonal = jnp.where((lane & (width - 1)) < lower, diagonal, 0.0)
    tiles[0] = jnp.concatenate([diagonal, jnp.zeros((7, wide), F32)], axis=0)
    parts = parts_ref.shape[0]
    share = half // (2 * parts)
    for height in range(heights):
        path = (high_ref[height], low_ref[height])
        term = product(tn, path, halves(product(nn, bottom, path)))
        if height == 0:
            first_ref[...] = pack(term)
            continue
        square, centre = fold(term)
        packed = pack(square)
        mine = packed[:share]
        for part in range(1, parts):
            mine = jnp.where(level_ref[0] == part, packed[part * share : (part + 1) * share], mine)
        centre = jnp.concatenate([centre, jnp.zeros((1, wide - half), F32)], axis=1)
        tiles[height] = jnp.concatenate([diagonal, mine, centre, jnp.zeros((6 - share, wide), F32)], axis=0)

    row = iota((width, wide), 0)
    lane = iota((width, wide), 1)
    column = lane & (width - 1)
    low = lane < width
    upper = jnp.where(low, rank_ref[0], rank_ref[2])
    lower = jnp.where(low, rank_ref[1], rank_ref[3])
    kept = jnp.maximum(row, column) < jnp.where(row <= column, upper, lower)
    share_rows = jnp.where(kept, folded, 0.0).astype(BF16)
    place = place_ref[0]
    for target in range(targets):
        device = 2 * target + 1
        height = reach(device, 2 * targets)
        inside = jnp.right_shift(place, height) == device >> height
        sent_ref[target, :width] = share_rows
        sent_ref[target, width:] = tiles[jnp.where(inside, height - 1, 0)].astype(BF16)

    row = iota((width, width), 0)
    even_first = jnp.where(row < half, 2 * row, 2 * row - width + 1)
    order = (iota((width, width), 1) == even_first).astype(F32).astype(BF16)
    for node in range(nodes):
        left_ref[node] = nt(nn(order, masked[node].astype(BF16)).astype(BF16), order).astype(BF16)


def sum_kernel(received_ref, out_ref):
    sources, rows, _ = received_ref.shape
    total = received_ref[0, rows - 8 :].astype(F32)
    for source in range(1, sources):
        total = total + received_ref[source, rows - 8 :].astype(F32)
    for copy in range(out_ref.shape[0]):
        out_ref[copy] = total


def top_kernel(core_ref, received_ref, first_ref, other_ref, done_ref, out_ref, scratch):
    parts = received_ref.shape[0] // 2
    wide = received_ref.shape[2]
    width = wide // 2
    half = width // 2
    share = half // (2 * parts)
    sums = [received_ref[part] + received_ref[parts + part] for part in range(parts)]
    packed = jnp.concatenate([value[1 : 1 + share] for value in sums], axis=0)
    high = unfold(unpack(packed), sums[0][1 + share : 2 + share, :half])
    scratch[...] = jnp.where(core_ref[0] == 1, high, unpack(first_ref[...] + other_ref[...]))
    natural = jnp.concatenate([scratch[pl.ds(side, half, stride=2), :] for side in range(2)], axis=1)
    for tile in range(half):
        out_ref[:, tile * wide : (tile + 1) * wide] = natural[tile : tile + 1]


def left_kernel(row_ref, blocks_ref, left_ref, out_ref, done_ref, spread):
    step = pl.program_id(0)
    count, flat = blocks_ref.shape
    width = left_ref.shape[1]
    wide = 2 * width
    tiles = flat // wide
    low = iota((width, wide), 1) < width
    for tile in range(tiles):
        spread[tile * count : (tile + 1) * count, :] = blocks_ref[:, tile * wide : (tile + 1) * wide].astype(F32)
    for index in range(0, count, 2):
        products = []
        for place in range(2):
            here = spread[pl.ds(index + place, tiles, stride=count), :]
            turned = pltpu.roll(here, width, 1)
            rows = jnp.where(
                low, jnp.concatenate([here, turned], axis=0), jnp.concatenate([turned, here], axis=0)
            ).astype(BF16)
            products.append(nn(left_ref[row_ref[step * count + index + place]], rows))
        out_ref[index // 2] = jnp.where(low, products[0], products[1]).astype(BF16)
    done_ref[...] = jnp.zeros_like(done_ref)


def project_kernel(
    owner_ref, column_ref, core_ref, rows_ref, own_ref, other_ref, out_ref, kept_ref, result, triangles
):
    step = pl.program_id(0)
    pairs, width, wide = rows_ref.shape
    count = 2 * pairs
    tiles = width // 2
    low = iota((tiles, wide), 1) < width
    none = jnp.zeros((width, wide), BF16)

    @pl.when(step == 0)
    def _():
        row = iota((width, wide), 0)
        lane = iota((width, wide), 1)
        column = lane & (width - 1)
        for cluster in range(4):
            mine = (lane < width) == (cluster < 2)
            parts = (row <= column, row < 0) if cluster % 2 == 0 else (row > column, row == column)
            for index, part in enumerate(parts):
                triangles[cluster, index] = (mine & part).astype(F32).astype(BF16)
        for place in range(2):
            mine = (lane < width) == (place == 0)
            triangles[4 + place, 0] = (mine & (row > column)).astype(F32).astype(BF16)
            triangles[4 + place, 1] = (mine & (row < column)).astype(F32).astype(BF16)

    for index in range(0, count, 2):
        folded = []
        for place in range(2):
            owner = owner_ref[step * count + index + place]
            source = jnp.right_shift(owner, 1)
            at_home = (owner & 1) == core_ref[0]
            folded.append(
                (
                    jnp.where(at_home, own_ref[source, :width], other_ref[source, :width]),
                    jnp.where(at_home, own_ref[source, width:], other_ref[source, width:])[:1],
                )
            )
        turned = jnp.concatenate([folded[0][0], folded[1][0]], axis=0).T
        for place in range(2):
            cluster = column_ref[step * count + index + place]
            here, centre = folded[place]
            mirrored = jnp.where(cluster < 2, turned[:width], turned[width:])
            right = (
                here * triangles[cluster, 0]
                + centre * triangles[cluster, 1]
                + mirrored * triangles[4 + place, cluster & 1]
            )
            weights = [right, none] if place == 0 else [none, right]
            full = nn(rows_ref[index // 2], jnp.concatenate(weights, axis=0))
            top, bottom = full[:tiles], full[tiles:]
            out = jnp.where(low, top, bottom) + pltpu.roll(jnp.where(low, bottom, top), width, 1)
            result[pl.ds(index + place, tiles, stride=count), :] = out
    for tile in range(tiles):
        out_ref[:, tile * wide : (tile + 1) * wide] = result[tile * count : (tile + 1) * count, :]


def shape(dims, dtype):
    return jax.ShapeDtypeStruct(dims, dtype)


def on_device(
    basis,
    bottom_transfer,
    bottom_rank,
    upper_transfer,
    upper_rank,
    couplings,
    row_cluster,
    column_owner,
    column_cluster,
):
    nodes, width, _ = basis.shape
    wide = 2 * width
    half = width // 2
    branches = lax.axis_size("branch")
    parts = lax.axis_size("level")
    levels = branches.bit_length() - 1
    me_branch = lax.axis_index("branch")
    me_level = lax.axis_index("level")
    core = me_branch & 1
    blk = couplings.shape[0]
    same_core = [list(range(c, branches, 2)) for c in range(2)]
    same_chip = [list(range(2 * parts * chip, 2 * parts * (chip + 1))) for chip in range(branches // 2)]
    partners = [(i, i ^ 1) for i in range(branches)]

    partial_sums = pl.pallas_call(
        gram_kernel,
        out_shape=shape((parts, width + 8, wide), F32),
        in_specs=[VMEM],
        out_specs=VMEM,
        compiler_params=SMALL,
        name="gram",
    )(basis)
    partial_sums, upper_transfer, upper_rank, bottom_transfer = lax.optimization_barrier(
        (partial_sums, upper_transfer, upper_rank, bottom_transfer)
    )
    gathered = lax.all_to_all(partial_sums, "level", 0, 0)
    heights = jnp.arange(levels, dtype=jnp.int32)
    slots = 2 * branches - jnp.right_shift(2 * branches, heights) + jnp.right_shift(me_branch, heights)
    path = jnp.take(upper_transfer, slots, axis=0).reshape(levels, width, width)
    path_high, path_low = pl.pallas_call(
        path_kernel,
        out_shape=[shape((levels, width, width), BF16)] * 2,
        in_specs=[SMEM, VMEM],
        out_specs=[VMEM, VMEM],
        compiler_params=SMALL,
        name="path",
    )(jnp.take(upper_rank, slots, axis=0), path)
    left, sent, first = pl.pallas_call(
        near_kernel,
        out_shape=[
            shape((nodes, width, width), BF16),
            shape((branches // 2, width + 8, wide), BF16),
            shape((half, wide), F32),
        ],
        in_specs=[SMEM, SMEM, SMEM, VMEM, VMEM, VMEM, VMEM],
        out_specs=[VMEM, VMEM, VMEM],
        scratch_shapes=[pltpu.VMEM((levels, 8, wide), F32)],
        compiler_params=SMALL,
        name="near",
    )(
        bottom_rank,
        me_branch[None],
        me_level[None],
        gathered,
        bottom_transfer.reshape(nodes, width, width),
        path_high,
        path_low,
    )
    own = lax.all_to_all(sent, "branch", 0, 0, axis_index_groups=same_core)
    first_other = lax.ppermute(first, "branch", partners)
    square = pl.BlockSpec((ROWS // 2, width, wide), lambda i, *_: (i, 0, 0))
    rows, done = pl.pallas_call(
        left_kernel,
        out_shape=[shape((blk // 2, width, wide), BF16), shape((8, wide), F32)],
        grid_spec=pltpu.PrefetchScalarGridSpec(
            num_scalar_prefetch=1,
            grid=(blk // ROWS,),
            in_specs=[
                pl.BlockSpec((ROWS, width * width), lambda i, *_: (i, 0)),
                pl.BlockSpec((nodes, width, width), lambda i, *_: (0, 0, 0)),
            ],
            out_specs=[square, pl.BlockSpec((8, wide), lambda i, *_: (0, 0))],
            scratch_shapes=[pltpu.VMEM((ROWS * half, wide), F32)],
        ),
        compiler_params=SMALL,
        cost_estimate=pl.CostEstimate(
            flops=4 * blk * width**3, bytes_accessed=4 * blk * width * width, transcendentals=0
        ),
        name="left",
    )(row_cluster, couplings, left)
    own, first_other, done = lax.optimization_barrier((own, first_other, done))
    summed = pl.pallas_call(
        sum_kernel,
        out_shape=shape((2 * parts, 8, wide), F32),
        in_specs=[VMEM],
        out_specs=VMEM,
        compiler_params=SMALL,
        name="sum",
    )(own)
    other = lax.ppermute(own, "branch", partners)
    quarters = lax.all_to_all(summed, ("branch", "level"), 0, 0, axis_index_groups=same_chip)

    whole = pl.BlockSpec(own.shape, lambda i, *_: (0, 0, 0))
    projected, _ = pl.pallas_call(
        project_kernel,
        out_shape=[shape((blk, width * width), F32), shape(rows.shape, BF16)],
        grid_spec=pltpu.PrefetchScalarGridSpec(
            num_scalar_prefetch=3,
            grid=(blk // ROWS,),
            in_specs=[square, whole, whole],
            out_specs=[
                pl.BlockSpec((ROWS, width * width), lambda i, *_: (i, 0)),
                pl.BlockSpec(memory_space=pl.ANY),
            ],
            scratch_shapes=[
                pltpu.VMEM((ROWS * half, wide), F32),
                pltpu.VMEM((6, 2, width, wide), BF16),
            ],
        ),
        compiler_params=pltpu.CompilerParams(vmem_limit_bytes=12 * 1024 * 1024),
        cost_estimate=pl.CostEstimate(
            flops=8 * blk * width**3, bytes_accessed=6 * blk * width * width, transcendentals=0
        ),
        input_output_aliases={3: 1},
        name="project",
    )(column_owner[:, 0], column_cluster, core[None], rows, own, other)
    projected, quarters = lax.optimization_barrier((projected, quarters))
    upper_grams = pl.pallas_call(
        top_kernel,
        out_shape=shape((1, width * width), F32),
        in_specs=[SMEM, VMEM, VMEM, VMEM, VMEM],
        out_specs=VMEM,
        scratch_shapes=[pltpu.VMEM((width, width), F32)],
        compiler_params=SMALL,
        name="top",
    )(core[None], quarters, first, first_other, done)
    return (upper_grams, projected)


def solution(mesh):
    placed = (
        P("branch", None, "level"),
        P("branch", None),
        P("branch"),
        P(),
        P(),
        P(("branch", "level"), None),
        P(("branch", "level")),
        P(("branch", "level"), None),
        P(("branch", "level")),
    )
    return jax.shard_map(
        on_device,
        mesh=mesh,
        in_specs=placed,
        out_specs=(P("branch", None), P(("branch", "level"), None)),
        check_vma=False,
    )
```

```python
import jax
import jax.numpy as jnp
from jax import lax
from jax.experimental import pallas as pl
from jax.experimental.pallas import tpu as pltpu
from jax.sharding import PartitionSpec as P

VMEM = pl.BlockSpec(memory_space=pltpu.VMEM)
SMEM = pl.BlockSpec(memory_space=pltpu.SMEM)
SMALL = pltpu.CompilerParams(vmem_limit_bytes=8 * 1024 * 1024)
ROWS = 16
F32 = jnp.float32
BF16 = jnp.bfloat16


def iota(shape, axis):
    return lax.broadcasted_iota(jnp.int32, shape, axis)


def nn(a, b):
    return jnp.dot(a, b, preferred_element_type=F32)


def nt(a, b):
    return lax.dot_general(a, b, (((1,), (1,)), ((), ())), preferred_element_type=F32)


def tn(a, b):
    return lax.dot_general(a, b, (((0,), (0,)), ((), ())), preferred_element_type=F32)


def halves(x):
    high = x.astype(BF16)
    return high, (x - high.astype(F32)).astype(BF16)


def keep_rank(gram, rank):
    return jnp.where((iota(gram.shape, 0) < rank) & (iota(gram.shape, 1) < rank), gram, 0.0)


def lift(masked, transfer):
    inner = []
    for gram, mat in zip(masked, transfer):
        high, low = halves(gram)
        inner.append(nn(high, mat) + nn(low, mat))
    high, low = halves(jnp.concatenate(inner, axis=0))
    mats = jnp.concatenate(transfer, axis=0)
    return tn(mats, high) + tn(mats, low)


def product(multiply, a, b):
    return multiply(a[0], b[0]) + (multiply(a[0], b[1]) + multiply(a[1], b[0]))


def fold(square):
    half = square.shape[0] // 2
    row, column = iota((half, half), 0), iota((half, half), 1)
    first = square[:half, :half]
    mixed = jnp.where(row < column, first, square[half:, half:])
    centre = jnp.sum(jnp.where(row == column, first, 0.0), axis=0, keepdims=True)
    return jnp.concatenate([mixed, square[:half, half:]], axis=1), centre


def unfold(folded, centre):
    half = folded.shape[0]
    row, column = iota((half, half), 0), iota((half, half), 1)
    turned = folded.T
    mixed, mixed_turned = folded[:, :half], turned[:half]
    first = jnp.where(row < column, mixed, jnp.where(row > column, mixed_turned, centre))
    last = jnp.where(row >= column, mixed, mixed_turned)
    top = jnp.concatenate([first, folded[:, half:]], axis=1)
    return jnp.concatenate([top, jnp.concatenate([turned[half:], last], axis=1)], axis=0)


def pack(square):
    half = square.shape[0] // 2
    return jnp.concatenate([square[:half], square[half:]], axis=1)


def unpack(packed):
    half = packed.shape[1] // 2
    return jnp.concatenate([packed[:, :half], packed[:, half:]], axis=0)


def reach(index, count):
    return (index ^ ((index + 1) % count)).bit_length()


def gram_kernel(basis_ref, out_ref):
    copies = out_ref.shape[0]
    width = basis_ref.shape[1]
    wide = 2 * width
    row = iota((width, wide), 0)
    lane = iota((width, wide), 1)
    column = lane & (width - 1)
    sides = []
    for side in range(2):
        both = jnp.concatenate([basis_ref[side], basis_ref[side + 2]], axis=0)
        crossed = nt(both, both)
        sides.append(jnp.where(lane < width, crossed[:width], crossed[width:]))
    folded = jnp.where(row <= column, sides[0], sides[1])
    diagonal = jnp.sum(jnp.where(row == column, sides[1], 0.0), axis=0, keepdims=True)
    for copy in range(copies):
        out_ref[copy, :width] = folded
        out_ref[copy, width:] = jnp.broadcast_to(diagonal, (8, wide))


def path_kernel(rank_ref, path_ref, high_ref, low_ref):
    heights = path_ref.shape[0]
    row = iota(path_ref.shape[1:], 0)
    for height in range(heights):
        step = jnp.where(row < rank_ref[height], path_ref[height].astype(F32), 0.0)
        if height == 0:
            whole = step
        else:
            step = step.astype(BF16)
            whole = nn(high, step) + nn(low, step)
        high, low = halves(whole)
        high_ref[height] = high
        low_ref[height] = low


def near_kernel(
    rank_ref, place_ref, level_ref, parts_ref, bottom_ref, high_ref, low_ref, left_ref, sent_ref, first_ref, tiles
):
    nodes, width, _ = bottom_ref.shape
    wide = 2 * width
    half = width // 2
    targets = sent_ref.shape[0]
    heights = high_ref.shape[0]
    total = parts_ref[0]
    for part in range(1, parts_ref.shape[0]):
        total = total + parts_ref[part]
    folded = total[:width]
    diagonal = total[width : width + 1]
    turned = folded.T
    row = iota((width, width), 0)
    column = iota((width, width), 1)
    masked = []
    for node in range(nodes):
        pair, side = node // 2, node % 2
        here = folded[:, pair * width : (pair + 1) * width]
        there = turned[pair * width : (pair + 1) * width]
        if side == 0:
            gram = jnp.where(row <= column, here, there)
        else:
            centre = jnp.broadcast_to(diagonal[:, pair * width : (pair + 1) * width], (width, width))
            gram = jnp.where(row > column, here, jnp.where(row < column, there, centre))
        masked.append(keep_rank(gram, rank_ref[node]))
    bottom = halves(lift(masked, [bottom_ref[node] for node in range(nodes)]))
    lane = iota((1, wide), 1)
    lower = jnp.where(lane < width, rank_ref[1], rank_ref[3])
    diagonal = jnp.where((lane & (width - 1)) < lower, diagonal, 0.0)
    tiles[0] = jnp.concatenate([diagonal, jnp.zeros((7, wide), F32)], axis=0)
    parts = parts_ref.shape[0]
    share = half // (2 * parts)
    for height in range(heights):
        path = (high_ref[height], low_ref[height])
        term = product(tn, path, halves(product(nn, bottom, path)))
        if height == 0:
            first_ref[...] = pack(term)
            continue
        square, centre = fold(term)
        packed = pack(square)
        mine = packed[:share]
        for part in range(1, parts):
            mine = jnp.where(level_ref[0] == part, packed[part * share : (part + 1) * share], mine)
        centre = jnp.concatenate([centre, jnp.zeros((1, wide - half), F32)], axis=1)
        tiles[height] = jnp.concatenate([diagonal, mine, centre, jnp.zeros((6 - share, wide), F32)], axis=0)

    row = iota((width, wide), 0)
    lane = iota((width, wide), 1)
    column = lane & (width - 1)
    low = lane < width
    upper = jnp.where(low, rank_ref[0], rank_ref[2])
    lower = jnp.where(low, rank_ref[1], rank_ref[3])
    kept = jnp.maximum(row, column) < jnp.where(row <= column, upper, lower)
    share_rows = jnp.where(kept, folded, 0.0).astype(BF16)
    place = place_ref[0]
    for target in range(targets):
        device = 2 * target + 1
        height = reach(device, 2 * targets)
        inside = jnp.right_shift(place, height) == device >> height
        sent_ref[target, :width] = share_rows
        sent_ref[target, width:] = tiles[jnp.where(inside, height - 1, 0)].astype(BF16)

    row = iota((width, width), 0)
    even_first = jnp.where(row < half, 2 * row, 2 * row - width + 1)
    order = (iota((width, width), 1) == even_first).astype(F32).astype(BF16)
    for node in range(nodes):
        left_ref[node] = nt(nn(order, masked[node].astype(BF16)).astype(BF16), order).astype(BF16)


def sum_kernel(received_ref, rows_ref, out_ref):
    sources, rows, _ = received_ref.shape
    total = received_ref[0, rows - 8 :].astype(F32)
    for source in range(1, sources):
        total = total + received_ref[source, rows - 8 :].astype(F32)
    for copy in range(out_ref.shape[0]):
        out_ref[copy] = total


def top_kernel(core_ref, received_ref, first_ref, other_ref, done_ref, out_ref, scratch):
    parts = received_ref.shape[0] // 2
    wide = received_ref.shape[2]
    width = wide // 2
    half = width // 2
    share = half // (2 * parts)
    sums = [received_ref[part] + received_ref[parts + part] for part in range(parts)]
    packed = jnp.concatenate([value[1 : 1 + share] for value in sums], axis=0)
    high = unfold(unpack(packed), sums[0][1 + share : 2 + share, :half])
    scratch[...] = jnp.where(core_ref[0] == 1, high, unpack(first_ref[...] + other_ref[...]))
    natural = jnp.concatenate([scratch[pl.ds(side, half, stride=2), :] for side in range(2)], axis=1)
    for tile in range(half):
        out_ref[:, tile * wide : (tile + 1) * wide] = natural[tile : tile + 1]


def left_kernel(row_ref, blocks_ref, left_ref, out_ref, done_ref, spread):
    step = pl.program_id(0)
    count, flat = blocks_ref.shape
    width = left_ref.shape[1]
    wide = 2 * width
    tiles = flat // wide
    low = iota((width, wide), 1) < width
    for tile in range(tiles):
        spread[tile * count : (tile + 1) * count, :] = blocks_ref[:, tile * wide : (tile + 1) * wide].astype(F32)
    for index in range(0, count, 2):
        products = []
        for place in range(2):
            here = spread[pl.ds(index + place, tiles, stride=count), :]
            turned = pltpu.roll(here, width, 1)
            rows = jnp.where(
                low, jnp.concatenate([here, turned], axis=0), jnp.concatenate([turned, here], axis=0)
            ).astype(BF16)
            products.append(nn(left_ref[row_ref[step * count + index + place]], rows))
        out_ref[index // 2] = jnp.where(low, products[0], products[1]).astype(BF16)
    done_ref[...] = jnp.zeros_like(done_ref)


def project_kernel(
    owner_ref, column_ref, core_ref, rows_ref, own_ref, other_ref, out_ref, result, triangles
):
    step = pl.program_id(0)
    pairs, width, wide = rows_ref.shape
    count = 2 * pairs
    tiles = width // 2
    low = iota((tiles, wide), 1) < width
    none = jnp.zeros((width, wide), BF16)

    @pl.when(step == 0)
    def _():
        row = iota((width, wide), 0)
        lane = iota((width, wide), 1)
        column = lane & (width - 1)
        for cluster in range(4):
            mine = (lane < width) == (cluster < 2)
            parts = (row <= column, row < 0) if cluster % 2 == 0 else (row > column, row == column)
            for index, part in enumerate(parts):
                triangles[cluster, index] = (mine & part).astype(F32).astype(BF16)
        for place in range(2):
            mine = (lane < width) == (place == 0)
            triangles[4 + place, 0] = (mine & (row > column)).astype(F32).astype(BF16)
            triangles[4 + place, 1] = (mine & (row < column)).astype(F32).astype(BF16)

    for index in range(0, count, 2):
        folded = []
        for place in range(2):
            owner = owner_ref[step * count + index + place]
            source = jnp.right_shift(owner, 1)
            at_home = (owner & 1) == core_ref[0]
            folded.append(
                (
                    jnp.where(at_home, own_ref[source, :width], other_ref[source, :width]),
                    jnp.where(at_home, own_ref[source, width:], other_ref[source, width:])[:1],
                )
            )
        turned = jnp.concatenate([folded[0][0], folded[1][0]], axis=0).T
        for place in range(2):
            cluster = column_ref[step * count + index + place]
            here, centre = folded[place]
            mirrored = jnp.where(cluster < 2, turned[:width], turned[width:])
            right = (
                here * triangles[cluster, 0]
                + centre * triangles[cluster, 1]
                + mirrored * triangles[4 + place, cluster & 1]
            )
            weights = [right, none] if place == 0 else [none, right]
            full = nn(rows_ref[index // 2], jnp.concatenate(weights, axis=0))
            top, bottom = full[:tiles], full[tiles:]
            out = jnp.where(low, top, bottom) + pltpu.roll(jnp.where(low, bottom, top), width, 1)
            result[pl.ds(index + place, tiles, stride=count), :] = out
    for tile in range(tiles):
        out_ref[:, tile * wide : (tile + 1) * wide] = result[tile * count : (tile + 1) * count, :]


def shape(dims, dtype):
    return jax.ShapeDtypeStruct(dims, dtype)


def on_device(
    basis,
    bottom_transfer,
    bottom_rank,
    upper_transfer,
    upper_rank,
    couplings,
    row_cluster,
    column_owner,
    column_cluster,
):
    nodes, width, _ = basis.shape
    wide = 2 * width
    half = width // 2
    branches = lax.axis_size("branch")
    parts = lax.axis_size("level")
    levels = branches.bit_length() - 1
    me_branch = lax.axis_index("branch")
    me_level = lax.axis_index("level")
    core = me_branch & 1
    blk = couplings.shape[0]
    same_core = [list(range(c, branches, 2)) for c in range(2)]
    same_chip = [list(range(2 * parts * chip, 2 * parts * (chip + 1))) for chip in range(branches // 2)]
    partners = [(i, i ^ 1) for i in range(branches)]

    partial_sums = pl.pallas_call(
        gram_kernel,
        out_shape=shape((parts, width + 8, wide), F32),
        in_specs=[VMEM],
        out_specs=VMEM,
        compiler_params=SMALL,
        name="gram",
    )(basis)
    partial_sums, upper_transfer, upper_rank, bottom_transfer = lax.optimization_barrier(
        (partial_sums, upper_transfer, upper_rank, bottom_transfer)
    )
    gathered = lax.all_to_all(partial_sums, "level", 0, 0)
    heights = jnp.arange(levels, dtype=jnp.int32)
    slots = 2 * branches - jnp.right_shift(2 * branches, heights) + jnp.right_shift(me_branch, heights)
    path = jnp.take(upper_transfer, slots, axis=0).reshape(levels, width, width)
    path_high, path_low = pl.pallas_call(
        path_kernel,
        out_shape=[shape((levels, width, width), BF16)] * 2,
        in_specs=[SMEM, VMEM],
        out_specs=[VMEM, VMEM],
        compiler_params=SMALL,
        name="path",
    )(jnp.take(upper_rank, slots, axis=0), path)
    left, sent, first = pl.pallas_call(
        near_kernel,
        out_shape=[
            shape((nodes, width, width), BF16),
            shape((branches // 2, width + 8, wide), BF16),
            shape((half, wide), F32),
        ],
        in_specs=[SMEM, SMEM, SMEM, VMEM, VMEM, VMEM, VMEM],
        out_specs=[VMEM, VMEM, VMEM],
        scratch_shapes=[pltpu.VMEM((levels, 8, wide), F32)],
        compiler_params=SMALL,
        name="near",
    )(
        bottom_rank,
        me_branch[None],
        me_level[None],
        gathered,
        bottom_transfer.reshape(nodes, width, width),
        path_high,
        path_low,
    )
    own = lax.all_to_all(sent, "branch", 0, 0, axis_index_groups=same_core)
    first_other = lax.ppermute(first, "branch", partners)
    square = pl.BlockSpec((ROWS // 2, width, wide), lambda i, *_: (i, 0, 0))
    rows, done = pl.pallas_call(
        left_kernel,
        out_shape=[shape((blk // 2, width, wide), BF16), shape((8, wide), F32)],
        grid_spec=pltpu.PrefetchScalarGridSpec(
            num_scalar_prefetch=1,
            grid=(blk // ROWS,),
            in_specs=[
                pl.BlockSpec((ROWS, width * width), lambda i, *_: (i, 0)),
                pl.BlockSpec((nodes, width, width), lambda i, *_: (0, 0, 0)),
            ],
            out_specs=[square, pl.BlockSpec((8, wide), lambda i, *_: (0, 0))],
            scratch_shapes=[pltpu.VMEM((ROWS * half, wide), F32)],
        ),
        compiler_params=SMALL,
        cost_estimate=pl.CostEstimate(
            flops=4 * blk * width**3, bytes_accessed=4 * blk * width * width, transcendentals=0
        ),
        name="left",
    )(row_cluster, couplings, left)
    own, first_other, done = lax.optimization_barrier((own, first_other, done))
    summed = pl.pallas_call(
        sum_kernel,
        out_shape=shape((2 * parts, 8, wide), F32),
        in_specs=[VMEM, pl.BlockSpec(memory_space=pl.ANY)],
        out_specs=VMEM,
        compiler_params=SMALL,
        name="sum",
    )(own, rows)
    other = lax.ppermute(own, "branch", partners)
    quarters = lax.all_to_all(summed, ("branch", "level"), 0, 0, axis_index_groups=same_chip)

    whole = pl.BlockSpec(own.shape, lambda i, *_: (0, 0, 0))
    projected = pl.pallas_call(
        project_kernel,
        out_shape=shape((blk, width * width), F32),
        grid_spec=pltpu.PrefetchScalarGridSpec(
            num_scalar_prefetch=3,
            grid=(blk // ROWS,),
            in_specs=[square, whole, whole],
            out_specs=pl.BlockSpec((ROWS, width * width), lambda i, *_: (i, 0)),
            scratch_shapes=[
                pltpu.VMEM((ROWS * half, wide), F32),
                pltpu.VMEM((6, 2, width, wide), BF16),
            ],
        ),
        compiler_params=pltpu.CompilerParams(vmem_limit_bytes=12 * 1024 * 1024),
        cost_estimate=pl.CostEstimate(
            flops=8 * blk * width**3, bytes_accessed=6 * blk * width * width, transcendentals=0
        ),
        name="project",
    )(column_owner[:, 0], column_cluster, core[None], rows, own, other)
    projected, quarters = lax.optimization_barrier((projected, quarters))
    upper_grams = pl.pallas_call(
        top_kernel,
        out_shape=shape((1, width * width), F32),
        in_specs=[SMEM, VMEM, VMEM, VMEM, VMEM],
        out_specs=VMEM,
        scratch_shapes=[pltpu.VMEM((width, width), F32)],
        compiler_params=SMALL,
        name="top",
    )(core[None], quarters, first, first_other, done)
    return (upper_grams, projected)


def solution(mesh):
    placed = (
        P("branch", None, "level"),
        P("branch", None),
        P("branch"),
        P(),
        P(),
        P(("branch", "level"), None),
        P(("branch", "level")),
        P(("branch", "level"), None),
        P(("branch", "level")),
    )
    return jax.shard_map(
        on_device,
        mesh=mesh,
        in_specs=placed,
        out_specs=(P("branch", None), P(("branch", "level"), None)),
        check_vma=False,
    )
```

```python
import jax
import jax.numpy as jnp
from jax import lax
from jax.experimental import pallas as pl
from jax.experimental.pallas import tpu as pltpu
from jax.sharding import PartitionSpec as P

VMEM = pl.BlockSpec(memory_space=pltpu.VMEM)
SMEM = pl.BlockSpec(memory_space=pltpu.SMEM)
SMALL = pltpu.CompilerParams(vmem_limit_bytes=8 * 1024 * 1024)
ROWS = 16
F32 = jnp.float32
BF16 = jnp.bfloat16


def iota(shape, axis):
    return lax.broadcasted_iota(jnp.int32, shape, axis)


def nn(a, b):
    return jnp.dot(a, b, preferred_element_type=F32)


def nt(a, b):
    return lax.dot_general(a, b, (((1,), (1,)), ((), ())), preferred_element_type=F32)


def tn(a, b):
    return lax.dot_general(a, b, (((0,), (0,)), ((), ())), preferred_element_type=F32)


def halves(x):
    high = x.astype(BF16)
    return high, (x - high.astype(F32)).astype(BF16)


def keep_rank(gram, rank):
    return jnp.where((iota(gram.shape, 0) < rank) & (iota(gram.shape, 1) < rank), gram, 0.0)


def lift(masked, transfer):
    inner = []
    for gram, mat in zip(masked, transfer):
        high, low = halves(gram)
        inner.append(nn(high, mat) + nn(low, mat))
    high, low = halves(jnp.concatenate(inner, axis=0))
    mats = jnp.concatenate(transfer, axis=0)
    return tn(mats, high) + tn(mats, low)


def product(multiply, a, b):
    return multiply(a[0], b[0]) + (multiply(a[0], b[1]) + multiply(a[1], b[0]))


def fold(square):
    half = square.shape[0] // 2
    row, column = iota((half, half), 0), iota((half, half), 1)
    first = square[:half, :half]
    mixed = jnp.where(row < column, first, square[half:, half:])
    centre = jnp.sum(jnp.where(row == column, first, 0.0), axis=0, keepdims=True)
    return jnp.concatenate([mixed, square[:half, half:]], axis=1), centre


def unfold(folded, centre):
    half = folded.shape[0]
    row, column = iota((half, half), 0), iota((half, half), 1)
    turned = folded.T
    mixed, mixed_turned = folded[:, :half], turned[:half]
    first = jnp.where(row < column, mixed, jnp.where(row > column, mixed_turned, centre))
    last = jnp.where(row >= column, mixed, mixed_turned)
    top = jnp.concatenate([first, folded[:, half:]], axis=1)
    return jnp.concatenate([top, jnp.concatenate([turned[half:], last], axis=1)], axis=0)


def pack(square):
    half = square.shape[0] // 2
    return jnp.concatenate([square[:half], square[half:]], axis=1)


def unpack(packed):
    half = packed.shape[1] // 2
    return jnp.concatenate([packed[:, :half], packed[:, half:]], axis=0)


def reach(index, count):
    return (index ^ ((index + 1) % count)).bit_length()


def gram_kernel(basis_ref, out_ref):
    copies = out_ref.shape[0]
    width = basis_ref.shape[1]
    wide = 2 * width
    row = iota((width, wide), 0)
    lane = iota((width, wide), 1)
    column = lane & (width - 1)
    sides = []
    for side in range(2):
        both = jnp.concatenate([basis_ref[side], basis_ref[side + 2]], axis=0)
        crossed = nt(both, both)
        sides.append(jnp.where(lane < width, crossed[:width], crossed[width:]))
    folded = jnp.where(row <= column, sides[0], sides[1])
    diagonal = jnp.sum(jnp.where(row == column, sides[1], 0.0), axis=0, keepdims=True)
    for copy in range(copies):
        out_ref[copy, :width] = folded
        out_ref[copy, width:] = jnp.broadcast_to(diagonal, (8, wide))


def path_kernel(rank_ref, path_ref, high_ref, low_ref):
    heights = path_ref.shape[0]
    row = iota(path_ref.shape[1:], 0)
    for height in range(heights):
        step = jnp.where(row < rank_ref[height], path_ref[height].astype(F32), 0.0)
        if height == 0:
            whole = step
        else:
            step = step.astype(BF16)
            whole = nn(high, step) + nn(low, step)
        high, low = halves(whole)
        high_ref[height] = high
        low_ref[height] = low


def near_kernel(
    rank_ref, place_ref, level_ref, parts_ref, bottom_ref, high_ref, low_ref, left_ref, sent_ref, first_ref, tiles
):
    nodes, width, _ = bottom_ref.shape
    wide = 2 * width
    half = width // 2
    targets = sent_ref.shape[0]
    heights = high_ref.shape[0]
    total = parts_ref[0]
    for part in range(1, parts_ref.shape[0]):
        total = total + parts_ref[part]
    folded = total[:width]
    diagonal = total[width : width + 1]
    turned = folded.T
    row = iota((width, width), 0)
    column = iota((width, width), 1)
    masked = []
    for node in range(nodes):
        pair, side = node // 2, node % 2
        here = folded[:, pair * width : (pair + 1) * width]
        there = turned[pair * width : (pair + 1) * width]
        if side == 0:
            gram = jnp.where(row <= column, here, there)
        else:
            centre = jnp.broadcast_to(diagonal[:, pair * width : (pair + 1) * width], (width, width))
            gram = jnp.where(row > column, here, jnp.where(row < column, there, centre))
        masked.append(keep_rank(gram, rank_ref[node]))
    bottom = halves(lift(masked, [bottom_ref[node] for node in range(nodes)]))
    lane = iota((1, wide), 1)
    lower = jnp.where(lane < width, rank_ref[1], rank_ref[3])
    diagonal = jnp.where((lane & (width - 1)) < lower, diagonal, 0.0)
    tiles[0] = jnp.concatenate([diagonal, jnp.zeros((7, wide), F32)], axis=0)
    parts = parts_ref.shape[0]
    share = half // (2 * parts)
    for height in range(heights):
        path = (high_ref[height], low_ref[height])
        term = product(tn, path, halves(product(nn, bottom, path)))
        if height == 0:
            first_ref[...] = pack(term)
            continue
        square, centre = fold(term)
        packed = pack(square)
        mine = packed[:share]
        for part in range(1, parts):
            mine = jnp.where(level_ref[0] == part, packed[part * share : (part + 1) * share], mine)
        centre = jnp.concatenate([centre, jnp.zeros((1, wide - half), F32)], axis=1)
        tiles[height] = jnp.concatenate([diagonal, mine, centre, jnp.zeros((6 - share, wide), F32)], axis=0)

    row = iota((width, wide), 0)
    lane = iota((width, wide), 1)
    column = lane & (width - 1)
    low = lane < width
    upper = jnp.where(low, rank_ref[0], rank_ref[2])
    lower = jnp.where(low, rank_ref[1], rank_ref[3])
    kept = jnp.maximum(row, column) < jnp.where(row <= column, upper, lower)
    share_rows = jnp.where(kept, folded, 0.0).astype(BF16)
    place = place_ref[0]
    for target in range(targets):
        device = 2 * target + 1
        height = reach(device, 2 * targets)
        inside = jnp.right_shift(place, height) == device >> height
        sent_ref[target, :width] = share_rows
        sent_ref[target, width:] = tiles[jnp.where(inside, height - 1, 0)].astype(BF16)

    for node in range(nodes):
        left_ref[node] = masked[node].astype(BF16)


def sum_kernel(received_ref, out_ref):
    sources, rows, _ = received_ref.shape
    total = received_ref[0, rows - 8 :].astype(F32)
    for source in range(1, sources):
        total = total + received_ref[source, rows - 8 :].astype(F32)
    for copy in range(out_ref.shape[0]):
        out_ref[copy] = total


def top_kernel(core_ref, received_ref, first_ref, other_ref, done_ref, out_ref, scratch):
    parts = received_ref.shape[0] // 2
    wide = received_ref.shape[2]
    width = wide // 2
    half = width // 2
    share = half // (2 * parts)
    sums = [received_ref[part] + received_ref[parts + part] for part in range(parts)]
    packed = jnp.concatenate([value[1 : 1 + share] for value in sums], axis=0)
    high = unfold(unpack(packed), sums[0][1 + share : 2 + share, :half])
    scratch[...] = jnp.where(core_ref[0] == 1, high, unpack(first_ref[...] + other_ref[...]))
    natural = jnp.concatenate([scratch[pl.ds(side, half, stride=2), :] for side in range(2)], axis=1)
    for tile in range(half):
        out_ref[:, tile * wide : (tile + 1) * wide] = natural[tile : tile + 1]


def left_kernel(row_ref, blocks_ref, masked_ref, out_ref, done_ref, spread, left_ref):
    step = pl.program_id(0)
    count, flat = blocks_ref.shape
    width = masked_ref.shape[1]
    wide = 2 * width
    tiles = flat // wide
    low = iota((width, wide), 1) < width

    @pl.when(step == 0)
    def _():
        row = iota((width, width), 0)
        even_first = jnp.where(row < tiles, 2 * row, 2 * row - width + 1)
        order = (iota((width, width), 1) == even_first).astype(F32).astype(BF16)
        for node in range(left_ref.shape[0]):
            left_ref[node] = nt(nn(order, masked_ref[node]).astype(BF16), order).astype(BF16)

    for tile in range(tiles):
        spread[tile * count : (tile + 1) * count, :] = blocks_ref[:, tile * wide : (tile + 1) * wide].astype(F32)
    for index in range(0, count, 2):
        products = []
        for place in range(2):
            here = spread[pl.ds(index + place, tiles, stride=count), :]
            turned = pltpu.roll(here, width, 1)
            rows = jnp.where(
                low, jnp.concatenate([here, turned], axis=0), jnp.concatenate([turned, here], axis=0)
            ).astype(BF16)
            products.append(nn(left_ref[row_ref[step * count + index + place]], rows))
        out_ref[index // 2] = jnp.where(low, products[0], products[1]).astype(BF16)
    done_ref[...] = jnp.zeros_like(done_ref)


def project_kernel(
    owner_ref, column_ref, core_ref, rows_ref, own_ref, other_ref, out_ref, kept_ref, result, triangles
):
    step = pl.program_id(0)
    pairs, width, wide = rows_ref.shape
    count = 2 * pairs
    tiles = width // 2
    low = iota((tiles, wide), 1) < width
    none = jnp.zeros((width, wide), BF16)

    @pl.when(step == 0)
    def _():
        row = iota((width, wide), 0)
        lane = iota((width, wide), 1)
        column = lane & (width - 1)
        for cluster in range(4):
            mine = (lane < width) == (cluster < 2)
            parts = (row <= column, row < 0) if cluster % 2 == 0 else (row > column, row == column)
            for index, part in enumerate(parts):
                triangles[cluster, index] = (mine & part).astype(F32).astype(BF16)
        for place in range(2):
            mine = (lane < width) == (place == 0)
            triangles[4 + place, 0] = (mine & (row > column)).astype(F32).astype(BF16)
            triangles[4 + place, 1] = (mine & (row < column)).astype(F32).astype(BF16)

    for index in range(0, count, 2):
        folded = []
        for place in range(2):
            owner = owner_ref[step * count + index + place]
            source = jnp.right_shift(owner, 1)
            at_home = (owner & 1) == core_ref[0]
            folded.append(
                (
                    jnp.where(at_home, own_ref[source, :width], other_ref[source, :width]),
                    jnp.where(at_home, own_ref[source, width:], other_ref[source, width:])[:1],
                )
            )
        turned = jnp.concatenate([folded[0][0], folded[1][0]], axis=0).T
        for place in range(2):
            cluster = column_ref[step * count + index + place]
            here, centre = folded[place]
            mirrored = jnp.where(cluster < 2, turned[:width], turned[width:])
            right = (
                here * triangles[cluster, 0]
                + centre * triangles[cluster, 1]
                + mirrored * triangles[4 + place, cluster & 1]
            )
            weights = [right, none] if place == 0 else [none, right]
            full = nn(rows_ref[index // 2], jnp.concatenate(weights, axis=0))
            top, bottom = full[:tiles], full[tiles:]
            out = jnp.where(low, top, bottom) + pltpu.roll(jnp.where(low, bottom, top), width, 1)
            result[pl.ds(index + place, tiles, stride=count), :] = out
    for tile in range(tiles):
        out_ref[:, tile * wide : (tile + 1) * wide] = result[tile * count : (tile + 1) * count, :]


def shape(dims, dtype):
    return jax.ShapeDtypeStruct(dims, dtype)


def on_device(
    basis,
    bottom_transfer,
    bottom_rank,
    upper_transfer,
    upper_rank,
    couplings,
    row_cluster,
    column_owner,
    column_cluster,
):
    nodes, width, _ = basis.shape
    wide = 2 * width
    half = width // 2
    branches = lax.axis_size("branch")
    parts = lax.axis_size("level")
    levels = branches.bit_length() - 1
    me_branch = lax.axis_index("branch")
    me_level = lax.axis_index("level")
    core = me_branch & 1
    blk = couplings.shape[0]
    same_core = [list(range(c, branches, 2)) for c in range(2)]
    same_chip = [list(range(2 * parts * chip, 2 * parts * (chip + 1))) for chip in range(branches // 2)]
    partners = [(i, i ^ 1) for i in range(branches)]

    partial_sums = pl.pallas_call(
        gram_kernel,
        out_shape=shape((parts, width + 8, wide), F32),
        in_specs=[VMEM],
        out_specs=VMEM,
        compiler_params=SMALL,
        name="gram",
    )(basis)
    partial_sums, upper_transfer, upper_rank, bottom_transfer = lax.optimization_barrier(
        (partial_sums, upper_transfer, upper_rank, bottom_transfer)
    )
    gathered = lax.all_to_all(partial_sums, "level", 0, 0)
    heights = jnp.arange(levels, dtype=jnp.int32)
    slots = 2 * branches - jnp.right_shift(2 * branches, heights) + jnp.right_shift(me_branch, heights)
    path = jnp.take(upper_transfer, slots, axis=0).reshape(levels, width, width)
    path_high, path_low = pl.pallas_call(
        path_kernel,
        out_shape=[shape((levels, width, width), BF16)] * 2,
        in_specs=[SMEM, VMEM],
        out_specs=[VMEM, VMEM],
        compiler_params=SMALL,
        name="path",
    )(jnp.take(upper_rank, slots, axis=0), path)
    left, sent, first = pl.pallas_call(
        near_kernel,
        out_shape=[
            shape((nodes, width, width), BF16),
            shape((branches // 2, width + 8, wide), BF16),
            shape((half, wide), F32),
        ],
        in_specs=[SMEM, SMEM, SMEM, VMEM, VMEM, VMEM, VMEM],
        out_specs=[VMEM, VMEM, VMEM],
        scratch_shapes=[pltpu.VMEM((levels, 8, wide), F32)],
        compiler_params=SMALL,
        name="near",
    )(
        bottom_rank,
        me_branch[None],
        me_level[None],
        gathered,
        bottom_transfer.reshape(nodes, width, width),
        path_high,
        path_low,
    )
    own = lax.all_to_all(sent, "branch", 0, 0, axis_index_groups=same_core)
    first_other = lax.ppermute(first, "branch", partners)
    square = pl.BlockSpec((ROWS // 2, width, wide), lambda i, *_: (i, 0, 0))
    rows, done = pl.pallas_call(
        left_kernel,
        out_shape=[shape((blk // 2, width, wide), BF16), shape((8, wide), F32)],
        grid_spec=pltpu.PrefetchScalarGridSpec(
            num_scalar_prefetch=1,
            grid=(blk // ROWS,),
            in_specs=[
                pl.BlockSpec((ROWS, width * width), lambda i, *_: (i, 0)),
                pl.BlockSpec((nodes, width, width), lambda i, *_: (0, 0, 0)),
            ],
            out_specs=[square, pl.BlockSpec((8, wide), lambda i, *_: (0, 0))],
            scratch_shapes=[pltpu.VMEM((ROWS * half, wide), F32), pltpu.VMEM((nodes, width, width), BF16)],
        ),
        compiler_params=SMALL,
        cost_estimate=pl.CostEstimate(
            flops=4 * blk * width**3, bytes_accessed=4 * blk * width * width, transcendentals=0
        ),
        name="left",
    )(row_cluster, couplings, left)
    own, first_other, done = lax.optimization_barrier((own, first_other, done))
    summed = pl.pallas_call(
        sum_kernel,
        out_shape=shape((2 * parts, 8, wide), F32),
        in_specs=[VMEM],
        out_specs=VMEM,
        compiler_params=SMALL,
        name="sum",
    )(own)
    other = lax.ppermute(own, "branch", partners)
    quarters = lax.all_to_all(summed, ("branch", "level"), 0, 0, axis_index_groups=same_chip)

    whole = pl.BlockSpec(own.shape, lambda i, *_: (0, 0, 0))
    projected, _ = pl.pallas_call(
        project_kernel,
        out_shape=[shape((blk, width * width), F32), shape(rows.shape, BF16)],
        grid_spec=pltpu.PrefetchScalarGridSpec(
            num_scalar_prefetch=3,
            grid=(blk // ROWS,),
            in_specs=[square, whole, whole],
            out_specs=[
                pl.BlockSpec((ROWS, width * width), lambda i, *_: (i, 0)),
                pl.BlockSpec(memory_space=pl.ANY),
            ],
            scratch_shapes=[
                pltpu.VMEM((ROWS * half, wide), F32),
                pltpu.VMEM((6, 2, width, wide), BF16),
            ],
        ),
        compiler_params=pltpu.CompilerParams(vmem_limit_bytes=12 * 1024 * 1024),
        cost_estimate=pl.CostEstimate(
            flops=8 * blk * width**3, bytes_accessed=6 * blk * width * width, transcendentals=0
        ),
        input_output_aliases={3: 1},
        name="project",
    )(column_owner[:, 0], column_cluster, core[None], rows, own, other)
    projected, quarters = lax.optimization_barrier((projected, quarters))
    upper_grams = pl.pallas_call(
        top_kernel,
        out_shape=shape((1, width * width), F32),
        in_specs=[SMEM, VMEM, VMEM, VMEM, VMEM],
        out_specs=VMEM,
        scratch_shapes=[pltpu.VMEM((width, width), F32)],
        compiler_params=SMALL,
        name="top",
    )(core[None], quarters, first, first_other, done)
    return (upper_grams, projected)


def solution(mesh):
    placed = (
        P("branch", None, "level"),
        P("branch", None),
        P("branch"),
        P(),
        P(),
        P(("branch", "level"), None),
        P(("branch", "level")),
        P(("branch", "level"), None),
        P(("branch", "level")),
    )
    return jax.shard_map(
        on_device,
        mesh=mesh,
        in_specs=placed,
        out_specs=(P("branch", None), P(("branch", "level"), None)),
        check_vma=False,
    )
```
